32 devices in a mesh: dp: 16 (over z, y, core), tensor: 2 (over x).
Axes of the slice: x: 2, y: 2, z: 4, core: 2. Of those that a mesh axis runs over, the one named last changes fastest.
Arguments:
- states_in: bfloat16 [16, 1024, 1024], P('dp', 'tensor'), may hold values from -6 to 6
- teacher: bfloat16 [16, 1024, 1024], P('dp', 'tensor'), may hold values from -6 to 6
- valid_mask: int32 [16, 1024], P('dp', 'tensor'), may hold values from 0 to 1, as said below
- prefix_len: int32 [16], P('dp'), may hold values from 102 to 512, as said below
- ln1_gain: bfloat16 [2, 1024], P(None, ('dp', 'tensor')), may hold values from 0.5 to 1.5
- ln1_shift: bfloat16 [2, 1024], P(None, ('dp', 'tensor')), may hold values from -2.5 to 2.5
- qkv_weight: bfloat16 [2, 1024, 3, 1024], P(None, 'dp', None, 'tensor'), may hold values from -0.1875 to 0.1875
- qkv_bias: bfloat16 [2, 3, 16, 64], P(None, None, 'tensor', 'dp'), may hold values from -2.5 to 2.5
- out_weight: bfloat16 [2, 1024, 1024], P(None, 'tensor', 'dp'), may hold values from -0.75 to 0.75
- out_bias: bfloat16 [2, 1024], P(None, ('dp', 'tensor')), may hold values from -2.5 to 2.5
- ln2_gain: bfloat16 [2, 1024], P(None, ('dp', 'tensor')), may hold values from 0.5 to 1.5
- ln2_shift: bfloat16 [2, 1024], P(None, ('dp', 'tensor')), may hold values from -2.5 to 2.5
- up_weight: bfloat16 [2, 1024, 4096], P(None, 'dp', 'tensor'), may hold values from -0.1875 to 0.1875
- up_bias: bfloat16 [2, 64, 64], P(None, 'tensor', 'dp'), may hold values from -2.5 to 2.5
- down_weight: bfloat16 [2, 4096, 1024], P(None, 'tensor', 'dp'), may hold values from -0.09375 to 0.09375
- down_bias: bfloat16 [2, 1024], P(None, ('dp', 'tensor')), may hold values from -2.5 to 2.5
Outputs:
- final_states: bfloat16 [16, 1024, 1024], P('dp', 'tensor')
- input_grad: float32 [16, 1024, 1024], P('dp', 'tensor')
- ln1_gain_grad: float32 [2, 1024], P(None, ('dp', 'tensor'))
- ln1_shift_grad: float32 [2, 1024], P(None, ('dp', 'tensor'))
- qkv_weight_grad: float32 [2, 1024, 3, 1024], P(None, 'dp', None, 'tensor')
- qkv_bias_grad: float32 [2, 3, 16, 64], P(None, None, 'tensor', 'dp')
- out_weight_grad: float32 [2, 1024, 1024], P(None, 'tensor', 'dp')
- out_bias_grad: float32 [2, 1024], P(None, ('dp', 'tensor'))
- ln2_gain_grad: float32 [2, 1024], P(None, ('dp', 'tensor'))
- ln2_shift_grad: float32 [2, 1024], P(None, ('dp', 'tensor'))
- up_weight_grad: float32 [2, 1024, 4096], P(None, 'dp', 'tensor')
- up_bias_grad: float32 [2, 64, 64], P(None, 'tensor', 'dp')
- down_weight_grad: float32 [2, 4096, 1024], P(None, 'tensor', 'dp')
- down_bias_grad: float32 [2, 1024], P(None, ('dp', 'tensor'))
The draws below stay inside these ranges and needn't reach their ends.
Inputs may be any that keep to these rules, and one draw needn't show every extreme that they name: `valid_mask`: the first token of every sequence has 1. `prefix_len`: some sequence has exactly 512 and some exactly 102.
All inputs are finite; a program needn't handle non-finite values.
Results may differ from the reference program's by a relative error of at most 0.015.
Values may be sent and summed in bfloat16 or wider, within the bound.
A program may use at most 256 MiB of HBM per device.

```python
import jax
import jax.numpy as jnp
from jax import lax

D = 1024
H = 16
HD = 64
FF = 4096
L = 2
LANE = 64
LEN = 1024
SEQS = 16
TOKENS = 16384


def draw_valid_mask(key, part):
    key = jax.random.fold_in(key, 23)
    level = 30 + 60 * jnp.arange(SEQS, dtype=jnp.int32) // max(SEQS - 1, 1)
    ticket = jax.random.randint(key, (SEQS, LEN), 0, 100)
    marks = (ticket < level[:, None]).astype(jnp.int32)
    return marks.at[:, 0].set(1)


def draw_prefix_len(key, part):
    key = jax.random.fold_in(key, 11)
    keys_split = jax.random.split(key, 3)
    low_end = LEN // 10
    high_end = LEN // 2
    lengths = jax.random.randint(keys_split[0], (SEQS,), low_end, high_end + 1)
    first_pick = jax.random.randint(keys_split[1], (), 0, SEQS)
    offset = jax.random.randint(keys_split[2], (), 1, SEQS)
    second_pick = (first_pick + offset) % SEQS
    lengths = lengths.at[first_pick].set(high_end)
    return lengths.at[second_pick].set(low_end)


def shard_levels(key, dims, shards, least, high):
    def one(dim, blocks):
        heights = jax.random.uniform(jax.random.fold_in(jax.random.fold_in(key, 6), dim), (blocks,), jnp.float32, least / len(shards), high / len(shards))
        return jnp.repeat(jnp.exp(heights), dims[dim] // blocks).reshape((-1,) + (1,) * (len(dims) - dim - 1))

    loudness = one(*shards[0])
    for cut in shards[1:]:
        loudness = loudness * one(*cut)
    return loudness


def noise(key, dims, spread, reach, cuts=(), kind=jnp.bfloat16):
    entries = spread * jax.random.normal(key, dims, jnp.float32)
    if cuts:
        entries = entries * shard_levels(key, dims, cuts, -0.22, 0.18)
    return jnp.clip(entries, -reach, reach).astype(kind)


def setup_inputs(seed: int = 0) -> dict:
    splits = jax.random.split(jax.random.key(seed), 17)
    states_in = noise(splits[0], (SEQS, LEN, D), 1.0, 6.0, ((0, 16), (1, 2)))
    teacher = noise(splits[1], (SEQS, LEN, D), 1.0, 6.0, ((0, 16), (1, 2)))
    valid_mask = draw_valid_mask(jax.random.fold_in(splits[16], 71), 0)
    prefix_len = draw_prefix_len(jax.random.fold_in(splits[16], 71), 0)
    ln1_gain = jnp.clip(1.0 + 0.1 * jax.random.normal(splits[4], (L, D), jnp.float32), 0.5, 1.5).astype(jnp.bfloat16)
    ln1_shift = noise(splits[5], (L, D), 0.3, 2.5, ((1, 32),))
    qkv_weight = noise(splits[6], (L, D, 3, D), D ** -0.5, 0.1875, ((1, 16), (3, 2)))
    qkv_bias = noise(splits[7], (L, 3, D // LANE, LANE), 0.3, 2.5, ((2, 2), (3, 16)))
    out_weight = noise(splits[8], (L, D, D), (D // 16) ** -0.5, 0.75, ((1, 2), (2, 16)))
    out_bias = noise(splits[9], (L, D), 0.3, 2.5, ((1, 32),))
    ln2_gain = jnp.clip(1.0 + 0.1 * jax.random.normal(splits[10], (L, D), jnp.float32), 0.5, 1.5).astype(jnp.bfloat16)
    ln2_shift = noise(splits[11], (L, D), 0.3, 2.5, ((1, 32),))
    up_weight = noise(splits[12], (L, D, FF), D ** -0.5, 0.1875, ((1, 16), (2, 2)))
    up_bias = noise(splits[13], (L, FF // LANE, LANE), 0.3, 2.5, ((1, 2), (2, 16)))
    down_weight = noise(splits[14], (L, FF, D), FF ** -0.5, 0.09375, ((1, 2), (2, 16)))
    down_bias = noise(splits[15], (L, D), 0.3, 2.5, ((1, 32),))
    return dict(states_in=states_in, teacher=teacher, valid_mask=valid_mask, prefix_len=prefix_len, ln1_gain=ln1_gain, ln1_shift=ln1_shift, qkv_weight=qkv_weight, qkv_bias=qkv_bias, out_weight=out_weight, out_bias=out_bias, ln2_gain=ln2_gain, ln2_shift=ln2_shift, up_weight=up_weight, up_bias=up_bias, down_weight=down_weight, down_bias=down_bias)


@jax.custom_vjp
def low(v):
    return lax.optimization_barrier(v.astype(jnp.bfloat16)).astype(jnp.float32)

@jax.custom_vjp
def low_back(v):
    return v

def low_keep(v):
    return (low(v), None)

def low_pass(kept, grad):
    return (grad,)

def back_keep(v):
    return (v, None)

def back_low(kept, grad):
    return (low(grad),)
low.defvjp(low_keep, low_pass)
low_back.defvjp(back_keep, back_low)
EPS = 1e-05
BIG = 1000000000.0
PRECISE = lax.Precision.HIGHEST

def norm_rows(states, norm_gain, norm_shift):
    row_mean = lax.optimization_barrier(jnp.mean(states, axis=-1, keepdims=True))
    centered = states - row_mean
    row_var = lax.optimization_barrier(jnp.mean(centered * centered, axis=-1, keepdims=True))
    return centered * lax.rsqrt(row_var + EPS) * norm_gain + norm_shift

def gelu_tanh(values):
    return 0.5 * values * (1.0 + jnp.tanh(0.7978845608028654 * (values + 0.044715 * values * values * values)))

def matmul(left, right):
    return jnp.dot(left, right, precision=PRECISE, preferred_element_type=jnp.float32)

def attend(qkv_rows, seq_prefix):
    block_len = min(512, LEN)
    head_ids = jnp.arange(H, dtype=jnp.float32)
    slopes = jnp.exp2(-(head_ids + 1.0) * 8.0 / H)
    scale = HD ** (-0.5)
    key_pos = jnp.arange(LEN, dtype=jnp.int32)
    queries = qkv_rows[:, 0]
    keys_all = qkv_rows[:, 1]
    values_all = qkv_rows[:, 2]

    def one_block(block_index):
        offset = (block_index * block_len).astype(jnp.int32)
        query_block = lax.dynamic_slice_in_dim(queries, offset, block_len, 0)
        positions = offset + jnp.arange(block_len, dtype=jnp.int32)
        distance = jnp.abs(positions[:, None] - key_pos[None, :]).astype(jnp.float32)
        raw = jnp.einsum('qhd,khd->hqk', query_block, keys_all, precision=PRECISE)
        scores = low_back(raw * scale - slopes[:, None, None] * distance[None])
        visible = (key_pos[None, :] <= positions[:, None]) | (key_pos[None, :] < seq_prefix)
        scores = jnp.where(visible[None], scores, -BIG)
        row_max = lax.optimization_barrier(jnp.max(scores, axis=-1, keepdims=True))
        raised = jnp.exp(scores - row_max)
        shares = low(raised / lax.optimization_barrier(jnp.sum(raised, axis=-1, keepdims=True)))
        return jnp.einsum('hqk,khd->qhd', shares, values_all, precision=PRECISE)
    outputs = lax.map(jax.checkpoint(one_block), jnp.arange(LEN // block_len, dtype=jnp.int32))
    return outputs.reshape(LEN, H * HD)

def block_forward(layer_params, states, seq_prefix):
    gain_one, shift_one, qkv_proj, qkv_add, out_proj, out_add, gain_two, shift_two, up_proj, up_add, down_proj, down_add = layer_params
    normed = low(norm_rows(states, gain_one, shift_one))
    mixed = matmul(normed, qkv_proj.reshape(D, 3 * D)) + qkv_add.reshape(3 * D)
    qkv_rows = low_back(low(mixed)).reshape(LEN, 3, H, HD)
    heads_out = low_back(low(attend(qkv_rows, seq_prefix)))
    middle = states + low_back(matmul(heads_out, out_proj) + out_add)
    normed_two = low(norm_rows(middle, gain_two, shift_two))
    hidden = low_back(matmul(normed_two, up_proj) + up_add.reshape(FF))
    active = low(gelu_tanh(hidden))
    return middle + low_back(matmul(active, down_proj) + down_add)

def sequence_loss(params, states, teacher_rows, mask_rows, seq_prefix, factor):
    for layer_index in range(L):
        states = block_forward(tuple((member[layer_index] for member in params)), states, seq_prefix)
    differ = states - teacher_rows
    seq_loss = 0.5 * factor * jnp.sum(mask_rows[:, None] * differ * differ)
    return (seq_loss, states)

def reference(states_in, teacher, valid_mask, prefix_len, ln1_gain, ln1_shift, qkv_weight, qkv_bias, out_weight, out_bias, ln2_gain, ln2_shift, up_weight, up_bias, down_weight, down_bias):
    params = tuple((member.astype(jnp.float32) for member in (ln1_gain, ln1_shift, qkv_weight, qkv_bias, out_weight, out_bias, ln2_gain, ln2_shift, up_weight, up_bias, down_weight, down_bias)))
    valid_count = jnp.sum(valid_mask.astype(jnp.float32))
    factor = TOKENS / valid_count

    def one_sequence(totals, seq_item):
        seq_states, seq_teacher, seq_mask, seq_prefix = seq_item

        def loss_of(weights, inputs):
            return sequence_loss(weights, inputs, seq_teacher, seq_mask, seq_prefix, factor)
        seq_loss, pullback, final = jax.vjp(loss_of, params, seq_states, has_aux=True)
        weight_grads, input_grad = pullback(jnp.ones_like(seq_loss))
        totals = jax.tree.map(lambda left, right: left + right, totals, weight_grads)
        return (totals, (final.astype(jnp.bfloat16), input_grad))
    start_totals = jax.tree.map(jnp.zeros_like, params)
    totals, (final_states, input_grad) = lax.scan(one_sequence, start_totals, (states_in.astype(jnp.float32), teacher.astype(jnp.float32), valid_mask.astype(jnp.float32), prefix_len))
    return (final_states, input_grad, totals[0], totals[1], totals[2], totals[3], totals[4], totals[5], totals[6], totals[7], totals[8], totals[9], totals[10], totals[11])
```

```python
import functools

import jax
import jax.numpy as jnp
import numpy as np
from jax import lax
from jax.experimental import pallas as pl
from jax.experimental.pallas import tpu as pltpu
from jax.sharding import PartitionSpec as P

LOG2E = 1.4426950408889634
BIG = 1000000000.0
NT = (((1,), (1,)), ((), ()))
NN = (((1,), (0,)), ((), ()))


def mm(a, b, dims):
    return lax.dot_general(a, b, dims, preferred_element_type=jnp.float32)


def lane_masks(width):
    lanes = lax.broadcasted_iota(jnp.int32, (1, width), 1)
    low = jnp.where(lanes < width // 2, 1.0, 0.0)
    return (low.astype(jnp.bfloat16), (1.0 - low).astype(jnp.bfloat16))


def rows_iota(n, m):
    return lax.broadcasted_iota(jnp.int32, (n, m), 0)


def cols_iota(n, m):
    return lax.broadcasted_iota(jnp.int32, (n, m), 1)


def scores_first(keys, query, slope, scale, prefix, start):
    n, m = (keys.shape[0], query.shape[0])
    key_pos = rows_iota(n, m)
    query_pos = cols_iota(n, m) + start
    distance = jnp.abs(query_pos - key_pos).astype(jnp.float32)
    raw = mm(keys, query, NT) * scale - slope * distance
    visible = (key_pos <= query_pos) | (key_pos < prefix)
    return jnp.where(visible, raw, -BIG)


def scores_second(keys, query, slope, scale, offset, mask_start):
    n, m = (keys.shape[0], query.shape[0])
    bias = slope * (rows_iota(n, 1) + offset).astype(jnp.float32)
    raw = mm(keys, query, NT) * scale + bias
    if mask_start is None:
        return raw
    return jnp.where(rows_iota(n, m) + mask_start <= cols_iota(n, m), raw, -BIG)


def score_parts(half, k_ref, k0_ref, query, slope, scale, prefix, start, step):
    rows = k_ref.shape[0]
    if half == 0:
        return [(None, 0, rows, scores_first(k_ref[...], query, slope, scale, prefix, start))]
    parts = [(0, 0, rows, scores_second(k0_ref[...], query, slope, scale, -2 * rows, None))]
    if start > 0:
        parts.append((1, 0, start, scores_second(k_ref[:start], query, slope, scale, -rows, None)))
    parts.append(
        (1, start, start + step, scores_second(k_ref[start : start + step], query, slope, scale, start - rows, 0))
    )
    return parts


def forward_body(half, slopes, prefix, scale, q_ref, k_ref, v_ref, k0_ref, v0_ref, o_ref, lse_ref, step):
    rows, width = q_ref.shape
    masks = lane_masks(width)
    pair = pl.program_id(0)
    head = width // 2
    values = v_ref[...].T
    values0 = v0_ref[...].T if half else None
    for start in range(0, rows, step):
        outs = []
        for side in range(2):
            query = q_ref[start : start + step] * masks[side]
            slope = slopes[pair * 2 + side]
            parts = score_parts(half, k_ref, k0_ref, query, slope, scale, prefix, start, step)
            top = parts[0][3].max(axis=0, keepdims=True)
            for part in parts[1:]:
                top = jnp.maximum(top, part[3].max(axis=0, keepdims=True))
            total = None
            out = None
            for which, low, high, raw in parts:
                raised = jnp.exp2(raw - top)
                part_sum = raised.sum(axis=0, keepdims=True)
                held = values0 if which == 0 else values
                held = held[side * head : (side + 1) * head, low:high]
                part_out = mm(held, raised.astype(jnp.bfloat16), NN)
                total = part_sum if total is None else total + part_sum
                out = part_out if out is None else out + part_out
            outs.append(out / total)
            lse_ref[0, side : side + 1, start : start + step] = top + jnp.log2(total)
        o_ref[start : start + step] = jnp.concatenate(outs, axis=0).T.astype(jnp.bfloat16)


def forward_kernel(meta, slopes, q_ref, k_ref, v_ref, k0_ref, v0_ref, o_ref, lse_ref, *, scale, step):
    args = (slopes, meta[1], scale, q_ref, k_ref, v_ref, k0_ref, v0_ref, o_ref, lse_ref, step)

    @pl.when(meta[0] == 0)
    def first():
        forward_body(0, *args)

    @pl.when(meta[0] != 0)
    def second():
        forward_body(1, *args)


def attention_forward(meta, slopes, qkv, kv0, scale):
    rows, width = qkv.shape
    pairs = width // 3 // 128
    block = lambda base: pl.BlockSpec((rows, 128), lambda j, *_: (0, base + j))
    return pl.pallas_call(
        functools.partial(forward_kernel, scale=scale * LOG2E, step=rows // 2),
        grid_spec=pltpu.PrefetchScalarGridSpec(
            num_scalar_prefetch=2,
            grid=(pairs,),
            in_specs=[block(0), block(pairs), block(2 * pairs), block(0), block(pairs)],
            out_specs=[block(0), pl.BlockSpec((1, 2, rows), lambda j, *_: (j, 0, 0))],
        ),
        out_shape=[
            jax.ShapeDtypeStruct((rows, width // 3), jnp.bfloat16),
            jax.ShapeDtypeStruct((pairs, 2, rows), jnp.float32),
        ],
        compiler_params=pltpu.CompilerParams(vmem_limit_bytes=40 * 1024 * 1024),
        cost_estimate=pl.CostEstimate(
            flops=pairs * 2 * rows * rows * 128 * 8, bytes_accessed=rows * width * 4, transcendentals=pairs * 4 * rows * rows
        ),
        name="attention_forward",
    )(meta, slopes, qkv, qkv, qkv, kv0, kv0)


def backward_body(half, slopes, prefix, scale, refs, step):
    q_ref, k_ref, v_ref, k0_ref, v0_ref, g_ref, lse_ref, gq_ref, gk_ref, gv_ref, gk0_ref, gv0_ref, sums = refs
    rows, width = q_ref.shape
    masks = lane_masks(width)
    pair = pl.program_id(0)
    head = width // 2
    keys = k_ref[...].T
    keys0 = k0_ref[...].T if half else None
    sums[...] = jnp.zeros_like(sums)
    for start in range(0, rows, step):
        outs = []
        for side in range(2):
            query = q_ref[start : start + step] * masks[side]
            grad = g_ref[start : start + step] * masks[side]
            slope = slopes[pair * 2 + side]
            parts = score_parts(half, k_ref, k0_ref, query, slope, scale * LOG2E, prefix, start, step)
            lse = lse_ref[0, side : side + 1, start : start + step]
            inner = None
            held = []
            for which, low, high, raw in parts:
                share = jnp.exp2(raw - lse)
                value = v0_ref[low:high] if which == 0 else v_ref[low:high]
                slot = 2 if which == 0 else 0
                grad_share = mm(value, grad, NT)
                part = (share * grad_share).sum(axis=0, keepdims=True)
                inner = part if inner is None else inner + part
                sums[slot + 1, low:high] += mm(share.astype(jnp.bfloat16), grad, NN)
                held.append((which, low, high, share, grad_share, slot))
            out = None
            for which, low, high, share, grad_share, slot in held:
                grad_score = (share * (grad_share - inner)).astype(jnp.bfloat16)
                sums[slot, low:high] += mm(grad_score, query, NN)
                key = keys0 if which == 0 else keys
                part = mm(key[side * head : (side + 1) * head, low:high], grad_score, NN)
                out = part if out is None else out + part
            outs.append(out)
        gq_ref[start : start + step] = (jnp.concatenate(outs, axis=0).T * scale).astype(jnp.bfloat16)
    gk_ref[...] = (sums[0] * scale).astype(jnp.bfloat16)
    gv_ref[...] = sums[1].astype(jnp.bfloat16)
    gk0_ref[...] = (sums[2] * scale).astype(jnp.bfloat16)
    gv0_ref[...] = sums[3].astype(jnp.bfloat16)


def backward_kernel(meta, slopes, *refs, scale, step):
    @pl.when(meta[0] == 0)
    def first():
        backward_body(0, slopes, meta[1], scale, refs, step)

    @pl.when(meta[0] != 0)
    def second():
        backward_body(1, slopes, meta[1], scale, refs, step)


def attention_backward(meta, slopes, qkv, kv0, grad_heads, lse, scale):
    rows, width = qkv.shape
    pairs = width // 3 // 128
    block = lambda base: pl.BlockSpec((rows, 128), lambda j, *_: (0, base + j))
    full = jax.ShapeDtypeStruct((rows, width // 3), jnp.bfloat16)
    return pl.pallas_call(
        functools.partial(backward_kernel, scale=scale, step=rows // 2),
        grid_spec=pltpu.PrefetchScalarGridSpec(
            num_scalar_prefetch=2,
            grid=(pairs,),
            in_specs=[
                block(0),
                block(pairs),
                block(2 * pairs),
                block(0),
                block(pairs),
                block(0),
                pl.BlockSpec((1, 2, rows), lambda j, *_: (j, 0, 0)),
            ],
            out_specs=[block(0)] * 5,
            scratch_shapes=[pltpu.VMEM((4, rows, 128), jnp.float32)],
        ),
        out_shape=[full] * 5,
        compiler_params=pltpu.CompilerParams(vmem_limit_bytes=40 * 1024 * 1024),
        cost_estimate=pl.CostEstimate(
            flops=pairs * 2 * rows * rows * 128 * 20, bytes_accessed=rows * width * 8, transcendentals=pairs * 4 * rows * rows
        ),
        name="attention_backward",
    )(meta, slopes, qkv, qkv, qkv, kv0, kv0, grad_heads, lse)


EPS = 1e-05
H = 16
HD = 64
ROWS_CONTRACT = (((0,), (0,)), ((), ()))


def norm_parts(states):
    centered = states - jnp.mean(states, axis=-1, keepdims=True)
    inverse = lax.rsqrt(jnp.mean(centered * centered, axis=-1, keepdims=True) + EPS)
    return (centered * inverse, inverse)


def norm_rows(states, gain, shift):
    return norm_parts(states)[0] * gain + shift


def norm_back(states, gain, grad):
    unit, inverse = norm_parts(states)
    scaled = grad * gain
    first = jnp.mean(scaled, axis=-1, keepdims=True)
    second = jnp.mean(scaled * unit, axis=-1, keepdims=True)
    return (inverse * (scaled - first - unit * second), jnp.sum(grad * unit, axis=0), jnp.sum(grad, axis=0))


def gelu_tanh(values):
    return 0.5 * values * (1.0 + jnp.tanh(0.7978845608028654 * (values + 0.044715 * values * values * values)))


class Ring:
    def __init__(self, devices):
        self.chips = devices // 2
        self.order = list(range(0, self.chips, 2)) + list(range(self.chips - 1, 0, -2))
        self.place = {chip: spot for spot, chip in enumerate(self.order)}
        self.ahead = self.pairs(1)
        self.behind = self.pairs(-1)
        self.sibling = [(i, i ^ 1) for i in range(devices)]

    def pairs(self, step):
        return [
            (2 * self.order[spot] + core, 2 * self.order[(spot + step) % self.chips] + core)
            for spot in range(self.chips)
            for core in range(2)
        ]

    def owners(self):
        table = []
        for device in range(2 * self.chips):
            spot = self.place[device // 2]
            table.append(
                [
                    2 * self.order[(spot - step) % self.chips] + ((device % 2) ^ core)
                    for core in range(2)
                    for step in range(self.chips)
                ]
            )
        return np.array(table, np.int32)

    def gather(self, block):
        half = self.chips // 2
        blocks = [None] * self.chips
        blocks[0] = block
        up = down = block
        for hop in range(1, half):
            up = lax.ppermute(up, "dp", self.ahead)
            down = lax.ppermute(down, "dp", self.behind)
            blocks[hop] = up
            blocks[self.chips - hop] = down
        middle = block.shape[0] // 2
        blocks[half] = jnp.concatenate(
            [lax.ppermute(up[:middle], "dp", self.ahead), lax.ppermute(down[middle:], "dp", self.behind)], axis=0
        )
        return blocks

    def scatter(self, parts):
        half = self.chips // 2
        middle = parts[0].shape[0] // 2
        low = jnp.bfloat16
        up = lax.ppermute(parts[half][middle:].astype(low), "dp", self.ahead)
        down = lax.ppermute(parts[half][:middle].astype(low), "dp", self.behind)
        zeros = jnp.zeros_like(up)
        up = jnp.concatenate([zeros, up], axis=0)
        down = jnp.concatenate([down, zeros], axis=0)
        for hop in range(half - 1, 0, -1):
            up = lax.ppermute(wide_sum(parts[self.chips - hop], up).astype(low), "dp", self.ahead)
            down = lax.ppermute(wide_sum(parts[hop], down).astype(low), "dp", self.behind)
        return wide_sum(wide_sum(parts[0], up), down)


def wide_sum(left, right):
    return left.astype(jnp.float32) + right.astype(jnp.float32)


SWAP = [(0, 1), (1, 0)]


def swap(block):
    return lax.ppermute(block, "tensor", SWAP)


def rows_of(blocks, low, high):
    return jnp.concatenate([block[:, low:high] for block in blocks], axis=0)


def fetch_attention(ring, qkv_shard, out_shard):
    rows = qkv_shard.shape[0]
    own = jnp.concatenate([qkv_shard.reshape(rows, -1), out_shard.T], axis=1)
    other = swap(own)
    size = own.shape[1] // 4
    both = [side[:, i * size : (i + 1) * size] for i in range(4) for side in (own, other)]
    blocks = ring.gather(jnp.concatenate(both, axis=1))
    blocks = blocks + [lax.ppermute(block, "dp", ring.sibling) for block in blocks]
    return (rows_of(blocks, 0, 6 * size), rows_of(blocks, 6 * size, 8 * size))


def fetch_mlp(ring, up_shard, down_shard):
    size = up_shard.shape[1]
    own = ring.gather(jnp.concatenate([up_shard, down_shard.T], axis=1))
    other = [swap(block) for block in own]
    own = own + [lax.ppermute(block, "dp", ring.sibling) for block in own]
    other = other + [lax.ppermute(block, "dp", ring.sibling) for block in other]
    return (
        [rows_of(own, 0, size), rows_of(other, 0, size)],
        [rows_of(own, size, 2 * size), rows_of(other, size, 2 * size)],
    )


def grad_rows(left, right, extra=None):
    half = left.shape[1] // 2

    def product(part):
        columns = slice(part * half, (part + 1) * half)
        out = lax.dot_general(left[:, columns], right, ROWS_CONTRACT, preferred_element_type=jnp.float32)
        if extra is not None:
            more = lax.dot_general(extra[0][:, columns], extra[1], ROWS_CONTRACT, preferred_element_type=jnp.float32)
            out = out + more
        return out

    return product


def sibling_sum(ring, product):
    arrived = lax.ppermute(product(1).astype(jnp.bfloat16), "dp", ring.sibling)
    return (product(0) + arrived.astype(jnp.float32)).astype(jnp.bfloat16)


def ring_sum(ring, total):
    rows = total.shape[0] // ring.chips
    return ring.scatter([total[i * rows : (i + 1) * rows] for i in range(ring.chips)])


def local(
    states_in,
    teacher,
    valid_mask,
    prefix_len,
    ln1_gain,
    ln1_shift,
    qkv_weight,
    qkv_bias,
    out_weight,
    out_bias,
    ln2_gain,
    ln2_shift,
    up_weight,
    up_bias,
    down_weight,
    down_bias,
):
    f32, low = (jnp.float32, jnp.bfloat16)
    layers, local_rows = (qkv_weight.shape[0], states_in.shape[1])
    width = states_in.shape[2]
    dp, tensor = (lax.axis_size("dp"), lax.axis_size("tensor"))
    here, side = (lax.axis_index("dp"), lax.axis_index("tensor"))
    ring = Ring(dp)
    piece = width // (dp * tensor)

    def by_half(pair, axis):
        return jnp.where(side == 0, pair, jnp.flip(pair, axis))

    owners = lax.dynamic_index_in_dim(jnp.asarray(ring.owners()), here, 0, keepdims=False)
    rows = width // dp
    columns = (owners[:, None] * rows + jnp.arange(rows, dtype=jnp.int32)[None]).reshape(1, width)
    to_ring = (jnp.arange(width, dtype=jnp.int32)[:, None] == columns).astype(low)

    def into_ring(values):
        return jnp.dot(values, to_ring, preferred_element_type=f32)

    def from_ring(values, precision=None):
        return lax.dot_general(
            values, to_ring.astype(values.dtype), NT, precision=precision, preferred_element_type=f32
        )

    count = jnp.sum(valid_mask)
    vectors = jnp.stack([ln1_gain, ln1_shift, out_bias, ln2_gain, ln2_shift, down_bias])
    packed = jnp.concatenate(
        [vectors.reshape(-1), qkv_bias.reshape(-1), up_bias.reshape(-1), jnp.stack([count // 256, count % 256]).astype(low)]
    )
    everything = lax.all_gather(packed, ("dp", "tensor"), axis=0, tiled=False)
    first, second, third = (vectors.size, vectors.size + qkv_bias.size, vectors.size + qkv_bias.size + up_bias.size)
    vectors = everything[:, :first].reshape(dp * tensor, 6 * layers, piece).transpose(1, 0, 2)
    small = into_ring(vectors.reshape(6 * layers, width)).reshape(6, layers, 1, width)
    qkv_add = everything[:, first:second].reshape((dp, tensor) + qkv_bias.shape).transpose(2, 3, 1, 4, 0, 5)
    qkv_add = by_half(qkv_add, 2).reshape(layers, 1, 3 * width).astype(f32)
    up_add = everything[:, second:third].reshape((dp, tensor) + up_bias.shape).transpose(2, 1, 3, 0, 4)
    up_add = by_half(up_add, 1).reshape(layers, tensor, 1, -1).astype(f32)
    counts = jnp.sum(everything[:, third:].astype(f32), axis=0)
    valid_count = counts[0] * 256.0 + counts[1]

    scale = HD ** (-0.5)
    pieces = jnp.arange(H, dtype=jnp.int32)
    heads_half = H // tensor
    heads = (pieces // heads_half ^ side) * heads_half + pieces % heads_half
    slopes = jnp.exp2(-(heads.astype(f32) + 1.0) * 8.0 / H) * LOG2E
    meta = jnp.stack([side.astype(jnp.int32), prefix_len[0]])

    before_first = lax.ppermute(states_in[0], "tensor", [(0, 1)])
    attention = []
    mlp = []
    for layer in range(layers):
        attention.append(fetch_attention(ring, qkv_weight[layer], out_weight[layer]))
        mlp.append(fetch_mlp(ring, up_weight[layer], down_weight[layer]))

    states = into_ring(states_in[0])
    target = into_ring(teacher[0])
    kept = []
    for layer in range(layers):
        qkv_proj, out_proj = attention[layer]
        up_proj, down_proj = mlp[layer]
        normed = norm_rows(states, small[0][layer], small[1][layer]).astype(low)
        if layer == 0:
            normed_first = norm_rows(into_ring(before_first), small[0][layer], small[1][layer]).astype(low)
        else:
            normed_first = lax.ppermute(normed, "tensor", [(0, 1)])
        qkv = (jnp.dot(normed, qkv_proj, preferred_element_type=f32) + qkv_add[layer]).astype(low)
        kv_first = jnp.dot(normed_first, qkv_proj[:, width:], preferred_element_type=f32) + qkv_add[layer][:, width:]
        kv_first = kv_first.astype(low)
        heads_out, lse = attention_forward(meta, slopes, qkv, kv_first, scale)
        middle = states + mm(heads_out, out_proj, NT) + small[2][layer]
        normed_two = norm_rows(middle, small[3][layer], small[4][layer]).astype(low)
        hidden = [jnp.dot(normed_two, up_proj[i], preferred_element_type=f32) + up_add[layer][i] for i in range(tensor)]
        active = [gelu_tanh(values).astype(low) for values in hidden]
        kept.append((states, normed, normed_first, qkv, kv_first, lse, heads_out, middle, normed_two, hidden, active))
        states = middle + mm(active[0], down_proj[0], NT) + mm(active[1], down_proj[1], NT) + small[5][layer]

    final_states = from_ring(states.astype(low)).astype(low)[None]
    factor = local_rows * tensor * dp / valid_count
    grad = factor * valid_mask[0][:, None].astype(f32) * (states - target)
    weight_grads = [None] * layers
    vector_grads = [None] * layers
    bias_grads = [None] * layers
    for layer in reversed(range(layers)):
        before, normed, normed_first, qkv, kv_first, lse, heads_out, middle, normed_two, hidden, active = kept[layer]
        qkv_proj, out_proj = attention[layer]
        up_proj, down_proj = mlp[layer]
        grad_mlp = grad.astype(low)
        down_shift = jnp.sum(grad_mlp.astype(f32), axis=0)
        grad_hidden = []
        for i in range(tensor):
            grad_active = jnp.dot(grad_mlp, down_proj[i], preferred_element_type=f32)
            grad_hidden.append(jax.vjp(gelu_tanh, hidden[i])[1](grad_active)[0].astype(low))
        down_grads = [sibling_sum(ring, grad_rows(grad_mlp, active[i])) for i in range(tensor)]
        down_grad = ring_sum(ring, wide_sum(down_grads[0], swap(down_grads[1])).astype(low))
        up_shift = jnp.stack([jnp.sum(values.astype(f32), axis=0) for values in grad_hidden])
        grad_normed = mm(grad_hidden[0], up_proj[0], NT) + mm(grad_hidden[1], up_proj[1], NT)
        up_grads = [sibling_sum(ring, grad_rows(normed_two, grad_hidden[i])) for i in range(tensor)]
        up_grad = ring_sum(ring, wide_sum(up_grads[0], swap(up_grads[1])).astype(low))
        part, gain_two, shift_two = norm_back(middle, small[3][layer], grad_normed)
        grad_middle = grad + part
        grad_attn = grad_middle.astype(low)
        out_shift = jnp.sum(grad_attn.astype(f32), axis=0)
        grad_heads = jnp.dot(grad_attn, out_proj, preferred_element_type=f32).astype(low)
        out_grad = ring_sum(ring, sibling_sum(ring, grad_rows(grad_attn, heads_out)))
        half = out_grad.shape[1] // 2
        out_grad = wide_sum(out_grad[:, :half], swap(out_grad[:, half:].astype(low)))
        grads = attention_backward(meta, slopes, qkv, kv_first, grad_heads, lse, scale)
        grad_qkv = jnp.concatenate(grads[:3], axis=1)
        grad_first = jnp.concatenate(grads[3:], axis=1)
        sent = mm(grad_first, qkv_proj[:, width:], NT).astype(low)
        arrived = lax.ppermute(sent, "tensor", [(1, 0)])
        qkv_shift = jnp.sum(grad_qkv.astype(f32), axis=0)
        first_shift = jnp.sum(grad_first.astype(f32), axis=0)
        qkv_shift = qkv_shift + jnp.pad(first_shift, (width, 0))
        query_grad = sibling_sum(ring, grad_rows(normed, grad_qkv[:, :width]))
        rest_grad = sibling_sum(ring, grad_rows(normed, grad_qkv[:, width:], (normed_first, grad_first)))
        qkv_grad = jnp.concatenate([ring_sum(ring, query_grad), ring_sum(ring, rest_grad)], axis=1)
        qkv_grad = qkv_grad.reshape(rows, 3, tensor, -1)
        qkv_grad = wide_sum(qkv_grad[:, :, 0], swap(qkv_grad[:, :, 1].astype(low)))
        grad_normed = mm(grad_qkv, qkv_proj, NT) + arrived.astype(f32)
        part, gain_one, shift_one = norm_back(before, small[0][layer], grad_normed)
        grad = grad_middle + part
        weight_grads[layer] = (qkv_grad, out_grad.T, up_grad, down_grad)
        vector_grads[layer] = (gain_one, shift_one, out_shift, gain_two, shift_two, down_shift)
        bias_grads[layer] = (qkv_shift, up_shift)

    input_grad = from_ring(grad, lax.Precision.HIGHEST)[None]
    qkv_grad, out_grad, up_grad, down_grad = [
        jnp.stack([weight_grads[layer][i] for layer in range(layers)]) for i in range(4)
    ]
    vectors = jnp.stack([vector_grads[layer][i] for i in range(6) for layer in range(layers)])
    vectors = from_ring(vectors, lax.Precision.HIGHEST).reshape(6 * layers, dp, tensor, piece).transpose(1, 2, 0, 3)
    qkv_shift = jnp.stack([bias_grads[layer][0] for layer in range(layers)])
    lane = qkv_bias.shape[3]
    qkv_shift = by_half(qkv_shift.reshape(layers, 3, tensor, -1, dp, lane), 2).transpose(4, 2, 0, 1, 3, 5)
    up_shift = jnp.stack([bias_grads[layer][1] for layer in range(layers)])
    up_shift = by_half(up_shift.reshape(layers, tensor, -1, dp, lane), 1).transpose(3, 1, 0, 2, 4)
    packed = jnp.concatenate([member.reshape(dp * tensor, -1) for member in (vectors, qkv_shift, up_shift)], axis=1)
    summed = lax.psum_scatter(packed, ("dp", "tensor"), scatter_dimension=0, tiled=True)[0]
    vectors = summed[:first].reshape(6, layers, piece)
    return (
        final_states,
        input_grad,
        vectors[0],
        vectors[1],
        qkv_grad,
        summed[first:second].reshape(qkv_bias.shape),
        out_grad,
        vectors[2],
        vectors[3],
        vectors[4],
        up_grad,
        summed[second:third].reshape(up_bias.shape),
        down_grad.transpose(0, 2, 1),
        vectors[5],
    )


def solution(mesh):
    return jax.shard_map(
        local,
        mesh=mesh,
        in_specs=(
            P("dp", "tensor", None),
            P("dp", "tensor", None),
            P("dp", "tensor"),
            P("dp"),
            P(None, ("dp", "tensor")),
            P(None, ("dp", "tensor")),
            P(None, "dp", None, "tensor"),
            P(None, None, "tensor", "dp"),
            P(None, "tensor", "dp"),
            P(None, ("dp", "tensor")),
            P(None, ("dp", "tensor")),
            P(None, ("dp", "tensor")),
            P(None, "dp", "tensor"),
            P(None, "tensor", "dp"),
            P(None, "tensor", "dp"),
            P(None, ("dp", "tensor")),
        ),
        out_specs=(
            P("dp", "tensor", None),
            P("dp", "tensor", None),
            P(None, ("dp", "tensor")),
            P(None, ("dp", "tensor")),
            P(None, "dp", None, "tensor"),
            P(None, None, "tensor", "dp"),
            P(None, "tensor", "dp"),
            P(None, ("dp", "tensor")),
            P(None, ("dp", "tensor")),
            P(None, ("dp", "tensor")),
            P(None, "dp", "tensor"),
            P(None, "tensor", "dp"),
            P(None, "tensor", "dp"),
            P(None, ("dp", "tensor")),
        ),
        check_vma=False,
    )
```

```python
import functools

import jax
import jax.numpy as jnp
import numpy as np
from jax import lax
from jax.experimental import pallas as pl
from jax.experimental.pallas import tpu as pltpu
from jax.sharding import PartitionSpec as P

LOG2E = 1.4426950408889634
BIG = 1000000000.0
NT = (((1,), (1,)), ((), ()))
NN = (((1,), (0,)), ((), ()))


def mm(a, b, dims):
    return lax.dot_general(a, b, dims, preferred_element_type=jnp.float32)


def lane_masks(width):
    lanes = lax.broadcasted_iota(jnp.int32, (1, width), 1)
    low = jnp.where(lanes < width // 2, 1.0, 0.0)
    return (low.astype(jnp.bfloat16), (1.0 - low).astype(jnp.bfloat16))


def rows_iota(n, m):
    return lax.broadcasted_iota(jnp.int32, (n, m), 0)


def cols_iota(n, m):
    return lax.broadcasted_iota(jnp.int32, (n, m), 1)


def scores_first(keys, query, slope, scale, prefix, start):
    n, m = (keys.shape[0], query.shape[0])
    key_pos = rows_iota(n, m)
    query_pos = cols_iota(n, m) + start
    distance = jnp.abs(query_pos - key_pos).astype(jnp.float32)
    raw = mm(keys, query, NT) * scale - slope * distance
    visible = (key_pos <= query_pos) | (key_pos < prefix)
    return jnp.where(visible, raw, -BIG)


def scores_second(keys, query, slope, scale, offset, mask_start):
    n, m = (keys.shape[0], query.shape[0])
    bias = slope * (rows_iota(n, 1) + offset).astype(jnp.float32)
    raw = mm(keys, query, NT) * scale + bias
    if mask_start is None:
        return raw
    return jnp.where(rows_iota(n, m) + mask_start <= cols_iota(n, m), raw, -BIG)


def score_parts(half, k_ref, k0_ref, query, slope, scale, prefix, start, step):
    rows = k_ref.shape[0]
    if half == 0:
        return [(None, 0, rows, scores_first(k_ref[...], query, slope, scale, prefix, start))]
    parts = [(0, 0, rows, scores_second(k0_ref[...], query, slope, scale, -2 * rows, None))]
    if start > 0:
        parts.append((1, 0, start, scores_second(k_ref[:start], query, slope, scale, -rows, None)))
    parts.append(
        (1, start, start + step, scores_second(k_ref[start : start + step], query, slope, scale, start - rows, 0))
    )
    return parts


def forward_body(half, slopes, prefix, scale, q_ref, k_ref, v_ref, k0_ref, v0_ref, o_ref, lse_ref, step):
    rows, width = q_ref.shape
    masks = lane_masks(width)
    pair = pl.program_id(0)
    head = width // 2
    values = v_ref[...].T
    values0 = v0_ref[...].T if half else None
    for start in range(0, rows, step):
        outs = []
        for side in range(2):
            query = q_ref[start : start + step] * masks[side]
            slope = slopes[pair * 2 + side]
            parts = score_parts(half, k_ref, k0_ref, query, slope, scale, prefix, start, step)
            top = parts[0][3].max(axis=0, keepdims=True)
            for part in parts[1:]:
                top = jnp.maximum(top, part[3].max(axis=0, keepdims=True))
            total = None
            out = None
            for which, low, high, raw in parts:
                raised = jnp.exp2(raw - top)
                part_sum = raised.sum(axis=0, keepdims=True)
                held = values0 if which == 0 else values
                held = held[side * head : (side + 1) * head, low:high]
                part_out = mm(held, raised.astype(jnp.bfloat16), NN)
                total = part_sum if total is None else total + part_sum
                out = part_out if out is None else out + part_out
            outs.append(out / total)
            lse_ref[0, side : side + 1, start : start + step] = top + jnp.log2(total)
        o_ref[start : start + step] = jnp.concatenate(outs, axis=0).T.astype(jnp.bfloat16)


def forward_kernel(meta, slopes, q_ref, k_ref, v_ref, k0_ref, v0_ref, o_ref, lse_ref, *, scale, step):
    args = (slopes, meta[1], scale, q_ref, k_ref, v_ref, k0_ref, v0_ref, o_ref, lse_ref, step)

    @pl.when(meta[0] == 0)
    def first():
        forward_body(0, *args)

    @pl.when(meta[0] != 0)
    def second():
        forward_body(1, *args)


def attention_forward(meta, slopes, qkv, kv0, scale):
    rows, width = qkv.shape
    pairs = width // 3 // 128
    block = lambda base: pl.BlockSpec((rows, 128), lambda j, *_: (0, base + j))
    return pl.pallas_call(
        functools.partial(forward_kernel, scale=scale * LOG2E, step=rows // 2),
        grid_spec=pltpu.PrefetchScalarGridSpec(
            num_scalar_prefetch=2,
            grid=(pairs,),
            in_specs=[block(0), block(pairs), block(2 * pairs), block(0), block(pairs)],
            out_specs=[block(0), pl.BlockSpec((1, 2, rows), lambda j, *_: (j, 0, 0))],
        ),
        out_shape=[
            jax.ShapeDtypeStruct((rows, width // 3), jnp.bfloat16),
            jax.ShapeDtypeStruct((pairs, 2, rows), jnp.float32),
        ],
        compiler_params=pltpu.CompilerParams(vmem_limit_bytes=40 * 1024 * 1024),
        cost_estimate=pl.CostEstimate(
            flops=pairs * 2 * rows * rows * 128 * 8, bytes_accessed=rows * width * 4, transcendentals=pairs * 4 * rows * rows
        ),
        name="attention_forward",
    )(meta, slopes, qkv, qkv, qkv, kv0, kv0)


def backward_body(half, slopes, prefix, scale, refs, step):
    q_ref, k_ref, v_ref, k0_ref, v0_ref, g_ref, lse_ref, gq_ref, gk_ref, gv_ref, gk0_ref, gv0_ref, sums = refs
    rows, width = q_ref.shape
    masks = lane_masks(width)
    pair = pl.program_id(0)
    head = width // 2
    keys = k_ref[...].T
    keys0 = k0_ref[...].T if half else None
    sums[...] = jnp.zeros_like(sums)
    for start in range(0, rows, step):
        outs = []
        for side in range(2):
            query = q_ref[start : start + step] * masks[side]
            grad = g_ref[start : start + step] * masks[side]
            slope = slopes[pair * 2 + side]
            parts = score_parts(half, k_ref, k0_ref, query, slope, scale * LOG2E, prefix, start, step)
            lse = lse_ref[0, side : side + 1, start : start + step]
            inner = None
            held = []
            for which, low, high, raw in parts:
                share = jnp.exp2(raw - lse)
                value = v0_ref[low:high] if which == 0 else v_ref[low:high]
                slot = 2 if which == 0 else 0
                grad_share = mm(value, grad, NT)
                part = (share * grad_share).sum(axis=0, keepdims=True)
                inner = part if inner is None else inner + part
                sums[slot + 1, low:high] += mm(share.astype(jnp.bfloat16), grad, NN)
                held.append((which, low, high, share, grad_share, slot))
            out = None
            for which, low, high, share, grad_share, slot in held:
                grad_score = (share * (grad_share - inner)).astype(jnp.bfloat16)
                sums[slot, low:high] += mm(grad_score, query, NN)
                key = keys0 if which == 0 else keys
                part = mm(key[side * head : (side + 1) * head, low:high], grad_score, NN)
                out = part if out is None else out + part
            outs.append(out)
        gq_ref[start : start + step] = (jnp.concatenate(outs, axis=0).T * scale).astype(jnp.bfloat16)
    gk_ref[...] = (sums[0] * scale).astype(jnp.bfloat16)
    gv_ref[...] = sums[1].astype(jnp.bfloat16)
    gk0_ref[...] = (sums[2] * scale).astype(jnp.bfloat16)
    gv0_ref[...] = sums[3].astype(jnp.bfloat16)


def backward_kernel(meta, slopes, *refs, scale, step):
    @pl.when(meta[0] == 0)
    def first():
        backward_body(0, slopes, meta[1], scale, refs, step)

    @pl.when(meta[0] != 0)
    def second():
        backward_body(1, slopes, meta[1], scale, refs, step)


def attention_backward(meta, slopes, qkv, kv0, grad_heads, lse, scale):
    rows, width = qkv.shape
    pairs = width // 3 // 128
    block = lambda base: pl.BlockSpec((rows, 128), lambda j, *_: (0, base + j))
    full = jax.ShapeDtypeStruct((rows, width // 3), jnp.bfloat16)
    return pl.pallas_call(
        functools.partial(backward_kernel, scale=scale, step=rows // 2),
        grid_spec=pltpu.PrefetchScalarGridSpec(
            num_scalar_prefetch=2,
            grid=(pairs,),
            in_specs=[
                block(0),
                block(pairs),
                block(2 * pairs),
                block(0),
                block(pairs),
                block(0),
                pl.BlockSpec((1, 2, rows), lambda j, *_: (j, 0, 0)),
            ],
            out_specs=[block(0)] * 5,
            scratch_shapes=[pltpu.VMEM((4, rows, 128), jnp.float32)],
        ),
        out_shape=[full] * 5,
        compiler_params=pltpu.CompilerParams(vmem_limit_bytes=40 * 1024 * 1024),
        cost_estimate=pl.CostEstimate(
            flops=pairs * 2 * rows * rows * 128 * 20, bytes_accessed=rows * width * 8, transcendentals=pairs * 4 * rows * rows
        ),
        name="attention_backward",
    )(meta, slopes, qkv, qkv, qkv, kv0, kv0, grad_heads, lse)


EPS = 1e-05
H = 16
HD = 64
ROWS_CONTRACT = (((0,), (0,)), ((), ()))


def norm_parts(states):
    centered = states - jnp.mean(states, axis=-1, keepdims=True)
    inverse = lax.rsqrt(jnp.mean(centered * centered, axis=-1, keepdims=True) + EPS)
    return (centered * inverse, inverse)


def norm_rows(states, gain, shift):
    return norm_parts(states)[0] * gain + shift


def norm_back(states, gain, grad):
    unit, inverse = norm_parts(states)
    scaled = grad * gain
    first = jnp.mean(scaled, axis=-1, keepdims=True)
    second = jnp.mean(scaled * unit, axis=-1, keepdims=True)
    return (inverse * (scaled - first - unit * second), jnp.sum(grad * unit, axis=0), jnp.sum(grad, axis=0))


def gelu_tanh(values):
    return 0.5 * values * (1.0 + jnp.tanh(0.7978845608028654 * (values + 0.044715 * values * values * values)))


MESH = pl.DeviceIdType.MESH


class Ring:
    def __init__(self, devices):
        self.chips = devices // 2
        self.order = list(range(0, self.chips, 2)) + list(range(self.chips - 1, 0, -2))
        self.place = {chip: spot for spot, chip in enumerate(self.order)}

    def owners(self):
        table = []
        for device in range(2 * self.chips):
            spot = self.place[device // 2]
            table.append(
                [
                    2 * self.order[(spot - step) % self.chips] + ((device % 2) ^ core)
                    for core in range(2)
                    for step in range(self.chips)
                ]
            )
        return np.array(table, np.int32)

    def spot_chip(self, spot):
        half = self.chips // 2
        return jnp.where(spot < half, 2 * spot, 2 * (self.chips - 1 - spot) + 1)

    def neighbours(self):
        here, side = (lax.axis_index("dp"), lax.axis_index("tensor"))
        chip, core = (here // 2, here % 2)
        spot = jnp.where(chip % 2 == 0, chip // 2, self.chips - 1 - chip // 2)
        ahead = self.spot_chip((spot + 1) % self.chips) * 2 + core
        behind = self.spot_chip((spot + self.chips - 1) % self.chips) * 2 + core
        sibling = chip * 2 + (1 - core)
        return ((ahead, side), (behind, side), (sibling, side), (here, 1 - side))


def greet(targets):
    barrier = pltpu.get_barrier_semaphore()
    for target in targets:
        pl.semaphore_signal(barrier, inc=1, device_id=target, device_id_type=MESH)
    pl.semaphore_wait(barrier, len(targets))


class Copies:
    def __init__(self, send, recv, near):
        self.send, self.recv, self.near = (send, recv, near)
        self.sent, self.moved = ([], [])

    def push(self, source, target, device):
        spot = len(self.sent)
        copy = pltpu.make_async_remote_copy(
            src_ref=source,
            dst_ref=target,
            send_sem=self.send.at[spot],
            recv_sem=self.recv.at[spot],
            device_id=device,
            device_id_type=MESH,
        )
        copy.start()
        self.sent.append(copy)
        return copy

    def move(self, source, target):
        copy = pltpu.make_async_copy(source, target, self.near.at[len(self.moved)])
        copy.start()
        self.moved.append(copy)
        return copy

    def finish(self):
        for copy in self.sent:
            copy.wait_send()


def run_all(steps):
    for unused in steps:
        pass


def gather_steps(copies, ids, chips, arrays):
    ahead, behind, sibling, across = ids
    half = chips // 2
    local, siblings, early_in, late_in, up, down = ([], [], [], [], {}, {})
    for shard, own, other, early in arrays:
        early_in.append(copies.push(shard.at[:, pl.ds(0, early)], other.at[0, 0, :, pl.ds(0, early)], across))
    for i, (shard, own, other, early) in enumerate(arrays):
        local.append(copies.move(shard, own.at[0, 0]))
        up[i, 1] = [copies.push(shard, own.at[0, 1], ahead)]
        down[i, 1] = [copies.push(shard, own.at[0, chips - 1], behind)]
        siblings.append(copies.push(shard, own.at[1, 0], sibling))
    for shard, own, other, early in arrays:
        width = shard.shape[1] - early
        late_in.append(copies.push(shard.at[:, pl.ds(early, width)], other.at[0, 0, :, pl.ds(early, width)], across))
    yield
    for i, (shard, own, other, early) in enumerate(arrays):
        early_in[i].wait_recv()
        part = other.at[0, 0, :, pl.ds(0, early)]
        up[i, 1].append(copies.push(part, other.at[0, 1, :, pl.ds(0, early)], ahead))
        down[i, 1].append(copies.push(part, other.at[0, chips - 1, :, pl.ds(0, early)], behind))
    late = [(0, late_in)]
    for hop in range(1, half + 1):
        yield
        spots = [(hop, up, ahead), (chips - hop, down, behind)]
        crossing = {}
        if hop < half:
            for spot, arrivals, target in spots:
                crossing[spot] = []
                step = 1 if target is ahead else -1
                for i, (shard, own, other, early) in enumerate(arrays):
                    size = shard.shape[1]
                    arrivals[i, hop][0].wait_recv()
                    if hop + 1 < half:
                        window, slim = (pl.ds(0, size), pl.ds(0, early))
                    elif step == 1:
                        window, slim = (pl.ds(0, size // 2), pl.ds(0, early // 2))
                    else:
                        window, slim = (pl.ds(size // 2, size // 2), pl.ds(early // 2, early // 2))
                    arrivals[i, hop + 1] = [
                        copies.push(own.at[0, spot, :, window], own.at[0, spot + step, :, window], target)
                    ]
                    rest = pl.ds(early, size - early)
                    crossing[spot].append(copies.push(own.at[0, spot, :, rest], other.at[0, spot, :, rest], across))
                    siblings.append(copies.push(own.at[0, spot], own.at[1, spot], sibling))
                    arrivals[i, hop][1].wait_recv()
                    arrivals[i, hop + 1].append(
                        copies.push(other.at[0, spot, :, slim], other.at[0, spot + step, :, slim], target)
                    )
        else:
            crossing[half] = []
            for i, (shard, own, other, early) in enumerate(arrays):
                up[i, half][0].wait_recv()
                down[i, half][0].wait_recv()
                rest = pl.ds(early, shard.shape[1] - early)
                crossing[half].append(copies.push(own.at[0, half, :, rest], other.at[0, half, :, rest], across))
                siblings.append(copies.push(own.at[0, half], own.at[1, half], sibling))
                up[i, half][1].wait_recv()
                down[i, half][1].wait_recv()
        for spot, arrivals in late:
            for i, (shard, own, other, early) in enumerate(arrays):
                arrivals[i].wait_recv()
                siblings.append(copies.push(other.at[0, spot], other.at[1, spot], sibling))
        late = list(crossing.items())
    yield
    for spot, arrivals in late:
        for i, (shard, own, other, early) in enumerate(arrays):
            arrivals[i].wait_recv()
            siblings.append(copies.push(other.at[0, spot], other.at[1, spot], sibling))
    for copy in local:
        copy.wait()
    yield
    for copy in siblings:
        copy.wait_recv()


def gather_count(chips, arrays):
    half = chips // 2
    return arrays * (5 + 2 + (half - 1) * 2 * 4 + 2 + chips)


def gather_weights(ring, groups, collective):
    flat = [member for group in groups for member in group]
    count = sum(gather_count(ring.chips, len(group)) for group in groups)
    shapes = [
        jax.ShapeDtypeStruct((2, ring.chips) + shard.shape, shard.dtype) for shard, early in flat for unused in range(2)
    ]

    def kernel(*refs):
        shards, outs = (refs[: len(flat)], refs[len(flat) : 3 * len(flat)])
        ids = ring.neighbours()
        greet(ids)
        copies = Copies(*refs[3 * len(flat) :])
        members = [(shards[i], outs[2 * i], outs[2 * i + 1], flat[i][1]) for i in range(len(flat))]
        at = 0
        running = []
        for group in groups:
            running.append(gather_steps(copies, ids, ring.chips, members[at : at + len(group)]))
            at += len(group)
        run_staggered(running, 3)
        copies.finish()

    outs = pl.pallas_call(
        kernel,
        in_specs=[pl.BlockSpec(memory_space=pl.ANY)] * len(flat),
        out_specs=[pl.BlockSpec(memory_space=pl.ANY)] * len(shapes),
        out_shape=shapes,
        scratch_shapes=[
            pltpu.SemaphoreType.DMA((count,)),
            pltpu.SemaphoreType.DMA((count,)),
            pltpu.SemaphoreType.DMA((len(flat),)),
        ],
        compiler_params=pltpu.CompilerParams(collective_id=collective, has_side_effects=True),
        name="gather_weights",
    )(*[shard for shard, early in flat])
    return [out.reshape(-1, out.shape[-1]) for out in outs]


def run_staggered(running, lead):
    waiting = list(running)
    active = []
    youngest = lead
    while waiting or active:
        if waiting and youngest >= lead:
            active.append(waiting.pop(0))
            youngest = 0
        youngest += 1
        for steps in list(active):
            try:
                next(steps)
            except StopIteration:
                active.remove(steps)


def add_rows(target, source):
    rows, columns = target.shape
    step = 256 if columns % 256 == 0 else 128

    @pl.loop(0, columns // step)
    def tile(i):
        window = pl.ds(pl.multiple_of(i * step, step), step)
        target[:, window] = (target[:, window].astype(jnp.float32) + source[:, window].astype(jnp.float32)).astype(
            target.dtype
        )


def scatter_steps(copies, ids, chips, arrays):
    ahead, behind, sibling, across = ids
    half = chips // 2
    blocks = [half] + [spot for hop in range(half - 1, 0, -1) for spot in (chips - hop, hop)] + [0]
    loaded, near = ({}, {})
    for spot in blocks:
        for i, (parts, early, out, room) in enumerate(arrays):
            for e in range(2):
                near[i, e, spot] = copies.push(parts[e][1].at[spot], room["near"].at[e, spot], sibling)
                loaded[i, e, spot] = copies.move(parts[e][0].at[spot], room["sum"].at[e, spot])
    crossed = {}

    def first(spot):
        for e in (1, 0):
            for i, (parts, early, out, room) in enumerate(arrays):
                loaded[i, e, spot].wait()
                near[i, e, spot].wait_recv()
                add_rows(room["sum"].at[e, spot], room["near"].at[e, spot])
                if e == 1:
                    rest = pl.ds(early, out.shape[1] - early)
                    crossed[i, spot] = copies.push(room["sum"].at[1, spot, :, rest], room["far"].at[spot], across)

    def second(spot):
        for i, (parts, early, out, room) in enumerate(arrays):
            rest = pl.ds(early, out.shape[1] - early)
            crossed[i, spot].wait_recv()
            add_rows(room["sum"].at[0, spot, :, rest], room["far"].at[spot])

    def windows(size, hop, upward):
        if hop > 0:
            return pl.ds(0, size)
        return pl.ds(size // 2, size // 2) if upward else pl.ds(0, size // 2)

    def send(hop, spot, upward):
        target = ahead if upward else behind
        kinds = ("up", "up_slim") if upward else ("down", "down_slim")
        out_copies = []
        for i, (parts, early, out, room) in enumerate(arrays):
            for e, size in ((0, out.shape[1]), (1, early)):
                window = windows(size, hop, upward)
                out_copies.append(
                    copies.push(room["sum"].at[e, spot, :, window], room[kinds[e]].at[hop, :, window], target)
                )
        return out_copies

    def receive(hop, spot, upward, arrivals):
        kinds = ("up", "up_slim") if upward else ("down", "down_slim")
        at = 0
        for i, (parts, early, out, room) in enumerate(arrays):
            for e, size in ((0, out.shape[1]), (1, early)):
                window = windows(size, hop, upward)
                arrivals[at].wait_recv()
                add_rows(room["sum"].at[e, spot, :, window], room[kinds[e]].at[hop, :, window])
                at += 1

    yield
    first(half)
    yield
    for spot in blocks[1:3]:
        first(spot)
    second(half)
    up = send(0, half, True)
    down = send(0, half, False)
    for hop in range(1, half):
        yield
        for spot in blocks[2 * hop + 1 : 2 * hop + 3]:
            first(spot)
        second(chips - half + hop)
        second(half - hop)
        receive(hop - 1, chips - half + hop, True, up)
        up = send(hop, chips - half + hop, True)
        receive(hop - 1, half - hop, False, down)
        down = send(hop, half - hop, False)
    yield
    second(0)
    yield
    final = []
    at = 0
    for i, (parts, early, out, room) in enumerate(arrays):
        for e in range(2):
            up[at].wait_recv()
            down[at].wait_recv()
            at += 1
        size = out.shape[1]
        part = room["sum"][1, 0, :, :early].astype(jnp.float32)
        part = part + room["up_slim"][half - 1].astype(jnp.float32) + room["down_slim"][half - 1].astype(jnp.float32)
        room["slim_out"][...] = part.astype(room["slim_out"].dtype)
        final.append(copies.push(room["slim_out"], room["slim_in"], across))
    yield
    for i, (parts, early, out, room) in enumerate(arrays):
        total = room["sum"][0, 0].astype(jnp.float32) + room["up"][half - 1].astype(jnp.float32)
        out[...] = total + room["down"][half - 1].astype(jnp.float32)
        final[i].wait_recv()
        out[:, :early] += room["slim_in"][...].astype(jnp.float32)


def scatter_count(chips, arrays):
    half = chips // 2
    return arrays * (2 * chips + chips + half * 4 + 1)


ROOM = ("sum", "near", "far", "up", "down", "up_slim", "down_slim", "slim_out", "slim_in")


def scatter_room(chips, rows, columns, early, dtype):
    half = chips // 2
    shapes = (
        (2, chips, rows, columns),
        (2, chips, rows, columns),
        (chips, rows, columns - early),
        (half, rows, columns),
        (half, rows, columns),
        (half, rows, early),
        (half, rows, early),
        (rows, early),
        (rows, early),
    )
    return [pltpu.VMEM(shape, dtype) for shape in shapes]


def scatter_grads(ring, arrays, collective):
    chips = ring.chips
    inputs, shapes, rooms = ([], [], [])
    for parts, early in arrays:
        height, columns = parts[0][0].shape
        rows = height // chips
        inputs += [parts[e][c].reshape(chips, rows, columns) for e in range(2) for c in range(2)]
        shapes.append(jax.ShapeDtypeStruct((rows, columns), jnp.float32))
        rooms += scatter_room(chips, rows, columns, early, parts[0][0].dtype)
    total = len(arrays)

    def kernel(*refs):
        ins, outs, scratch = (refs[: 4 * total], refs[4 * total : 5 * total], refs[5 * total :])
        ids = ring.neighbours()
        greet(ids)
        copies = Copies(*scratch[len(rooms) :])
        members = []
        for i in range(total):
            parts = [[ins[4 * i + 2 * e + c] for c in range(2)] for e in range(2)]
            room = dict(zip(ROOM, scratch[i * len(ROOM) : (i + 1) * len(ROOM)]))
            members.append((parts, arrays[i][1], outs[i], room))
        run_all(scatter_steps(copies, ids, chips, members))
        copies.finish()

    return pl.pallas_call(
        kernel,
        in_specs=[pl.BlockSpec(memory_space=pl.ANY)] * (4 * total),
        out_specs=[pl.BlockSpec(memory_space=pltpu.VMEM)] * total,
        out_shape=shapes,
        scratch_shapes=rooms
        + [
            pltpu.SemaphoreType.DMA((scatter_count(chips, total),)),
            pltpu.SemaphoreType.DMA((scatter_count(chips, total),)),
            pltpu.SemaphoreType.DMA((2 * chips * total,)),
        ],
        compiler_params=pltpu.CompilerParams(
            collective_id=collective, has_side_effects=True, vmem_limit_bytes=56 * 1024 * 1024
        ),
        name="scatter_grads",
    )(*inputs)


def wide_sum(left, right):
    return left.astype(jnp.float32) + right.astype(jnp.float32)


def grad_parts(left, right, extra=None):
    half = left.shape[1] // 2
    parts = []
    for core in range(2):
        columns = slice(core * half, (core + 1) * half)
        out = lax.dot_general(left[:, columns], right, ROWS_CONTRACT, preferred_element_type=jnp.float32)
        if extra is not None:
            more = lax.dot_general(extra[0][:, columns], extra[1], ROWS_CONTRACT, preferred_element_type=jnp.float32)
            out = out + more
        parts.append(out.astype(jnp.bfloat16))
    return parts


def small_parts(vector_grads, bias_grads, by_half, placed, piece, lane):
    layers, dp = (len(vector_grads), placed.shape[0])
    vectors = jnp.stack([vector_grads[layer][i] for i in range(6) for layer in range(layers)])
    vectors = by_half(vectors.reshape(6 * layers, dp, 2, piece).transpose(2, 1, 0, 3), 0).reshape(2, dp, -1)
    shifts = [jnp.stack([bias_grads[layer][i] for layer in range(layers)], axis=1) for i in range(2)]
    shifts = jnp.concatenate([member.reshape(2, -1, dp, lane) for member in shifts], axis=1)
    shifts = jnp.einsum("tndl,bd->tbnl", shifts, placed, precision=lax.Precision.HIGHEST).reshape(2, dp, -1)
    packed = jnp.concatenate([vectors, shifts], axis=2)
    packed = jnp.pad(packed, ((0, 0), (0, 0), (0, 8 * 512 - packed.shape[2]))).reshape(2, 2, -1, 512)
    return [[packed[e, c] for c in range(2)] for e in range(2)]


def local(
    states_in,
    teacher,
    valid_mask,
    prefix_len,
    ln1_gain,
    ln1_shift,
    qkv_weight,
    qkv_bias,
    out_weight,
    out_bias,
    ln2_gain,
    ln2_shift,
    up_weight,
    up_bias,
    down_weight,
    down_bias,
):
    f32, low = (jnp.float32, jnp.bfloat16)
    layers, local_rows = (qkv_weight.shape[0], states_in.shape[1])
    width = states_in.shape[2]
    dp, tensor = (lax.axis_size("dp"), lax.axis_size("tensor"))
    here, side = (lax.axis_index("dp"), lax.axis_index("tensor"))
    ring = Ring(dp)
    piece = width // (dp * tensor)

    def by_half(pair, axis):
        return jnp.where(side == 0, pair, jnp.flip(pair, axis))

    owners = lax.dynamic_index_in_dim(jnp.asarray(ring.owners()), here, 0, keepdims=False)
    rows = width // dp
    columns = (owners[:, None] * rows + jnp.arange(rows, dtype=jnp.int32)[None]).reshape(1, width)
    to_ring = (jnp.arange(width, dtype=jnp.int32)[:, None] == columns).astype(low)

    placed = (owners[:, None] == jnp.arange(dp, dtype=jnp.int32)[None]).astype(f32)

    def into_ring(values):
        return jnp.dot(values, to_ring, preferred_element_type=f32)

    def from_ring(values, precision=None):
        return lax.dot_general(
            values, to_ring.astype(values.dtype), NT, precision=precision, preferred_element_type=f32
        )

    count = jnp.sum(valid_mask)
    vectors = jnp.stack([ln1_gain, ln1_shift, out_bias, ln2_gain, ln2_shift, down_bias])
    packed = jnp.concatenate(
        [vectors.reshape(-1), qkv_bias.reshape(-1), up_bias.reshape(-1), jnp.stack([count // 256, count % 256]).astype(low)]
    )
    first, second, third = (vectors.size, vectors.size + qkv_bias.size, vectors.size + qkv_bias.size + up_bias.size)
    packed = jnp.pad(packed, (0, 16 * 512 - packed.size)).reshape(16, 512)
    groups = []
    for layer in range(layers):
        groups.append([(qkv_weight[layer].reshape(rows, -1), 512), (out_weight[layer].T, 256)])
        groups.append([(up_weight[layer], 768), (down_weight[layer].T, 768)])
    groups[0].insert(0, (packed, 256))
    gathered = gather_weights(ring, groups, 1)
    everything = by_half(jnp.stack([member.reshape(dp, -1) for member in gathered[:2]]), 0)
    gathered = gathered[2:]
    vectors = everything[:, :, :first].reshape(tensor, dp, 6, layers, piece).transpose(2, 3, 1, 0, 4)
    small = vectors.reshape(6, layers, 1, width).astype(f32)
    lane = qkv_bias.shape[3]
    biases = everything[:, :, first:third].reshape(tensor, dp, -1, lane)
    biases = jnp.einsum("tbnl,bd->tndl", biases, placed.astype(low), preferred_element_type=f32)
    biases = by_half(biases.reshape(tensor, -1, dp * lane), 0)
    split = (second - first) // lane
    qkv_add = biases[:, :split].reshape(tensor, layers, 1, -1).transpose(1, 0, 2, 3)
    up_add = biases[:, split:].reshape(tensor, layers, 1, -1).transpose(1, 0, 2, 3)
    counts = jnp.sum(everything[:, :, third : third + 2].astype(f32), axis=(0, 1))
    valid_count = counts[0] * 256.0 + counts[1]

    scale = HD ** (-0.5)
    pieces = jnp.arange(H, dtype=jnp.int32)
    heads_half = H // tensor
    heads = (pieces // heads_half ^ side) * heads_half + pieces % heads_half
    slopes = jnp.exp2(-(heads.astype(f32) + 1.0) * 8.0 / H) * LOG2E
    meta = jnp.stack([side.astype(jnp.int32), prefix_len[0]])

    before_first = lax.ppermute(states_in[0], "tensor", [(0, 1)])
    states = into_ring(states_in[0])
    target = into_ring(teacher[0])
    kept = []
    for layer in range(layers):
        qkv_proj, out_proj, up_proj, down_proj = [gathered[8 * layer + i : 8 * layer + i + 2] for i in (0, 2, 4, 6)]
        normed = norm_rows(states, small[0][layer], small[1][layer]).astype(low)
        if layer == 0:
            normed_first = norm_rows(into_ring(before_first), small[0][layer], small[1][layer]).astype(low)
        else:
            normed_first = lax.ppermute(normed, "tensor", [(0, 1)])
        qkv, kv_first, heads_out, lse = ([], [], [], [])
        for i in range(tensor):
            query = qkv_proj[i].shape[1] // 3
            mixed = jnp.dot(normed, qkv_proj[i], preferred_element_type=f32) + qkv_add[layer][i]
            qkv.append(mixed.astype(low))
            mixed = jnp.dot(normed_first, qkv_proj[i][:, query:], preferred_element_type=f32)
            kv_first.append((mixed + qkv_add[layer][i][:, query:]).astype(low))
            made, total = attention_forward(meta, slopes[i * heads_half : (i + 1) * heads_half], qkv[i], kv_first[i], scale)
            heads_out.append(made)
            lse.append(total)
        middle = states + mm(heads_out[0], out_proj[0], NT) + mm(heads_out[1], out_proj[1], NT) + small[2][layer]
        normed_two = norm_rows(middle, small[3][layer], small[4][layer]).astype(low)
        hidden = [jnp.dot(normed_two, up_proj[i], preferred_element_type=f32) + up_add[layer][i] for i in range(tensor)]
        active = [gelu_tanh(values).astype(low) for values in hidden]
        kept.append((states, normed, normed_first, qkv, kv_first, lse, heads_out, middle, normed_two, hidden, active))
        states = middle + mm(active[0], down_proj[0], NT) + mm(active[1], down_proj[1], NT) + small[5][layer]

    final_states = from_ring(states.astype(low)).astype(low)[None]
    factor = local_rows * tensor * dp / valid_count
    grad = factor * valid_mask[0][:, None].astype(f32) * (states - target)
    weight_grads = [None] * layers
    vector_grads = [None] * layers
    bias_grads = [None] * layers
    for layer in reversed(range(layers)):
        before, normed, normed_first, qkv, kv_first, lse, heads_out, middle, normed_two, hidden, active = kept[layer]
        qkv_proj, out_proj, up_proj, down_proj = [gathered[8 * layer + i : 8 * layer + i + 2] for i in (0, 2, 4, 6)]
        grad_mlp = grad.astype(low)
        down_shift = jnp.sum(grad_mlp.astype(f32), axis=0)
        grad_hidden = []
        for i in range(tensor):
            grad_active = jnp.dot(grad_mlp, down_proj[i], preferred_element_type=f32)
            grad_hidden.append(jax.vjp(gelu_tanh, hidden[i])[1](grad_active)[0].astype(low))
        down_parts = [grad_parts(grad_mlp, active[i]) for i in range(tensor)]
        up_shift = jnp.stack([jnp.sum(values.astype(f32), axis=0) for values in grad_hidden])
        grad_normed = mm(grad_hidden[0], up_proj[0], NT) + mm(grad_hidden[1], up_proj[1], NT)
        up_parts = [grad_parts(normed_two, grad_hidden[i]) for i in range(tensor)]
        up_grad, down_grad = scatter_grads(ring, [(up_parts, 768), (down_parts, 768)], 2 + 2 * layer)
        part, gain_two, shift_two = norm_back(middle, small[3][layer], grad_normed)
        grad_middle = grad + part
        grad_attn = grad_middle.astype(low)
        out_shift = jnp.sum(grad_attn.astype(f32), axis=0)
        grad_normed = 0.0
        qkv_shift = []
        sent = 0.0
        query_parts, rest_parts, out_parts = ([], [], [])
        for i in range(tensor):
            grad_heads = jnp.dot(grad_attn, out_proj[i], preferred_element_type=f32).astype(low)
            out_parts.append(grad_parts(grad_attn, heads_out[i]))
            grads = attention_backward(
                meta, slopes[i * heads_half : (i + 1) * heads_half], qkv[i], kv_first[i], grad_heads, lse[i], scale
            )
            grad_qkv = jnp.concatenate(grads[:3], axis=1)
            grad_first = jnp.concatenate(grads[3:], axis=1)
            query = grads[0].shape[1]
            sent = sent + mm(grad_first, qkv_proj[i][:, query:], NT)
            query_parts.append(grad_parts(normed, grads[0]))
            rest_parts.append(grad_parts(normed, grad_qkv[:, query:], (normed_first, grad_first)))
            shift = jnp.sum(grad_qkv.astype(f32), axis=0)
            qkv_shift.append(shift + jnp.pad(jnp.sum(grad_first.astype(f32), axis=0), (query, 0)))
            grad_normed = grad_normed + mm(grad_qkv, qkv_proj[i], NT)
        arrived = lax.ppermute(sent.astype(low), "tensor", [(1, 0)])
        qkv_shift = jnp.stack(qkv_shift)
        projections = [(query_parts, 256), (rest_parts, 256), (out_parts, 256)]
        grad_normed = grad_normed + arrived.astype(f32)
        part, gain_one, shift_one = norm_back(before, small[0][layer], grad_normed)
        grad = grad_middle + part
        vector_grads[layer] = (gain_one, shift_one, out_shift, gain_two, shift_two, down_shift)
        bias_grads[layer] = (qkv_shift, up_shift)
        if layer == 0:
            projections.append((small_parts(vector_grads, bias_grads, by_half, placed, piece, lane), 256))
        query_grad, rest_grad, out_grad, *last = scatter_grads(ring, projections, 3 + 2 * layer)
        qkv_grad = jnp.concatenate([query_grad, rest_grad], axis=1).reshape(rows, 3, -1)
        weight_grads[layer] = (qkv_grad, out_grad.T, up_grad, down_grad)

    input_grad = from_ring(grad, lax.Precision.HIGHEST)[None]
    qkv_grad, out_grad, up_grad, down_grad = [
        jnp.stack([weight_grads[layer][i] for layer in range(layers)]) for i in range(4)
    ]
    summed = last[0].reshape(-1)
    vectors = summed[:first].reshape(6, layers, piece)
    return (
        final_states,
        input_grad,
        vectors[0],
        vectors[1],
        qkv_grad,
        summed[first:second].reshape(qkv_bias.shape),
        out_grad,
        vectors[2],
        vectors[3],
        vectors[4],
        up_grad,
        summed[second:third].reshape(up_bias.shape),
        down_grad.transpose(0, 2, 1),
        vectors[5],
    )


def solution(mesh):
    return jax.shard_map(
        local,
        mesh=mesh,
        in_specs=(
            P("dp", "tensor", None),
            P("dp", "tensor", None),
            P("dp", "tensor"),
            P("dp"),
            P(None, ("dp", "tensor")),
            P(None, ("dp", "tensor")),
            P(None, "dp", None, "tensor"),
            P(None, None, "tensor", "dp"),
            P(None, "tensor", "dp"),
            P(None, ("dp", "tensor")),
            P(None, ("dp", "tensor")),
            P(None, ("dp", "tensor")),
            P(None, "dp", "tensor"),
            P(None, "tensor", "dp"),
            P(None, "tensor", "dp"),
            P(None, ("dp", "tensor")),
        ),
        out_specs=(
            P("dp", "tensor", None),
            P("dp", "tensor", None),
            P(None, ("dp", "tensor")),
            P(None, ("dp", "tensor")),
            P(None, "dp", None, "tensor"),
            P(None, None, "tensor", "dp"),
            P(None, "tensor", "dp"),
            P(None, ("dp", "tensor")),
            P(None, ("dp", "tensor")),
            P(None, ("dp", "tensor")),
            P(None, "dp", "tensor"),
            P(None, "tensor", "dp"),
            P(None, "tensor", "dp"),
            P(None, ("dp", "tensor")),
        ),
        check_vma=False,
    )
```

```python
import functools

import jax
import jax.numpy as jnp
import numpy as np
from jax import lax
from jax.experimental import pallas as pl
from jax.experimental.pallas import tpu as pltpu
from jax.sharding import PartitionSpec as P

LOG2E = 1.4426950408889634
BIG = 1000000000.0
NT = (((1,), (1,)), ((), ()))
NN = (((1,), (0,)), ((), ()))


def mm(a, b, dims):
    return lax.dot_general(a, b, dims, preferred_element_type=jnp.float32)


def lane_masks(width):
    lanes = lax.broadcasted_iota(jnp.int32, (1, width), 1)
    low = jnp.where(lanes < width // 2, 1.0, 0.0)
    return (low.astype(jnp.bfloat16), (1.0 - low).astype(jnp.bfloat16))


def rows_iota(n, m):
    return lax.broadcasted_iota(jnp.int32, (n, m), 0)


def cols_iota(n, m):
    return lax.broadcasted_iota(jnp.int32, (n, m), 1)


def scores_first(keys, query, slope, scale, prefix, start):
    n, m = (keys.shape[0], query.shape[0])
    key_pos = rows_iota(n, m)
    query_pos = cols_iota(n, m) + start
    distance = jnp.abs(query_pos - key_pos).astype(jnp.float32)
    raw = mm(keys, query, NT) * scale - slope * distance
    visible = (key_pos <= query_pos) | (key_pos < prefix)
    return jnp.where(visible, raw, -BIG)


def scores_second(keys, query, slope, scale, offset, mask_start):
    n, m = (keys.shape[0], query.shape[0])
    bias = slope * (rows_iota(n, 1) + offset).astype(jnp.float32)
    raw = mm(keys, query, NT) * scale + bias
    if mask_start is None:
        return raw
    return jnp.where(rows_iota(n, m) + mask_start <= cols_iota(n, m), raw, -BIG)


def score_parts(half, k_ref, k0_ref, query, slope, scale, prefix, start, step):
    rows = k_ref.shape[0]
    if half == 0:
        return [(None, 0, rows, scores_first(k_ref[...], query, slope, scale, prefix, start))]
    parts = [(0, 0, rows, scores_second(k0_ref[...], query, slope, scale, -2 * rows, None))]
    if start > 0:
        parts.append((1, 0, start, scores_second(k_ref[:start], query, slope, scale, -rows, None)))
    parts.append(
        (1, start, start + step, scores_second(k_ref[start : start + step], query, slope, scale, start - rows, 0))
    )
    return parts


def forward_body(half, pair, slopes, prefix, scale, q_ref, k_ref, v_ref, k0_ref, v0_ref, o_ref, lse_ref, step):
    rows, width = q_ref.shape
    masks = lane_masks(width)
    head = width // 2
    values = v_ref[...].T
    values0 = v0_ref[...].T if half else None
    for start in range(0, rows, step):
        outs = []
        for side in range(2):
            query = q_ref[start : start + step] * masks[side]
            slope = slopes[pair * 2 + side]
            parts = score_parts(half, k_ref, k0_ref, query, slope, scale, prefix, start, step)
            top = parts[0][3].max(axis=0, keepdims=True)
            for part in parts[1:]:
                top = jnp.maximum(top, part[3].max(axis=0, keepdims=True))
            total = None
            out = None
            for which, low, high, raw in parts:
                raised = jnp.exp2(raw - top)
                part_sum = raised.sum(axis=0, keepdims=True)
                held = values0 if which == 0 else values
                held = held[side * head : (side + 1) * head, low:high]
                part_out = mm(held, raised.astype(jnp.bfloat16), NN)
                total = part_sum if total is None else total + part_sum
                out = part_out if out is None else out + part_out
            outs.append(out / total)
            lse_ref[0, side : side + 1, start : start + step] = top + jnp.log2(total)
        o_ref[start : start + step] = jnp.concatenate(outs, axis=0).T.astype(jnp.bfloat16)


def backward_body(half, pair, slopes, prefix, scale, refs, step):
    q_ref, k_ref, v_ref, k0_ref, v0_ref, g_ref, lse_ref, gq_ref, gk_ref, gv_ref, gk0_ref, gv0_ref, sums = refs
    rows, width = q_ref.shape
    masks = lane_masks(width)
    head = width // 2
    keys = k_ref[...].T
    keys0 = k0_ref[...].T if half else None
    sums[...] = jnp.zeros_like(sums)
    for start in range(0, rows, step):
        outs = []
        for side in range(2):
            query = q_ref[start : start + step] * masks[side]
            grad = g_ref[start : start + step] * masks[side]
            slope = slopes[pair * 2 + side]
            parts = score_parts(half, k_ref, k0_ref, query, slope, scale * LOG2E, prefix, start, step)
            lse = lse_ref[0, side : side + 1, start : start + step]
            inner = None
            held = []
            for which, low, high, raw in parts:
                share = jnp.exp2(raw - lse)
                value = v0_ref[low:high] if which == 0 else v_ref[low:high]
                slot = 2 if which == 0 else 0
                grad_share = mm(value, grad, NT)
                part = (share * grad_share).sum(axis=0, keepdims=True)
                inner = part if inner is None else inner + part
                sums[slot + 1, low:high] += mm(share.astype(jnp.bfloat16), grad, NN)
                held.append((which, low, high, share, grad_share, slot))
            out = None
            for which, low, high, share, grad_share, slot in held:
                grad_score = (share * (grad_share - inner)).astype(jnp.bfloat16)
                sums[slot, low:high] += mm(grad_score, query, NN)
                key = keys0 if which == 0 else keys
                part = mm(key[side * head : (side + 1) * head, low:high], grad_score, NN)
                out = part if out is None else out + part
            outs.append(out)
        gq_ref[start : start + step] = (jnp.concatenate(outs, axis=0).T * scale).astype(jnp.bfloat16)
    gk_ref[...] = (sums[0] * scale).astype(jnp.bfloat16)
    gv_ref[...] = sums[1].astype(jnp.bfloat16)
    gk0_ref[...] = (sums[2] * scale).astype(jnp.bfloat16)
    gv0_ref[...] = sums[3].astype(jnp.bfloat16)


def head_pairs(low, high, body):
    @pl.loop(low, high)
    def step(pair):
        columns = pl.multiple_of(pair * 128, 128)
        for half in range(2):
            @pl.when(lax.axis_index("tensor") == half)
            def one():
                body(half, pair, columns)


def forward_work(parts, slopes, prefix, scale):
    work = []
    for e, (qkv, first, out, lse) in enumerate(parts):
        pairs = out.shape[1] // 128
        rows = out.shape[0]

        def body(half, pair, columns, e=e, qkv=qkv, first=first, out=out, lse=lse, pairs=pairs, rows=rows):
            at = lambda ref, base: ref.at[:, pl.ds(columns + base * pairs * 128, 128)]
            forward_body(
                half,
                pair + e * pairs,
                slopes,
                prefix,
                scale * LOG2E,
                at(qkv, 0),
                at(qkv, 1),
                at(qkv, 2),
                at(first, 0),
                at(first, 1),
                at(out, 0),
                lse.at[pl.ds(pair, 1)],
                rows // 2,
            )

        work.append(functools.partial(head_pairs, 0, pairs, body))
    return work


def backward_work(parts, slopes, prefix, scale, sums):
    work = []
    for e, (qkv, first, grad, lse, outs) in enumerate(parts):
        pairs = grad.shape[1] // 128
        rows = grad.shape[0]

        def body(half, pair, columns, e=e, qkv=qkv, first=first, grad=grad, lse=lse, outs=outs, pairs=pairs, rows=rows):
            at = lambda ref, base: ref.at[:, pl.ds(columns + base * pairs * 128, 128)]
            refs = [at(qkv, 0), at(qkv, 1), at(qkv, 2), at(first, 0), at(first, 1), at(grad, 0), lse.at[pl.ds(pair, 1)]]
            refs += [at(out, 0) for out in outs] + [sums]
            backward_body(half, pair + e * pairs, slopes, prefix, scale, refs, rows // 2)

        for low in range(0, pairs, 2):
            work.append(functools.partial(head_pairs, low, low + 2, body))
    return work


EPS = 1e-05
H = 16
HD = 64
ROWS_CONTRACT = (((0,), (0,)), ((), ()))


def norm_parts(states):
    centered = states - jnp.mean(states, axis=-1, keepdims=True)
    inverse = lax.rsqrt(jnp.mean(centered * centered, axis=-1, keepdims=True) + EPS)
    return (centered * inverse, inverse)


def norm_rows(states, gain, shift):
    return norm_parts(states)[0] * gain + shift


def norm_back(states, gain, grad):
    unit, inverse = norm_parts(states)
    scaled = grad * gain
    first = jnp.mean(scaled, axis=-1, keepdims=True)
    second = jnp.mean(scaled * unit, axis=-1, keepdims=True)
    return (inverse * (scaled - first - unit * second), jnp.sum(grad * unit, axis=0), jnp.sum(grad, axis=0))


def gelu_tanh(values):
    return 0.5 * values * (1.0 + jnp.tanh(0.7978845608028654 * (values + 0.044715 * values * values * values)))


MESH = pl.DeviceIdType.MESH


class Ring:
    def __init__(self, devices):
        self.chips = devices // 2
        self.order = list(range(0, self.chips, 2)) + list(range(self.chips - 1, 0, -2))
        self.place = {chip: spot for spot, chip in enumerate(self.order)}
        half = self.chips // 2
        self.turns = [half] + [step for hop in range(half - 1, 0, -1) for step in (self.chips - hop, hop)] + [0]

    def owners(self):
        table = []
        for device in range(2 * self.chips):
            spot = self.place[device // 2]
            table.append(
                [
                    2 * self.order[(spot - step) % self.chips] + ((device % 2) ^ core)
                    for core in range(2)
                    for step in self.turns
                ]
            )
        return np.array(table, np.int32)

    def spot_chip(self, spot):
        half = self.chips // 2
        return jnp.where(spot < half, 2 * spot, 2 * (self.chips - 1 - spot) + 1)

    def neighbours(self):
        here, side = (lax.axis_index("dp"), lax.axis_index("tensor"))
        chip, core = (here // 2, here % 2)
        spot = jnp.where(chip % 2 == 0, chip // 2, self.chips - 1 - chip // 2)
        ahead = self.spot_chip((spot + 1) % self.chips) * 2 + core
        behind = self.spot_chip((spot + self.chips - 1) % self.chips) * 2 + core
        sibling = chip * 2 + (1 - core)
        return ((ahead, side), (behind, side), (sibling, side), (here, 1 - side))


def greet(targets):
    barrier = pltpu.get_barrier_semaphore()
    for target in targets:
        pl.semaphore_signal(barrier, inc=1, device_id=target, device_id_type=MESH)
    pl.semaphore_wait(barrier, len(targets))


class Copies:
    def __init__(self, send, recv, near):
        self.send, self.recv, self.near = (send, recv, near)
        self.sent, self.moved, self.spots = ([], [], 0)

    def push(self, source, target, device):
        spot = self.spots
        copy = pltpu.make_async_remote_copy(
            src_ref=source,
            dst_ref=target,
            send_sem=self.send.at[spot],
            recv_sem=self.recv.at[spot],
            device_id=device,
            device_id_type=MESH,
        )
        copy.start()
        self.sent.append(copy)
        self.spots += 1
        return copy

    def move(self, source, target):
        copy = pltpu.make_async_copy(source, target, self.near.at[len(self.moved)])
        copy.start()
        self.moved.append(copy)
        return copy

    def settle(self, copy):
        copy.wait_send()
        self.sent = [other for other in self.sent if other is not copy]

    def finish(self):
        for copy in self.sent:
            copy.wait_send()


def run_all(steps):
    for unused in steps:
        pass


def gather_steps(copies, ids, ring, arrays):
    ahead, behind, sibling, across = ids
    chips = ring.chips
    half = chips // 2
    slot = ring.turns.index
    local, siblings, early_in, late_in, up, down = ([], [], [], [], {}, {})
    for shard, own, other, early in arrays:
        early_in.append(copies.push(shard.at[:, pl.ds(0, early)], other.at[0, slot(0), :, pl.ds(0, early)], across))
    for i, (shard, own, other, early) in enumerate(arrays):
        local.append(copies.move(shard, own.at[0, slot(0)]))
        up[i, 1] = [copies.push(shard, own.at[0, slot(1)], ahead)]
        down[i, 1] = [copies.push(shard, own.at[0, slot(chips - 1)], behind)]
        siblings.append(copies.push(shard, own.at[1, slot(0)], sibling))
    for shard, own, other, early in arrays:
        width = shard.shape[1] - early
        late_in.append(copies.push(shard.at[:, pl.ds(early, width)], other.at[0, slot(0), :, pl.ds(early, width)], across))
    yield
    for i, (shard, own, other, early) in enumerate(arrays):
        early_in[i].wait_recv()
        part = other.at[0, slot(0), :, pl.ds(0, early)]
        up[i, 1].append(copies.push(part, other.at[0, slot(1), :, pl.ds(0, early)], ahead))
        down[i, 1].append(copies.push(part, other.at[0, slot(chips - 1), :, pl.ds(0, early)], behind))
    late = [(0, late_in)]
    for hop in range(1, half + 1):
        yield
        spots = [(hop, up, ahead), (chips - hop, down, behind)]
        crossing = {}
        if hop < half:
            for spot, arrivals, target in spots:
                crossing[spot] = []
                step = 1 if target is ahead else -1
                for i, (shard, own, other, early) in enumerate(arrays):
                    size = shard.shape[1]
                    arrivals[i, hop][0].wait_recv()
                    if hop + 1 < half:
                        window, slim = (pl.ds(0, size), pl.ds(0, early))
                    elif step == 1:
                        window, slim = (pl.ds(0, size // 2), pl.ds(0, early // 2))
                    else:
                        window, slim = (pl.ds(size // 2, size // 2), pl.ds(early // 2, early // 2))
                    arrivals[i, hop + 1] = [
                        copies.push(own.at[0, slot(spot), :, window], own.at[0, slot(spot + step), :, window], target)
                    ]
                    rest = pl.ds(early, size - early)
                    crossing[spot].append(copies.push(own.at[0, slot(spot), :, rest], other.at[0, slot(spot), :, rest], across))
                    siblings.append(copies.push(own.at[0, slot(spot)], own.at[1, slot(spot)], sibling))
                    arrivals[i, hop][1].wait_recv()
                    arrivals[i, hop + 1].append(
                        copies.push(other.at[0, slot(spot), :, slim], other.at[0, slot(spot + step), :, slim], target)
                    )
        else:
            crossing[half] = []
            for i, (shard, own, other, early) in enumerate(arrays):
                up[i, half][0].wait_recv()
                down[i, half][0].wait_recv()
                rest = pl.ds(early, shard.shape[1] - early)
                crossing[half].append(copies.push(own.at[0, slot(half), :, rest], other.at[0, slot(half), :, rest], across))
                siblings.append(copies.push(own.at[0, slot(half)], own.at[1, slot(half)], sibling))
                up[i, half][1].wait_recv()
                down[i, half][1].wait_recv()
        for spot, arrivals in late:
            for i, (shard, own, other, early) in enumerate(arrays):
                arrivals[i].wait_recv()
                siblings.append(copies.push(other.at[0, slot(spot)], other.at[1, slot(spot)], sibling))
        late = list(crossing.items())
    yield
    for spot, arrivals in late:
        for i, (shard, own, other, early) in enumerate(arrays):
            arrivals[i].wait_recv()
            siblings.append(copies.push(other.at[0, slot(spot)], other.at[1, slot(spot)], sibling))
    for copy in local:
        copy.wait()
    yield
    for copy in siblings:
        copy.wait_recv()


def gather_count(chips, arrays):
    half = chips // 2
    return arrays * (5 + 2 + (half - 1) * 2 * 4 + 2 + chips)


def on_vmem(count):
    return [pl.BlockSpec(memory_space=pltpu.VMEM)] * count


def on_smem(count):
    return [pl.BlockSpec(memory_space=pltpu.SMEM)] * count


def anywhere(count):
    return [pl.BlockSpec(memory_space=pl.ANY)] * count


def gather_weights(ring, groups, collective, attention=None):
    flat = [member for group in groups for member in group]
    total = len(flat)
    count = sum(gather_count(ring.chips, len(group)) for group in groups)
    shapes = [
        jax.ShapeDtypeStruct((2, ring.chips) + shard.shape, shard.dtype) for shard, early in flat for unused in range(2)
    ]
    inputs, more = ([], [])
    if attention is not None:
        qkv, first, slopes, prefix, scale = attention
        inputs = list(qkv) + list(first) + [slopes, prefix]
        rows, width = (qkv[0].shape[0], qkv[0].shape[1] // 3)
        more = [jax.ShapeDtypeStruct((rows, width), jnp.bfloat16)] * 2
        more += [jax.ShapeDtypeStruct((width // 128, 2, rows), jnp.float32)] * 2

    def kernel(*refs):
        shards, extra, refs = (refs[:total], refs[total : total + len(inputs)], refs[total + len(inputs) :])
        outs, made, scratch = (refs[: 2 * total], refs[2 * total : 2 * total + len(more)], refs[2 * total + len(more) :])
        ids = ring.neighbours()
        greet(ids)
        copies = Copies(*scratch)
        members = [(shards[i], outs[2 * i], outs[2 * i + 1], flat[i][1]) for i in range(total)]
        at = 0
        running = []
        for group in groups:
            running.append(gather_steps(copies, ids, ring, members[at : at + len(group)]))
            at += len(group)
        work = []
        if attention is not None:
            parts = [(extra[e], extra[2 + e], made[e], made[2 + e]) for e in range(2)]
            work = forward_work(parts, extra[4], extra[5][0], scale)
        run_staggered(running, 3, work)
        copies.finish()

    outs = pl.pallas_call(
        kernel,
        in_specs=anywhere(total) + (on_vmem(4) + on_smem(2) if inputs else []),
        out_specs=anywhere(len(shapes)) + on_vmem(len(more)),
        out_shape=shapes + more,
        scratch_shapes=[
            pltpu.SemaphoreType.DMA((count,)),
            pltpu.SemaphoreType.DMA((count,)),
            pltpu.SemaphoreType.DMA((total,)),
        ],
        compiler_params=pltpu.CompilerParams(
            collective_id=collective, has_side_effects=True, vmem_limit_bytes=40 * 1024 * 1024
        ),
        name="gather_weights",
    )(*[shard for shard, early in flat], *inputs)
    weights = [out.reshape(-1, out.shape[-1]) for out in outs[: 2 * total]]
    return (weights, outs[2 * total : 2 * total + 2], outs[2 * total + 2 :])


def run_staggered(running, lead, work=()):
    waiting, work = (list(running), list(work))
    active = []
    youngest = lead
    while waiting or active:
        if waiting and youngest >= lead:
            active.append(waiting.pop(0))
            youngest = 0
        youngest += 1
        for steps in list(active):
            try:
                next(steps)
            except StopIteration:
                active.remove(steps)
        if work:
            work.pop(0)()
    for piece in work:
        piece()


def add_rows(target, source):
    rows, columns = target.shape
    step = 256 if columns % 256 == 0 else 128

    @pl.loop(0, columns // step)
    def tile(i):
        window = pl.ds(pl.multiple_of(i * step, step), step)
        target[:, window] = (target[:, window].astype(jnp.float32) + source[:, window].astype(jnp.float32)).astype(
            target.dtype
        )


def products(lefts, rights, held, columns, target, near):
    for i, left in enumerate(lefts):
        held[i] = left[:, columns].T
    blocks, rows, width = target.shape
    step = 512

    @pl.loop(0, width // step)
    def tile(i):
        window = pl.ds(pl.multiple_of(i * step, step), step)
        out = mm(held[0], rights[0][:, window], NN)
        for j in range(1, len(rights)):
            out = out + mm(held[j], rights[j][:, window], NN)
        out = out.reshape(blocks, rows, step)
        if near is not None:
            out = out + near[:, :, window].astype(jnp.float32)
        target[:, :, window] = out.astype(target.dtype)


def scatter_steps(copies, ids, ring, arrays, held):
    ahead, behind, sibling, across = ids
    chips = ring.chips
    half = chips // 2
    group_blocks = chips // 2
    slot = ring.turns.index
    near = {}
    crossed = {}

    def outgoing(group):
        blocks = pl.ds(group * group_blocks, group_blocks)
        for i, (source, early, out, room) in enumerate(arrays):
            for e in (1, 0):
                if source[0] == "given":
                    sent = source[1][e][1].at[blocks]
                else:
                    sent = room["outbox"].at[e]
                    if group > 0:
                        copies.settle(near[i, e, group - 1])
                    height = group_blocks * out.shape[0]
                    columns = slice((chips // group_blocks + group) * height, (chips // group_blocks + group + 1) * height)
                    products(source[1], source[2][e], held, columns, sent, None)
                near[i, e, group] = copies.push(sent, room["near"].at[e, blocks], sibling)

    def own(group):
        blocks = pl.ds(group * group_blocks, group_blocks)
        for e in (1, 0):
            for i, (source, early, out, room) in enumerate(arrays):
                near[i, e, group].wait_recv()
                target = room["sum"].at[e, blocks]
                if source[0] == "given":
                    target[...] = source[1][e][0][blocks] + room["near"][e, blocks]
                else:
                    height = group_blocks * out.shape[0]
                    columns = slice(group * height, (group + 1) * height)
                    products(source[1], source[2][e], held, columns, target, room["near"].at[e, blocks])
                if e == 1:
                    rest = pl.ds(early, out.shape[1] - early)
                    for block in range(group * group_blocks, (group + 1) * group_blocks):
                        crossed[i, block] = copies.push(room["sum"].at[1, block, :, rest], room["far"].at[block], across)

    def second(spot):
        block = slot(spot)
        for i, (source, early, out, room) in enumerate(arrays):
            rest = pl.ds(early, out.shape[1] - early)
            crossed[i, block].wait_recv()
            add_rows(room["sum"].at[0, block, :, rest], room["far"].at[block])

    def windows(size, hop, upward):
        if hop > 0:
            return pl.ds(0, size)
        return pl.ds(size // 2, size // 2) if upward else pl.ds(0, size // 2)

    def send(hop, spot, upward):
        target = ahead if upward else behind
        kinds = ("up", "up_slim") if upward else ("down", "down_slim")
        out_copies = []
        for i, (source, early, out, room) in enumerate(arrays):
            for e, size in ((0, out.shape[1]), (1, early)):
                window = windows(size, hop, upward)
                out_copies.append(
                    copies.push(room["sum"].at[e, slot(spot), :, window], room[kinds[e]].at[hop, :, window], target)
                )
        return out_copies

    def receive(hop, spot, upward, arrivals):
        kinds = ("up", "up_slim") if upward else ("down", "down_slim")
        at = 0
        for i, (source, early, out, room) in enumerate(arrays):
            for e, size in ((0, out.shape[1]), (1, early)):
                window = windows(size, hop, upward)
                arrivals[at].wait_recv()
                add_rows(room["sum"].at[e, slot(spot), :, window], room[kinds[e]].at[hop, :, window])
                at += 1

    outgoing(0)
    yield
    own(0)
    yield
    outgoing(1)
    own(1)
    yield
    second(half)
    up = send(0, half, True)
    down = send(0, half, False)
    yield
    for hop in range(1, half):
        second(chips - half + hop)
        second(half - hop)
        receive(hop - 1, chips - half + hop, True, up)
        up = send(hop, chips - half + hop, True)
        receive(hop - 1, half - hop, False, down)
        down = send(hop, half - hop, False)
        yield
    second(0)
    final = []
    at = 0
    for i, (source, early, out, room) in enumerate(arrays):
        for e in range(2):
            up[at].wait_recv()
            down[at].wait_recv()
            at += 1
        part = room["sum"][1, slot(0), :, :early].astype(jnp.float32)
        part = part + room["up_slim"][half - 1].astype(jnp.float32) + room["down_slim"][half - 1].astype(jnp.float32)
        room["slim_out"][...] = part.astype(room["slim_out"].dtype)
        final.append(copies.push(room["slim_out"], room["slim_in"], across))
    yield
    for i, (source, early, out, room) in enumerate(arrays):
        total = room["sum"][0, slot(0)].astype(jnp.float32) + room["up"][half - 1].astype(jnp.float32)
        out[...] = total + room["down"][half - 1].astype(jnp.float32)
        final[i].wait_recv()
        out[:, :early] += room["slim_in"][...].astype(jnp.float32)


def scatter_order(chips, groups):
    hops = chips // 2 - 1
    order = [0] * 4
    for group in range(1, groups):
        order += [group] * 3
    order += [0, -1] * hops
    for group in range(1, groups):
        order += [group, group - 1] + [group, -1] * hops
    return order + [groups - 1] + list(range(groups))


def scatter_count(chips, arrays):
    half = chips // 2
    return arrays * (4 + chips + half * 4 + 1)


ROOM = ("outbox", "sum", "near", "far", "up", "down", "up_slim", "down_slim", "slim_out", "slim_in")


def scatter_room(chips, rows, columns, early, dtype):
    half = chips // 2
    shapes = (
        (2, half, rows, columns),
        (2, chips, rows, columns),
        (2, chips, rows, columns),
        (chips, rows, columns - early),
        (half, rows, columns),
        (half, rows, columns),
        (half, rows, early),
        (half, rows, early),
        (rows, early),
        (rows, early),
    )
    return [pltpu.VMEM(shape, dtype) for shape in shapes]


def scatter_grads(ring, groups, collective, attention=None):
    chips = ring.chips
    arrays = [member for group in groups for member in group]
    inputs, counts, shapes, rooms = ([], [], [], [])
    tokens = 0
    for lefts, rights, early in arrays:
        if lefts is None:
            height, columns = rights[0][0].shape
            rows = height // chips
            dtype = rights[0][0].dtype
            members = [rights[e][c].reshape(chips, rows, columns) for e in range(2) for c in range(2)]
        else:
            tokens, height = lefts[0].shape
            columns = rights[0][0].shape[1]
            rows = height // chips // 2
            dtype = jnp.bfloat16
            members = list(lefts) + list(rights[0]) + list(rights[1])
        counts.append(len(members))
        inputs += members
        shapes.append(jax.ShapeDtypeStruct((rows, columns), jnp.float32))
        rooms += scatter_room(chips, rows, columns, early, dtype)
    total = len(arrays)
    extra, made = ([], [])
    if attention is not None:
        qkv, first, grad_heads, lse, slopes, prefix, scale = attention
        extra = list(qkv) + list(first) + list(grad_heads) + list(lse) + [slopes, prefix]
        made = [jax.ShapeDtypeStruct(grad_heads[0].shape, jnp.bfloat16)] * 10

    def kernel(*refs):
        ins, refs = (refs[: len(inputs)], refs[len(inputs) :])
        more, refs = (refs[: len(extra)], refs[len(extra) :])
        outs, refs = (refs[:total], refs[total:])
        back, scratch = (refs[: len(made)], refs[len(made) :])
        ids = ring.neighbours()
        greet(ids)
        held, sums, send, recv, near = scratch[len(rooms) :]
        copies = Copies(send, recv, near)
        members = []
        at = 0
        for i, (lefts, rights, early) in enumerate(arrays):
            mine = ins[at : at + counts[i]]
            at += counts[i]
            if lefts is None:
                source = ("given", (mine[:2], mine[2:]))
            else:
                terms = len(lefts)
                source = ("product", mine[:terms], (mine[terms : 2 * terms], mine[2 * terms :]))
            members.append((source, early, outs[i], dict(zip(ROOM, scratch[i * len(ROOM) : (i + 1) * len(ROOM)]))))
        work = []
        if attention is not None:
            parts = [(more[e], more[2 + e], more[4 + e], more[6 + e], back[5 * e : 5 * e + 5]) for e in range(2)]
            work = backward_work(parts, more[8], more[9][0], scale, sums)
        running = []
        for group in groups:
            running.append(scatter_steps(copies, ids, ring, members[: len(group)], held))
            members = members[len(group) :]
        for turn in scatter_order(chips, len(groups)):
            if turn >= 0:
                next(running[turn], None)
            elif work:
                work.pop(0)()
        for piece in work:
            piece()
        copies.finish()

    pieces = chips // 2 * (inputs[0].shape[1] // chips // 2)
    outs = pl.pallas_call(
        kernel,
        in_specs=on_vmem(len(inputs)) + (on_vmem(8) + on_smem(2) if extra else []),
        out_specs=on_vmem(total + len(made)),
        out_shape=shapes + made,
        scratch_shapes=rooms
        + [
            pltpu.VMEM((2, pieces, tokens), jnp.bfloat16),
            pltpu.VMEM((4, tokens, 128), jnp.float32),
            pltpu.SemaphoreType.DMA((scatter_count(chips, total),)),
            pltpu.SemaphoreType.DMA((scatter_count(chips, total),)),
            pltpu.SemaphoreType.DMA((1,)),
        ],
        compiler_params=pltpu.CompilerParams(
            collective_id=collective, has_side_effects=True, vmem_limit_bytes=62 * 1024 * 1024
        ),
        name="scatter_grads",
    )(*inputs, *extra)
    return (outs[:total], outs[total:])


def small_parts(vector_grads, bias_grads, by_half, placed, piece, lane):
    layers, dp = (len(vector_grads), placed.shape[0])
    vectors = jnp.stack([vector_grads[layer][i] for i in range(6) for layer in range(layers)])
    vectors = by_half(vectors.reshape(6 * layers, dp, 2, piece).transpose(2, 1, 0, 3), 0).reshape(2, dp, -1)
    shifts = [jnp.stack([bias_grads[layer][i] for layer in range(layers)], axis=1) for i in range(2)]
    shifts = jnp.concatenate([member.reshape(2, -1, dp, lane) for member in shifts], axis=1)
    shifts = jnp.einsum("tndl,bd->tbnl", shifts, placed, precision=lax.Precision.HIGHEST).reshape(2, dp, -1)
    packed = jnp.concatenate([vectors, shifts], axis=2)
    packed = jnp.pad(packed, ((0, 0), (0, 0), (0, 8 * 512 - packed.shape[2]))).reshape(2, 2, -1, 512)
    return [[packed[e, c] for c in range(2)] for e in range(2)]


def local(
    states_in,
    teacher,
    valid_mask,
    prefix_len,
    ln1_gain,
    ln1_shift,
    qkv_weight,
    qkv_bias,
    out_weight,
    out_bias,
    ln2_gain,
    ln2_shift,
    up_weight,
    up_bias,
    down_weight,
    down_bias,
):
    f32, low = (jnp.float32, jnp.bfloat16)
    layers, local_rows = (qkv_weight.shape[0], states_in.shape[1])
    width = states_in.shape[2]
    dp, tensor = (lax.axis_size("dp"), lax.axis_size("tensor"))
    here, side = (lax.axis_index("dp"), lax.axis_index("tensor"))
    ring = Ring(dp)
    piece = width // (dp * tensor)

    def by_half(pair, axis):
        return jnp.where(side == 0, pair, jnp.flip(pair, axis))

    owners = lax.dynamic_index_in_dim(jnp.asarray(ring.owners()), here, 0, keepdims=False)
    rows = width // dp
    columns = (owners[:, None] * rows + jnp.arange(rows, dtype=jnp.int32)[None]).reshape(1, width)
    to_ring = (jnp.arange(width, dtype=jnp.int32)[:, None] == columns).astype(low)

    placed = (owners[:, None] == jnp.arange(dp, dtype=jnp.int32)[None]).astype(f32)

    def into_ring(values):
        return jnp.dot(values, to_ring, preferred_element_type=f32)

    def from_ring(values, precision=None):
        return lax.dot_general(
            values, to_ring.astype(values.dtype), NT, precision=precision, preferred_element_type=f32
        )

    count = jnp.sum(valid_mask)
    vectors = jnp.stack([ln1_gain, ln1_shift, out_bias, ln2_gain, ln2_shift, down_bias])
    packed = jnp.concatenate(
        [vectors.reshape(-1), qkv_bias.reshape(-1), up_bias.reshape(-1), jnp.stack([count // 256, count % 256]).astype(low)]
    )
    first, second, third = (vectors.size, vectors.size + qkv_bias.size, vectors.size + qkv_bias.size + up_bias.size)
    packed = jnp.pad(packed, (0, 16 * 512 - packed.size)).reshape(16, 512)
    groups = []
    for layer in range(layers):
        groups.append([(qkv_weight[layer].reshape(rows, -1), 512), (out_weight[layer].T, 256)])
        groups.append([(up_weight[layer], 768), (down_weight[layer].T, 768)])
    weights = gather_weights(ring, [[(packed, 256)] + groups[0]], 1)[0]
    everything = by_half(jnp.stack([member.reshape(dp, -1) for member in weights[:2]]), 0)
    gathered = weights[2:]
    vectors = everything[:, :, :first].reshape(tensor, dp, 6, layers, piece).transpose(2, 3, 1, 0, 4)
    small = vectors.reshape(6, layers, 1, width).astype(f32)
    lane = qkv_bias.shape[3]
    biases = everything[:, :, first:third].reshape(tensor, dp, -1, lane)
    biases = jnp.einsum("tbnl,bd->tndl", biases, placed.astype(low), preferred_element_type=f32)
    biases = by_half(biases.reshape(tensor, -1, dp * lane), 0)
    split = (second - first) // lane
    qkv_add = biases[:, :split].reshape(tensor, layers, 1, -1).transpose(1, 0, 2, 3)
    up_add = biases[:, split:].reshape(tensor, layers, 1, -1).transpose(1, 0, 2, 3)
    counts = jnp.sum(everything[:, :, third : third + 2].astype(f32), axis=(0, 1))
    valid_count = counts[0] * 256.0 + counts[1]

    scale = HD ** (-0.5)
    pieces = jnp.arange(H, dtype=jnp.int32)
    heads_half = H // tensor
    heads = (pieces // heads_half ^ side) * heads_half + pieces % heads_half
    slopes = jnp.exp2(-(heads.astype(f32) + 1.0) * 8.0 / H) * LOG2E

    before_first = lax.ppermute(states_in[0], "tensor", [(0, 1)])
    states = into_ring(states_in[0])
    target = into_ring(teacher[0])
    kept = []
    for layer in range(layers):
        qkv_proj, out_proj = (gathered[8 * layer : 8 * layer + 2], gathered[8 * layer + 2 : 8 * layer + 4])
        normed = norm_rows(states, small[0][layer], small[1][layer]).astype(low)
        if layer == 0:
            normed_first = norm_rows(into_ring(before_first), small[0][layer], small[1][layer]).astype(low)
        else:
            normed_first = lax.ppermute(normed, "tensor", [(0, 1)])
        qkv, kv_first = ([], [])
        for i in range(tensor):
            query = qkv_proj[i].shape[1] // 3
            mixed = jnp.dot(normed, qkv_proj[i], preferred_element_type=f32) + qkv_add[layer][i]
            qkv.append(mixed.astype(low))
            mixed = jnp.dot(normed_first, qkv_proj[i][:, query:], preferred_element_type=f32)
            kv_first.append((mixed + qkv_add[layer][i][:, query:]).astype(low))
        coming = groups[2 * layer + 1 : 2 * layer + 3]
        weights, heads_out, lse = gather_weights(ring, coming, 2 + layer, (qkv, kv_first, slopes, prefix_len, scale))
        gathered += weights
        up_proj, down_proj = (gathered[8 * layer + 4 : 8 * layer + 6], gathered[8 * layer + 6 : 8 * layer + 8])
        middle = states + mm(heads_out[0], out_proj[0], NT) + mm(heads_out[1], out_proj[1], NT) + small[2][layer]
        normed_two = norm_rows(middle, small[3][layer], small[4][layer]).astype(low)
        hidden = [jnp.dot(normed_two, up_proj[i], preferred_element_type=f32) + up_add[layer][i] for i in range(tensor)]
        active = [gelu_tanh(values).astype(low) for values in hidden]
        kept.append((states, normed, normed_first, qkv, kv_first, lse, heads_out, middle, normed_two, hidden, active))
        states = middle + mm(active[0], down_proj[0], NT) + mm(active[1], down_proj[1], NT) + small[5][layer]

    final_states = from_ring(states.astype(low)).astype(low)[None]
    factor = local_rows * tensor * dp / valid_count
    grad = factor * valid_mask[0][:, None].astype(f32) * (states - target)
    weight_grads = [None] * layers
    vector_grads = [None] * layers
    bias_grads = [None] * layers
    for layer in reversed(range(layers)):
        before, normed, normed_first, qkv, kv_first, lse, heads_out, middle, normed_two, hidden, active = kept[layer]
        qkv_proj, out_proj, up_proj, down_proj = [gathered[8 * layer + i : 8 * layer + i + 2] for i in (0, 2, 4, 6)]
        grad_mlp = grad.astype(low)
        down_shift = jnp.sum(grad_mlp.astype(f32), axis=0)
        grad_hidden = []
        for i in range(tensor):
            grad_active = jnp.dot(grad_mlp, down_proj[i], preferred_element_type=f32)
            grad_hidden.append(jax.vjp(gelu_tanh, hidden[i])[1](grad_active)[0].astype(low))
        up_shift = jnp.stack([jnp.sum(values.astype(f32), axis=0) for values in grad_hidden])
        grad_normed = mm(grad_hidden[0], up_proj[0], NT) + mm(grad_hidden[1], up_proj[1], NT)
        part, gain_two, shift_two = norm_back(middle, small[3][layer], grad_normed)
        grad_middle = grad + part
        grad_attn = grad_middle.astype(low)
        out_shift = jnp.sum(grad_attn.astype(f32), axis=0)
        grad_heads = [jnp.dot(grad_attn, out_proj[i], preferred_element_type=f32).astype(low) for i in range(tensor)]
        (down_grad, up_grad), grads = scatter_grads(
            ring,
            [
                [([grad_mlp], [[values] for values in active], 768)],
                [([normed_two], [[values] for values in grad_hidden], 768)],
            ],
            10 + 2 * layer,
            (qkv, kv_first, grad_heads, lse, slopes, prefix_len, scale),
        )
        grad_normed = 0.0
        qkv_shift = []
        sent = 0.0
        query_terms, rest_terms = ([], [])
        for i in range(tensor):
            query = grads[5 * i].shape[1]
            grad_qkv = jnp.concatenate(grads[5 * i : 5 * i + 3], axis=1)
            grad_first = jnp.concatenate(grads[5 * i + 3 : 5 * i + 5], axis=1)
            sent = sent + mm(grad_first, qkv_proj[i][:, query:], NT)
            query_terms.append([grads[5 * i]])
            rest_terms.append([grad_qkv[:, query:], grad_first])
            shift = jnp.sum(grad_qkv.astype(f32), axis=0)
            qkv_shift.append(shift + jnp.pad(jnp.sum(grad_first.astype(f32), axis=0), (query, 0)))
            grad_normed = grad_normed + mm(grad_qkv, qkv_proj[i], NT)
        arrived = lax.ppermute(sent.astype(low), "tensor", [(1, 0)])
        qkv_shift = jnp.stack(qkv_shift)
        projections = [
            [
                ([grad_attn], [[values] for values in heads_out], 256),
                ([normed], query_terms, 256),
                ([normed, normed_first], rest_terms, 256),
            ]
        ]
        grad_normed = grad_normed + arrived.astype(f32)
        part, gain_one, shift_one = norm_back(before, small[0][layer], grad_normed)
        grad = grad_middle + part
        vector_grads[layer] = (gain_one, shift_one, out_shift, gain_two, shift_two, down_shift)
        bias_grads[layer] = (qkv_shift, up_shift)
        if layer == 0:
            projections[0].append((None, small_parts(vector_grads, bias_grads, by_half, placed, piece, lane), 256))
        (out_grad, query_grad, rest_grad, *last), unused = scatter_grads(ring, projections, 11 + 2 * layer)
        qkv_grad = jnp.concatenate([query_grad, rest_grad], axis=1).reshape(rows, 3, -1)
        weight_grads[layer] = (qkv_grad, out_grad.T, up_grad, down_grad)

    input_grad = from_ring(grad, lax.Precision.HIGHEST)[None]
    qkv_grad, out_grad, up_grad, down_grad = [
        jnp.stack([weight_grads[layer][i] for layer in range(layers)]) for i in range(4)
    ]
    summed = last[0].reshape(-1)
    vectors = summed[:first].reshape(6, layers, piece)
    return (
        final_states,
        input_grad,
        vectors[0],
        vectors[1],
        qkv_grad,
        summed[first:second].reshape(qkv_bias.shape),
        out_grad,
        vectors[2],
        vectors[3],
        vectors[4],
        up_grad,
        summed[second:third].reshape(up_bias.shape),
        down_grad.transpose(0, 2, 1),
        vectors[5],
    )


def solution(mesh):
    return jax.shard_map(
        local,
        mesh=mesh,
        in_specs=(
            P("dp", "tensor", None),
            P("dp", "tensor", None),
            P("dp", "tensor"),
            P("dp"),
            P(None, ("dp", "tensor")),
            P(None, ("dp", "tensor")),
            P(None, "dp", None, "tensor"),
            P(None, None, "tensor", "dp"),
            P(None, "tensor", "dp"),
            P(None, ("dp", "tensor")),
            P(None, ("dp", "tensor")),
            P(None, ("dp", "tensor")),
            P(None, "dp", "tensor"),
            P(None, "tensor", "dp"),
            P(None, "tensor", "dp"),
            P(None, ("dp", "tensor")),
        ),
        out_specs=(
            P("dp", "tensor", None),
            P("dp", "tensor", None),
            P(None, ("dp", "tensor")),
            P(None, ("dp", "tensor")),
            P(None, "dp", None, "tensor"),
            P(None, None, "tensor", "dp"),
            P(None, "tensor", "dp"),
            P(None, ("dp", "tensor")),
            P(None, ("dp", "tensor")),
            P(None, ("dp", "tensor")),
            P(None, "dp", "tensor"),
            P(None, "tensor", "dp"),
            P(None, "tensor", "dp"),
            P(None, ("dp", "tensor")),
        ),
        check_vma=False,
    )
```

```python
import functools

import jax
import jax.numpy as jnp
import numpy as np
from jax import lax
from jax.experimental import pallas as pl
from jax.experimental.pallas import tpu as pltpu
from jax.sharding import PartitionSpec as P

LOG2E = 1.4426950408889634
BIG = 1000000000.0
NT = (((1,), (1,)), ((), ()))
NN = (((1,), (0,)), ((), ()))


def mm(a, b, dims):
    return lax.dot_general(a, b, dims, preferred_element_type=jnp.float32)


def lane_masks(width):
    lanes = lax.broadcasted_iota(jnp.int32, (1, width), 1)
    low = jnp.where(lanes < width // 2, 1.0, 0.0)
    return (low.astype(jnp.bfloat16), (1.0 - low).astype(jnp.bfloat16))


def rows_iota(n, m):
    return lax.broadcasted_iota(jnp.int32, (n, m), 0)


def cols_iota(n, m):
    return lax.broadcasted_iota(jnp.int32, (n, m), 1)


def scores_first(keys, query, slope, scale, prefix, start):
    n, m = (keys.shape[0], query.shape[0])
    key_pos = rows_iota(n, m)
    query_pos = cols_iota(n, m) + start
    distance = jnp.abs(query_pos - key_pos).astype(jnp.float32)
    raw = mm(keys, query, NT) * scale - slope * distance
    visible = (key_pos <= query_pos) | (key_pos < prefix)
    return jnp.where(visible, raw, -BIG)


def scores_second(keys, query, slope, scale, offset, mask_start):
    n, m = (keys.shape[0], query.shape[0])
    bias = slope * (rows_iota(n, 1) + offset).astype(jnp.float32)
    raw = mm(keys, query, NT) * scale + bias
    if mask_start is None:
        return raw
    return jnp.where(rows_iota(n, m) + mask_start <= cols_iota(n, m), raw, -BIG)


def score_parts(half, k_ref, k0_ref, query, slope, scale, prefix, start, step):
    rows = k_ref.shape[0]
    if half == 0:
        return [(None, 0, rows, scores_first(k_ref[...], query, slope, scale, prefix, start))]
    parts = [(0, 0, rows, scores_second(k0_ref[...], query, slope, scale, -2 * rows, None))]
    if start > 0:
        parts.append((1, 0, start, scores_second(k_ref[:start], query, slope, scale, -rows, None)))
    parts.append(
        (1, start, start + step, scores_second(k_ref[start : start + step], query, slope, scale, start - rows, 0))
    )
    return parts


def forward_body(half, pair, slopes, prefix, scale, q_ref, k_ref, v_ref, k0_ref, v0_ref, o_ref, lse_ref, step):
    rows, width = q_ref.shape
    masks = lane_masks(width)
    head = width // 2
    values = v_ref[...].T
    values0 = v0_ref[...].T if half else None
    for start in range(0, rows, step):
        outs = []
        for side in range(2):
            query = q_ref[start : start + step] * masks[side]
            slope = slopes[pair * 2 + side]
            parts = score_parts(half, k_ref, k0_ref, query, slope, scale, prefix, start, step)
            top = parts[0][3].max(axis=0, keepdims=True)
            for part in parts[1:]:
                top = jnp.maximum(top, part[3].max(axis=0, keepdims=True))
            total = None
            out = None
            for which, low, high, raw in parts:
                raised = jnp.exp2(raw - top)
                part_sum = raised.sum(axis=0, keepdims=True)
                held = values0 if which == 0 else values
                held = held[side * head : (side + 1) * head, low:high]
                part_out = mm(held, raised.astype(jnp.bfloat16), NN)
                total = part_sum if total is None else total + part_sum
                out = part_out if out is None else out + part_out
            outs.append(out / total)
            lse_ref[0, side : side + 1, start : start + step] = top + jnp.log2(total)
        o_ref[start : start + step] = jnp.concatenate(outs, axis=0).T.astype(jnp.bfloat16)


def backward_body(half, pair, slopes, prefix, scale, refs, step):
    q_ref, k_ref, v_ref, k0_ref, v0_ref, g_ref, lse_ref, gq_ref, gk_ref, gv_ref, gk0_ref, gv0_ref, sums = refs
    rows, width = q_ref.shape
    masks = lane_masks(width)
    head = width // 2
    keys = k_ref[...].T
    keys0 = k0_ref[...].T if half else None
    sums[...] = jnp.zeros_like(sums)
    for start in range(0, rows, step):
        outs = []
        for side in range(2):
            query = q_ref[start : start + step] * masks[side]
            grad = g_ref[start : start + step] * masks[side]
            slope = slopes[pair * 2 + side]
            parts = score_parts(half, k_ref, k0_ref, query, slope, scale * LOG2E, prefix, start, step)
            lse = lse_ref[0, side : side + 1, start : start + step]
            inner = None
            held = []
            for which, low, high, raw in parts:
                share = jnp.exp2(raw - lse)
                value = v0_ref[low:high] if which == 0 else v_ref[low:high]
                slot = 2 if which == 0 else 0
                grad_share = mm(value, grad, NT)
                part = (share * grad_share).sum(axis=0, keepdims=True)
                inner = part if inner is None else inner + part
                sums[slot + 1, low:high] += mm(share.astype(jnp.bfloat16), grad, NN)
                held.append((which, low, high, share, grad_share, slot))
            out = None
            for which, low, high, share, grad_share, slot in held:
                grad_score = (share * (grad_share - inner)).astype(jnp.bfloat16)
                sums[slot, low:high] += mm(grad_score, query, NN)
                key = keys0 if which == 0 else keys
                part = mm(key[side * head : (side + 1) * head, low:high], grad_score, NN)
                out = part if out is None else out + part
            outs.append(out)
        gq_ref[start : start + step] = (jnp.concatenate(outs, axis=0).T * scale).astype(jnp.bfloat16)
    gk_ref[...] = (sums[0] * scale).astype(jnp.bfloat16)
    gv_ref[...] = sums[1].astype(jnp.bfloat16)
    gk0_ref[...] = (sums[2] * scale).astype(jnp.bfloat16)
    gv0_ref[...] = sums[3].astype(jnp.bfloat16)


def head_pairs(low, high, body):
    @pl.loop(low, high)
    def step(pair):
        columns = pl.multiple_of(pair * 128, 128)
        for half in range(2):
            @pl.when(lax.axis_index("tensor") == half)
            def one():
                body(half, pair, columns)


def forward_work(parts, slopes, prefix, scale):
    work = []
    for e, (qkv, first, out, lse) in enumerate(parts):
        pairs = out.shape[1] // 128
        rows = out.shape[0]

        def body(half, pair, columns, e=e, qkv=qkv, first=first, out=out, lse=lse, pairs=pairs, rows=rows):
            at = lambda ref, base: ref.at[:, pl.ds(columns + base * pairs * 128, 128)]
            forward_body(
                half,
                pair + e * pairs,
                slopes,
                prefix,
                scale * LOG2E,
                at(qkv, 0),
                at(qkv, 1),
                at(qkv, 2),
                at(first, 0),
                at(first, 1),
                at(out, 0),
                lse.at[pl.ds(pair, 1)],
                rows // 2,
            )

        for low in range(0, pairs, 2):
            work.append(functools.partial(head_pairs, low, low + 2, body))
    return work


def backward_work(parts, slopes, prefix, scale, sums):
    work = []
    for e, (qkv, first, grad, lse, outs) in enumerate(parts):
        pairs = grad.shape[1] // 128
        rows = grad.shape[0]

        def body(half, pair, columns, e=e, qkv=qkv, first=first, grad=grad, lse=lse, outs=outs, pairs=pairs, rows=rows):
            at = lambda ref, base: ref.at[:, pl.ds(columns + base * pairs * 128, 128)]
            refs = [at(qkv, 0), at(qkv, 1), at(qkv, 2), at(first, 0), at(first, 1), at(grad, 0), lse.at[pl.ds(pair, 1)]]
            refs += [at(out, 0) for out in outs] + [sums]
            backward_body(half, pair + e * pairs, slopes, prefix, scale, refs, rows // 2)

        for low in range(0, pairs, 2):
            work.append(functools.partial(head_pairs, low, low + 2, body))
    return work


EPS = 1e-05
H = 16
HD = 64
ROWS_CONTRACT = (((0,), (0,)), ((), ()))


def norm_parts(states):
    centered = states - jnp.mean(states, axis=-1, keepdims=True)
    inverse = lax.rsqrt(jnp.mean(centered * centered, axis=-1, keepdims=True) + EPS)
    return (centered * inverse, inverse)


def norm_rows(states, gain, shift):
    return norm_parts(states)[0] * gain + shift


def norm_back(states, gain, grad):
    unit, inverse = norm_parts(states)
    scaled = grad * gain
    first = jnp.mean(scaled, axis=-1, keepdims=True)
    second = jnp.mean(scaled * unit, axis=-1, keepdims=True)
    return (inverse * (scaled - first - unit * second), jnp.sum(grad * unit, axis=0), jnp.sum(grad, axis=0))


def gelu_tanh(values):
    return 0.5 * values * (1.0 + jnp.tanh(0.7978845608028654 * (values + 0.044715 * values * values * values)))


MESH = pl.DeviceIdType.MESH


class Ring:
    def __init__(self, devices):
        self.chips = devices // 2
        self.order = list(range(0, self.chips, 2)) + list(range(self.chips - 1, 0, -2))
        self.place = {chip: spot for spot, chip in enumerate(self.order)}
        half = self.chips // 2
        self.turns = [half] + [step for hop in range(half - 1, 0, -1) for step in (self.chips - hop, hop)] + [0]

    def owners(self):
        table = []
        for device in range(2 * self.chips):
            spot = self.place[device // 2]
            table.append(
                [
                    2 * self.order[(spot - step) % self.chips] + ((device % 2) ^ core)
                    for core in range(2)
                    for step in self.turns
                ]
            )
        return np.array(table, np.int32)

    def spot_chip(self, spot):
        half = self.chips // 2
        return jnp.where(spot < half, 2 * spot, 2 * (self.chips - 1 - spot) + 1)

    def neighbours(self):
        here, side = (lax.axis_index("dp"), lax.axis_index("tensor"))
        chip, core = (here // 2, here % 2)
        spot = jnp.where(chip % 2 == 0, chip // 2, self.chips - 1 - chip // 2)
        ahead = self.spot_chip((spot + 1) % self.chips) * 2 + core
        behind = self.spot_chip((spot + self.chips - 1) % self.chips) * 2 + core
        sibling = chip * 2 + (1 - core)
        return ((ahead, side), (behind, side), (sibling, side), (here, 1 - side))


def greet(targets):
    barrier = pltpu.get_barrier_semaphore()
    for target in targets:
        pl.semaphore_signal(barrier, inc=1, device_id=target, device_id_type=MESH)
    pl.semaphore_wait(barrier, len(targets))


class Copies:
    def __init__(self, send, recv, near):
        self.send, self.recv, self.near = (send, recv, near)
        self.sent, self.moved, self.spots = ([], [], 0)

    def push(self, source, target, device):
        spot = self.spots
        copy = pltpu.make_async_remote_copy(
            src_ref=source,
            dst_ref=target,
            send_sem=self.send.at[spot],
            recv_sem=self.recv.at[spot],
            device_id=device,
            device_id_type=MESH,
        )
        copy.start()
        self.sent.append(copy)
        self.spots += 1
        return copy

    def move(self, source, target):
        copy = pltpu.make_async_copy(source, target, self.near.at[len(self.moved)])
        copy.start()
        self.moved.append(copy)
        return copy

    def settle(self, copy):
        copy.wait_send()
        self.sent = [other for other in self.sent if other is not copy]

    def finish(self):
        for copy in self.sent:
            copy.wait_send()


def run_all(steps):
    for unused in steps:
        pass


def gather_steps(copies, ids, ring, arrays):
    ahead, behind, sibling, across = ids
    chips = ring.chips
    half = chips // 2
    slot = ring.turns.index
    local, siblings, early_in, late_in, up, down = ([], [], [], [], {}, {})
    for shard, own, other, early in arrays:
        early_in.append(copies.push(shard.at[:, pl.ds(0, early)], other.at[0, slot(0), :, pl.ds(0, early)], across))
    for i, (shard, own, other, early) in enumerate(arrays):
        local.append(copies.move(shard, own.at[0, slot(0)]))
        up[i, 1] = [copies.push(shard, own.at[0, slot(1)], ahead)]
        down[i, 1] = [copies.push(shard, own.at[0, slot(chips - 1)], behind)]
        siblings.append(copies.push(shard, own.at[1, slot(0)], sibling))
    for shard, own, other, early in arrays:
        width = shard.shape[1] - early
        late_in.append(copies.push(shard.at[:, pl.ds(early, width)], other.at[0, slot(0), :, pl.ds(early, width)], across))
    yield
    for i, (shard, own, other, early) in enumerate(arrays):
        early_in[i].wait_recv()
        part = other.at[0, slot(0), :, pl.ds(0, early)]
        up[i, 1].append(copies.push(part, other.at[0, slot(1), :, pl.ds(0, early)], ahead))
        down[i, 1].append(copies.push(part, other.at[0, slot(chips - 1), :, pl.ds(0, early)], behind))
    late = [(0, late_in)]
    for hop in range(1, half + 1):
        yield
        spots = [(hop, up, ahead), (chips - hop, down, behind)]
        crossing = {}
        if hop < half:
            for spot, arrivals, target in spots:
                crossing[spot] = []
                step = 1 if target is ahead else -1
                for i, (shard, own, other, early) in enumerate(arrays):
                    size = shard.shape[1]
                    arrivals[i, hop][0].wait_recv()
                    if hop + 1 < half:
                        window, slim = (pl.ds(0, size), pl.ds(0, early))
                    elif step == 1:
                        window, slim = (pl.ds(0, size // 2), pl.ds(0, early // 2))
                    else:
                        window, slim = (pl.ds(size // 2, size // 2), pl.ds(early // 2, early // 2))
                    arrivals[i, hop + 1] = [
                        copies.push(own.at[0, slot(spot), :, window], own.at[0, slot(spot + step), :, window], target)
                    ]
                    rest = pl.ds(early, size - early)
                    crossing[spot].append(copies.push(own.at[0, slot(spot), :, rest], other.at[0, slot(spot), :, rest], across))
                    siblings.append(copies.push(own.at[0, slot(spot)], own.at[1, slot(spot)], sibling))
                    arrivals[i, hop][1].wait_recv()
                    arrivals[i, hop + 1].append(
                        copies.push(other.at[0, slot(spot), :, slim], other.at[0, slot(spot + step), :, slim], target)
                    )
        else:
            crossing[half] = []
            for i, (shard, own, other, early) in enumerate(arrays):
                up[i, half][0].wait_recv()
                down[i, half][0].wait_recv()
                rest = pl.ds(early, shard.shape[1] - early)
                crossing[half].append(copies.push(own.at[0, slot(half), :, rest], other.at[0, slot(half), :, rest], across))
                siblings.append(copies.push(own.at[0, slot(half)], own.at[1, slot(half)], sibling))
                up[i, half][1].wait_recv()
                down[i, half][1].wait_recv()
        for spot, arrivals in late:
            for i, (shard, own, other, early) in enumerate(arrays):
                arrivals[i].wait_recv()
                siblings.append(copies.push(other.at[0, slot(spot)], other.at[1, slot(spot)], sibling))
        late = list(crossing.items())
    yield
    for spot, arrivals in late:
        for i, (shard, own, other, early) in enumerate(arrays):
            arrivals[i].wait_recv()
            siblings.append(copies.push(other.at[0, slot(spot)], other.at[1, slot(spot)], sibling))
    for copy in local:
        copy.wait()
    yield
    for copy in siblings:
        copy.wait_recv()


def gather_count(chips, arrays):
    half = chips // 2
    return arrays * (5 + 2 + (half - 1) * 2 * 4 + 2 + chips)


def on_vmem(count):
    return [pl.BlockSpec(memory_space=pltpu.VMEM)] * count


def on_smem(count):
    return [pl.BlockSpec(memory_space=pltpu.SMEM)] * count


def anywhere(count):
    return [pl.BlockSpec(memory_space=pl.ANY)] * count


def gather_weights(ring, groups, collective, attention=None):
    flat = [member for group in groups for member in group]
    total = len(flat)
    count = sum(gather_count(ring.chips, len(group)) for group in groups)
    shapes = [
        jax.ShapeDtypeStruct((2, ring.chips) + shard.shape, shard.dtype) for shard, early in flat for unused in range(2)
    ]
    inputs, more = ([], [])
    if attention is not None:
        qkv, first, slopes, prefix, scale = attention
        inputs = list(qkv) + list(first) + [slopes, prefix]
        rows, width = (qkv[0].shape[0], qkv[0].shape[1] // 3)
        more = [jax.ShapeDtypeStruct((rows, width), jnp.bfloat16)] * 2
        more += [jax.ShapeDtypeStruct((width // 128, 2, rows), jnp.float32)] * 2

    def kernel(*refs):
        shards, extra, refs = (refs[:total], refs[total : total + len(inputs)], refs[total + len(inputs) :])
        outs, made, scratch = (refs[: 2 * total], refs[2 * total : 2 * total + len(more)], refs[2 * total + len(more) :])
        ids = ring.neighbours()
        greet(ids)
        copies = Copies(*scratch)
        members = [(shards[i], outs[2 * i], outs[2 * i + 1], flat[i][1]) for i in range(total)]
        at = 0
        running = []
        for group in groups:
            running.append(gather_steps(copies, ids, ring, members[at : at + len(group)]))
            at += len(group)
        work = []
        if attention is not None:
            parts = [(extra[e], extra[2 + e], made[e], made[2 + e]) for e in range(2)]
            work = [(piece, None) for piece in forward_work(parts, extra[4], extra[5][0], scale)]
        run_staggered(running, (3,), work)
        copies.finish()

    outs = pl.pallas_call(
        kernel,
        in_specs=anywhere(total) + (on_vmem(4) + on_smem(2) if inputs else []),
        out_specs=anywhere(len(shapes)) + on_vmem(len(more)),
        out_shape=shapes + more,
        scratch_shapes=[
            pltpu.SemaphoreType.DMA((count,)),
            pltpu.SemaphoreType.DMA((count,)),
            pltpu.SemaphoreType.DMA((total,)),
        ],
        compiler_params=pltpu.CompilerParams(
            collective_id=collective, has_side_effects=True, vmem_limit_bytes=40 * 1024 * 1024
        ),
        name="gather_weights",
    )(*[shard for shard, early in flat], *inputs)
    weights = [out.reshape(-1, out.shape[-1]) for out in outs[: 2 * total]]
    return (weights, outs[2 * total : 2 * total + 2], outs[2 * total + 2 :])


def run_staggered(running, leads, work=(), most=1):
    waiting, work = (list(enumerate(running)), list(work))
    active, ended = ([], {None})
    leads = list(leads)
    needed, youngest = (0, 0)
    while waiting or active:
        if waiting and (youngest >= needed or not active):
            active.append(waiting.pop(0))
            needed, youngest = (leads.pop(0) if leads else 0, 0)
        youngest += 1
        for member in list(active):
            try:
                next(member[1])
            except StopIteration:
                active.remove(member)
                ended.add(member[0])
        for unused in range(most):
            if work and work[0][1] in ended:
                work.pop(0)[0]()
    for piece, need in work:
        piece()


def unit_rows(values):
    centered = values - jnp.mean(values, axis=-1, keepdims=True)
    return centered * lax.rsqrt(jnp.mean(centered * centered, axis=-1, keepdims=True) + EPS)


def row_chunks(rows, body):
    step = 256

    @pl.loop(0, rows // step)
    def chunk(i):
        body(pl.ds(pl.multiple_of(i * step, step), step))


FORWARD_SPANS = ((0, 1536, (512, 512)), (1536, 512, (256, 256)))
FORWARD_LEADS = (3, 3)


def forward_layer(ring, mlp, coming, collective, attention, states, out_proj, vectors, up_add):
    qkv, first, slopes, prefix, scale = attention
    shards = list(mlp) + [shard for shard, early in coming]
    total = len(shards)
    chips = ring.chips
    tokens, width = states.shape
    inner = mlp[0].shape[1]
    rows = mlp[0].shape[0]
    heads = qkv[0].shape[1] // 3
    tile = 512
    spans = FORWARD_SPANS
    count = len(spans) * gather_count(chips, 2) + gather_count(chips, max(len(coming), 1)) + 1
    shapes = [jax.ShapeDtypeStruct((2, chips) + shard.shape, shard.dtype) for shard in shards for unused in range(2)]
    f32, low = (jnp.float32, jnp.bfloat16)
    more = [jax.ShapeDtypeStruct((tokens, heads), low)] * 2
    more += [jax.ShapeDtypeStruct((heads // 128, 2, tokens), f32)] * 2
    more += [jax.ShapeDtypeStruct((tokens, width), f32), jax.ShapeDtypeStruct((tokens, width), low)]
    more += [jax.ShapeDtypeStruct((tokens, inner), f32)] * 2 + [jax.ShapeDtypeStruct((tokens, inner), low)] * 2
    more += [jax.ShapeDtypeStruct((tokens, width), f32)]
    if coming:
        more += [jax.ShapeDtypeStruct((tokens, width), low)] * 2
    inputs = list(qkv) + list(first) + [states] + list(out_proj) + [vectors, up_add, slopes, prefix]

    def kernel(*refs):
        sources, refs = (refs[:total], refs[total:])
        qkv, first, (states, out_0, out_1, vectors, up_add, slopes, prefix) = (refs[:2], refs[2:4], refs[4:11])
        outs, refs = (refs[11 : 11 + 2 * total], refs[11 + 2 * total :])
        heads_out, lse, middle, normed, hidden, active, after = (refs[:2], refs[2:4], refs[4], refs[5], refs[6:8], refs[8:10], refs[10])
        following, scratch = (refs[11 : len(more)], refs[len(more) :])
        up_tile, down_tile, send, recv, near = scratch
        ids = ring.neighbours()
        greet(ids)
        copies = Copies(send, recv, near)
        running = []
        for column, size, earlies in spans:
            window = pl.ds(column, size)
            members = []
            for i, early in enumerate(earlies):
                views = [outs[2 * i + j].at[:, :, :, window] for j in range(2)]
                members.append((sources[i].at[:, window], views[0], views[1], early))
            running.append(gather_steps(copies, ids, ring, members))
        if coming:
            members = [(sources[2 + i], outs[4 + 2 * i], outs[5 + 2 * i], coming[i][1]) for i in range(len(coming))]
            running.append(gather_steps(copies, ids, ring, members))
        parts = [(qkv[e], first[e], heads_out[e], lse[e]) for e in range(2)]
        work = [(piece, None) for piece in forward_work(parts, slopes, prefix[0], scale)]

        def project():
            def body(span):
                value = states[span] + mm(heads_out[0][span], out_0[...], NT) + mm(heads_out[1][span], out_1[...], NT)
                value = value + vectors[0:1]
                middle[span] = value
                normed[span] = (unit_rows(value) * vectors[1:2] + vectors[2:3]).astype(low)
                after[span] = value + vectors[3:4]

            row_chunks(tokens, body)

        work.append((project, None))
        tiles = [
            (group, e, column + i * tile)
            for group, (column, size, earlies) in enumerate(spans)
            for e in range(2)
            for i in range(size // tile)
        ]
        loads = {}

        def load(spot):
            half, e, column = tiles[spot]
            window = pl.ds(column, tile)
            loads[spot] = [
                copies.move(outs[e].at[:, :, :, window], up_tile.at[spot % 2]),
                copies.move(outs[2 + e].at[:, :, :, window], down_tile.at[spot % 2]),
            ]

        def feed(spot):
            half, e, column = tiles[spot]
            if spot not in loads:
                load(spot)
            for copy in loads[spot]:
                copy.wait()
            if spot + 1 < len(tiles) and tiles[spot + 1][0] == half:
                load(spot + 1)
            up = up_tile.at[spot % 2]
            down = down_tile.at[spot % 2]

            def body(span):
                value = mm(normed[span], up[...].reshape(width, tile), NN) + up_add[e : e + 1, column : column + tile]
                hidden[e][span, column : column + tile] = value
                value = gelu_tanh(value).astype(low)
                active[e][span, column : column + tile] = value
                after[span] += mm(value, down[...].reshape(width, tile), NT)

            row_chunks(tokens, body)

        work += [(functools.partial(feed, spot), tiles[spot][0]) for spot in range(len(tiles))]
        crossing = []

        def follow():
            def body(span):
                following[0][span] = (unit_rows(after[span]) * vectors[4:5] + vectors[5:6]).astype(low)

            row_chunks(tokens, body)
            crossing.append(copies.push(following[0], following[1], ids[3]))

        if coming:
            work.append((follow, None))
        run_staggered(running, FORWARD_LEADS, work, 2)
        for copy in crossing:
            copy.wait_recv()
        copies.finish()

    outs = pl.pallas_call(
        kernel,
        in_specs=anywhere(total) + on_vmem(len(inputs) - 2) + on_smem(2),
        out_specs=anywhere(len(shapes)) + on_vmem(len(more)),
        out_shape=shapes + more,
        scratch_shapes=[
            pltpu.VMEM((2, 2, chips, rows, tile), low),
            pltpu.VMEM((2, 2, chips, rows, tile), low),
            pltpu.SemaphoreType.DMA((count,)),
            pltpu.SemaphoreType.DMA((count,)),
            pltpu.SemaphoreType.DMA((total + 2 + 8 * inner // tile,)),
        ],
        compiler_params=pltpu.CompilerParams(
            collective_id=collective, has_side_effects=True, vmem_limit_bytes=58 * 1024 * 1024
        ),
        name="forward_layer",
    )(*shards, *inputs)
    weights = [out.reshape(-1, out.shape[-1]) for out in outs[: 2 * total]]
    return (weights, outs[2 * total :])


def add_rows(target, source):
    rows, columns = target.shape
    step = 256 if columns % 256 == 0 else 128

    @pl.loop(0, columns // step)
    def tile(i):
        window = pl.ds(pl.multiple_of(i * step, step), step)
        target[:, window] = (target[:, window].astype(jnp.float32) + source[:, window].astype(jnp.float32)).astype(
            target.dtype
        )


def products(lefts, rights, span, target, near):
    blocks, rows, width = target.shape
    step = 512

    def tile(window):
        out = mm(lefts[0][span], rights[0][:, window], NN)
        for j in range(1, len(rights)):
            out = out + mm(lefts[j][span], rights[j][:, window], NN)
        out = out.reshape(blocks, rows, step)
        if near is not None:
            out = out + near[:, :, window].astype(jnp.float32)
        target[:, :, window] = out.astype(target.dtype)

    if width == step:
        tile(slice(None))
        return

    @pl.loop(0, width // step)
    def one(i):
        tile(pl.ds(pl.multiple_of(i * step, step), step))


def scatter_steps(copies, ids, ring, arrays, shared, place):
    ahead, behind, sibling, across = ids
    chips = ring.chips
    half = chips // 2
    group_blocks = chips // 2
    slot = ring.turns.index
    near = {}
    crossed = {}
    loads = {}

    def rights(i, e):
        source = arrays[i][0]
        if not source[3]:
            return source[2][e]
        if e in loads:
            loads.pop(e).wait()
        return [shared["wide"].at[e]]

    def outgoing(group):
        blocks = pl.ds(group * group_blocks, group_blocks)
        if group == 0:
            for source, early, out, room in arrays:
                if source[0] == "product" and source[3]:
                    for e in (1, 0):
                        loads[e] = pltpu.make_async_copy(source[2][e][0], shared["wide"].at[e], shared["loaded"].at[e])
                        loads[e].start()
        for copy in shared["busy"]:
            copies.settle(copy)
        shared["busy"] = []
        if group == 0 and not place[0]:
            pl.semaphore_wait(shared["free"], 1)
        for i, (source, early, out, room) in enumerate(arrays):
            for e in (1, 0):
                if source[0] == "given":
                    near[i, e, group] = copies.push(source[1][e][1].at[blocks], room["near"].at[e, blocks], sibling)
                    continue
                sent = room["outbox"].at[e]
                height = group_blocks * out.shape[0]
                span = pl.ds((2 + group) * height, height)
                products(source[1], rights(i, e), span, sent, None)
                near[i, e, group] = copies.push(sent, room["near"].at[e, blocks], sibling)
                shared["busy"].append(near[i, e, group])

    def own(group):
        blocks = pl.ds(group * group_blocks, group_blocks)
        for e in (1, 0):
            for i, (source, early, out, room) in enumerate(arrays):
                near[i, e, group].wait_recv()
                target = room["sum"].at[e, blocks]
                if source[0] == "given":
                    target[...] = source[1][e][0][blocks] + room["near"][e, blocks]
                else:
                    height = group_blocks * out.shape[0]
                    span = pl.ds(group * height, height)
                    products(source[1], rights(i, e), span, target, room["near"].at[e, blocks])
                if e == 1:
                    rest = pl.ds(early, out.shape[1] - early)
                    for block in range(group * group_blocks, (group + 1) * group_blocks):
                        crossed[i, block] = copies.push(room["sum"].at[1, block, :, rest], room["far"].at[block], across)
        if group == 1 and not place[1]:
            pl.semaphore_signal(shared["free"], inc=1, device_id=sibling, device_id_type=MESH)

    def second(spot):
        block = slot(spot)
        for i, (source, early, out, room) in enumerate(arrays):
            rest = pl.ds(early, out.shape[1] - early)
            crossed[i, block].wait_recv()
            add_rows(room["sum"].at[0, block, :, rest], room["far"].at[block])

    def windows(size, hop, upward):
        if hop > 0:
            return pl.ds(0, size)
        return pl.ds(size // 2, size // 2) if upward else pl.ds(0, size // 2)

    def send(hop, spot, upward):
        target = ahead if upward else behind
        kinds = ("up", "up_slim") if upward else ("down", "down_slim")
        out_copies = []
        for i, (source, early, out, room) in enumerate(arrays):
            for e, size in ((0, out.shape[1]), (1, early)):
                window = windows(size, hop, upward)
                out_copies.append(
                    copies.push(room["sum"].at[e, slot(spot), :, window], room[kinds[e]].at[hop, :, window], target)
                )
        return out_copies

    def receive(hop, spot, upward, arrivals):
        kinds = ("up", "up_slim") if upward else ("down", "down_slim")
        at = 0
        for i, (source, early, out, room) in enumerate(arrays):
            for e, size in ((0, out.shape[1]), (1, early)):
                window = windows(size, hop, upward)
                arrivals[at].wait_recv()
                add_rows(room["sum"].at[e, slot(spot), :, window], room[kinds[e]].at[hop, :, window])
                at += 1

    outgoing(0)
    yield
    own(0)
    yield
    outgoing(1)
    own(1)
    yield
    second(half)
    up = send(0, half, True)
    down = send(0, half, False)
    yield
    for hop in range(1, half):
        second(chips - half + hop)
        second(half - hop)
        receive(hop - 1, chips - half + hop, True, up)
        up = send(hop, chips - half + hop, True)
        receive(hop - 1, half - hop, False, down)
        down = send(hop, half - hop, False)
        yield
    second(0)
    final = []
    at = 0
    for i, (source, early, out, room) in enumerate(arrays):
        for e in range(2):
            up[at].wait_recv()
            down[at].wait_recv()
            at += 1
        part = room["sum"][1, slot(0), :, :early].astype(jnp.float32)
        part = part + room["up_slim"][half - 1].astype(jnp.float32) + room["down_slim"][half - 1].astype(jnp.float32)
        room["slim_out"][...] = part.astype(room["slim_out"].dtype)
        final.append(copies.push(room["slim_out"], room["slim_in"], across))
    yield
    for i, (source, early, out, room) in enumerate(arrays):
        total = room["sum"][0, slot(0)].astype(jnp.float32) + room["up"][half - 1].astype(jnp.float32)
        out[...] = total + room["down"][half - 1].astype(jnp.float32)
        final[i].wait_recv()
        out[:, :early] += room["slim_in"][...].astype(jnp.float32)


def scatter_order(chips, groups):
    hops = chips // 2 - 1
    if groups == 1:
        return [0] * (hops + 6)
    order = [0] * 4 + [1] * 3 + [0, -1] * hops + [1, 0, -1] + [1, -1] * (hops - 1)
    return order + [-2] + [2] * 3 + [1] + [2, 1] + [2] * hops + [2] + [0, 1, 2]


def scatter_count(chips, arrays):
    half = chips // 2
    return arrays * (4 + chips + half * 4 + 1)


ROOM = ("sum", "far", "up", "down", "up_slim", "down_slim", "slim_out", "slim_in", "near")


def scatter_room(chips, rows, columns, early, dtype, given):
    half = chips // 2
    shapes = [
        (2, chips, rows, columns),
        (chips, rows, columns - early),
        (half, rows, columns),
        (half, rows, columns),
        (half, rows, early),
        (half, rows, early),
        (rows, early),
        (rows, early),
    ]
    if given:
        shapes.append((2, chips, rows, columns))
    return [pltpu.VMEM(shape, dtype) for shape in shapes]


def scatter_given(ring, parts, early, collective):
    chips = ring.chips
    height, columns = parts[0][0].shape
    rows = height // chips
    dtype = parts[0][0].dtype
    room = scatter_room(chips, rows, columns, early, dtype, True)
    count = scatter_count(chips, 1)

    def kernel(*refs):
        ids = ring.neighbours()
        greet(ids)
        scratch = refs[5:]
        copies = Copies(scratch[len(room)], scratch[len(room) + 1], None)
        source = ("given", (refs[:2], refs[2:4]))
        members = [(source, early, refs[4], dict(zip(ROOM, scratch)))]
        run_all(scatter_steps(copies, ids, ring, members, {"busy": []}, (True, True)))
        copies.finish()

    return pl.pallas_call(
        kernel,
        in_specs=on_vmem(4),
        out_specs=on_vmem(1)[0],
        out_shape=jax.ShapeDtypeStruct((rows, columns), dtype),
        scratch_shapes=room + [pltpu.SemaphoreType.DMA((count,)), pltpu.SemaphoreType.DMA((count,))],
        compiler_params=pltpu.CompilerParams(collective_id=collective, has_side_effects=True),
        name="scatter_given",
    )(*[parts[e][c].reshape(chips, rows, columns) for e in range(2) for c in range(2)])


def backward_layer(ring, groups, collective, attention):
    chips = ring.chips
    arrays = [member for group in groups for member in group]
    total = len(arrays)
    qkv, first, grad_heads, lse, slopes, prefix, scale = attention
    height, tokens = arrays[0][0][0].shape
    rows = height // chips // 2
    low = jnp.bfloat16
    inputs, wide = ([], [])

    def entry(array):
        if isinstance(array, int):
            return array
        for spot, other in enumerate(inputs):
            if other is array:
                return ("in", spot)
        inputs.append(array)
        wide.append(array.shape[1] > 1024)
        return ("in", len(inputs) - 1)

    plans, shapes, rooms, widths = ([], [], [], [])
    for lefts, rights, early in arrays:
        plans.append(([entry(left) for left in lefts], [[entry(right) for right in side] for side in rights], early))
        sample = rights[0][0]
        columns = grad_heads[0].shape[1] if isinstance(sample, int) else sample.shape[1]
        widths.append(columns)
        shapes.append(jax.ShapeDtypeStruct((rows, columns), jnp.float32))
        rooms += scatter_room(chips, rows, columns, early, low, False)
    extra = list(qkv) + list(first) + list(grad_heads) + list(lse) + [slopes, prefix]
    made = [jax.ShapeDtypeStruct(grad_heads[0].shape, low)] * 10
    sizes = iter(widths)
    span = max(sum(next(sizes) for unused in group) for group in groups)

    def kernel(*refs):
        ins, refs = (refs[: len(inputs)], refs[len(inputs) :])
        more, refs = (refs[: len(extra)], refs[len(extra) :])
        outs, refs = (refs[:total], refs[total:])
        back, scratch = (refs[: len(made)], refs[len(made) :])
        ids = ring.neighbours()
        greet(ids)
        held, outbox, near, sums, send, recv, loaded, free = scratch[len(rooms) :]
        copies = Copies(send, recv, None)
        shared = {"wide": held, "loaded": loaded, "free": free, "busy": []}
        find = lambda spot: back[spot] if isinstance(spot, int) else ins[spot[1]]
        running = []
        at = 0
        for number, group in enumerate(groups):
            members = []
            column = 0
            for unused in group:
                lefts, rights, early = plans[at]
                source = ("product", [find(spot) for spot in lefts], [[find(spot) for spot in half] for half in rights])
                source += (widths[at] > 1024,)
                room = dict(zip(ROOM, scratch[at * (len(ROOM) - 1) : (at + 1) * (len(ROOM) - 1)]))
                window = pl.ds(column, widths[at])
                room["outbox"] = outbox.at[:, :, :, window]
                room["near"] = near.at[:, :, :, window]
                members.append((source, early, outs[at], room))
                column += widths[at]
                at += 1
            place = (number == 0, number == len(groups) - 1)
            running.append(scatter_steps(copies, ids, ring, members, shared, place))
        parts = [(more[e], more[2 + e], more[4 + e], more[6 + e], back[5 * e : 5 * e + 5]) for e in range(2)]
        work = backward_work(parts, more[8], more[9][0], scale, sums)
        for turn in scatter_order(chips, len(groups)):
            if turn >= 0:
                next(running[turn], None)
            elif turn == -1 and work:
                work.pop(0)()
            elif turn == -2:
                while work:
                    work.pop(0)()
        copies.finish()

    count = scatter_count(chips, total)
    outs = pl.pallas_call(
        kernel,
        in_specs=[pl.BlockSpec(memory_space=pl.ANY if far else pltpu.VMEM) for far in wide] + on_vmem(8) + on_smem(2),
        out_specs=on_vmem(total + len(made)),
        out_shape=shapes + made,
        scratch_shapes=rooms
        + [
            pltpu.VMEM((2, tokens, max(widths)), low),
            pltpu.VMEM((2, chips // 2, rows, span), low),
            pltpu.VMEM((2, chips, rows, span), low),
            pltpu.VMEM((4, tokens, 128), jnp.float32),
            pltpu.SemaphoreType.DMA((count,)),
            pltpu.SemaphoreType.DMA((count,)),
            pltpu.SemaphoreType.DMA((2,)),
            pltpu.SemaphoreType.REGULAR,
        ],
        compiler_params=pltpu.CompilerParams(
            collective_id=collective, has_side_effects=True, vmem_limit_bytes=62 * 1024 * 1024
        ),
        name="backward_layer",
    )(*inputs, *extra)
    return (outs[:total], outs[total:])


def small_parts(vector_grads, bias_grads, by_half, placed, piece, lane):
    layers, dp = (len(vector_grads), placed.shape[0])
    vectors = jnp.stack([vector_grads[layer][i] for i in range(6) for layer in range(layers)])
    vectors = by_half(vectors.reshape(6 * layers, dp, 2, piece).transpose(2, 1, 0, 3), 0).reshape(2, dp, -1)
    shifts = [jnp.stack([bias_grads[layer][i] for layer in range(layers)], axis=1) for i in range(2)]
    shifts = jnp.concatenate([member.reshape(2, -1, dp, lane) for member in shifts], axis=1)
    shifts = jnp.einsum("tndl,bd->tbnl", shifts, placed, precision=lax.Precision.HIGHEST).reshape(2, dp, -1)
    packed = jnp.concatenate([vectors, shifts], axis=2)
    packed = jnp.pad(packed, ((0, 0), (0, 0), (0, 8 * 512 - packed.shape[2]))).reshape(2, 2, -1, 512)
    return [[packed[e, c] for c in range(2)] for e in range(2)]


def local(
    states_in,
    teacher,
    valid_mask,
    prefix_len,
    ln1_gain,
    ln1_shift,
    qkv_weight,
    qkv_bias,
    out_weight,
    out_bias,
    ln2_gain,
    ln2_shift,
    up_weight,
    up_bias,
    down_weight,
    down_bias,
):
    f32, low = (jnp.float32, jnp.bfloat16)
    layers, local_rows = (qkv_weight.shape[0], states_in.shape[1])
    width = states_in.shape[2]
    dp, tensor = (lax.axis_size("dp"), lax.axis_size("tensor"))
    here, side = (lax.axis_index("dp"), lax.axis_index("tensor"))
    ring = Ring(dp)
    piece = width // (dp * tensor)

    def by_half(pair, axis):
        return jnp.where(side == 0, pair, jnp.flip(pair, axis))

    owners = lax.dynamic_index_in_dim(jnp.asarray(ring.owners()), here, 0, keepdims=False)
    rows = width // dp
    columns = (owners[:, None] * rows + jnp.arange(rows, dtype=jnp.int32)[None]).reshape(1, width)
    to_ring = (jnp.arange(width, dtype=jnp.int32)[:, None] == columns).astype(low)

    placed = (owners[:, None] == jnp.arange(dp, dtype=jnp.int32)[None]).astype(f32)

    def into_ring(values):
        return jnp.dot(values, to_ring, preferred_element_type=f32)

    def from_ring(values, precision=None):
        return lax.dot_general(
            values, to_ring.astype(values.dtype), NT, precision=precision, preferred_element_type=f32
        )

    count = jnp.sum(valid_mask)
    vectors = jnp.stack([ln1_gain, ln1_shift, out_bias, ln2_gain, ln2_shift, down_bias])
    packed = jnp.concatenate(
        [vectors.reshape(-1), qkv_bias.reshape(-1), up_bias.reshape(-1), jnp.stack([count // 256, count % 256]).astype(low)]
    )
    first, second, third = (vectors.size, vectors.size + qkv_bias.size, vectors.size + qkv_bias.size + up_bias.size)
    packed = jnp.pad(packed, (0, 16 * 512 - packed.size)).reshape(16, 512)
    groups = []
    for layer in range(layers):
        groups.append([(qkv_weight[layer].reshape(rows, -1), 512), (out_weight[layer].T, 256)])
        groups.append([(up_weight[layer], 768), (down_weight[layer].T, 768)])
    weights = gather_weights(ring, [[(packed, 256)] + groups[0]], 1)[0]
    everything = by_half(jnp.stack([member.reshape(dp, -1) for member in weights[:2]]), 0)
    gathered = weights[2:]
    vectors = everything[:, :, :first].reshape(tensor, dp, 6, layers, piece).transpose(2, 3, 1, 0, 4)
    small = vectors.reshape(6, layers, 1, width).astype(f32)
    lane = qkv_bias.shape[3]
    biases = everything[:, :, first:third].reshape(tensor, dp, -1, lane)
    biases = jnp.einsum("tbnl,bd->tndl", biases, placed.astype(low), preferred_element_type=f32)
    biases = by_half(biases.reshape(tensor, -1, dp * lane), 0)
    split = (second - first) // lane
    qkv_add = biases[:, :split].reshape(tensor, layers, 1, -1).transpose(1, 0, 2, 3)
    up_add = biases[:, split:].reshape(tensor, layers, 1, -1).transpose(1, 0, 2, 3)
    counts = jnp.sum(everything[:, :, third : third + 2].astype(f32), axis=(0, 1))
    valid_count = counts[0] * 256.0 + counts[1]

    scale = HD ** (-0.5)
    pieces = jnp.arange(H, dtype=jnp.int32)
    heads_half = H // tensor
    heads = (pieces // heads_half ^ side) * heads_half + pieces % heads_half
    slopes = jnp.exp2(-(heads.astype(f32) + 1.0) * 8.0 / H) * LOG2E

    before_first = lax.ppermute(states_in[0], "tensor", [(0, 1)])
    states = into_ring(states_in[0])
    target = into_ring(teacher[0])
    kept = []
    for layer in range(layers):
        qkv_proj, out_proj = (gathered[8 * layer : 8 * layer + 2], gathered[8 * layer + 2 : 8 * layer + 4])
        if layer == 0:
            normed = norm_rows(states, small[0][layer], small[1][layer]).astype(low)
            normed_first = norm_rows(into_ring(before_first), small[0][layer], small[1][layer]).astype(low)
        else:
            normed, normed_first = following
        qkv, kv_first = ([], [])
        for i in range(tensor):
            query = qkv_proj[i].shape[1] // 3
            mixed = jnp.dot(normed, qkv_proj[i], preferred_element_type=f32) + qkv_add[layer][i]
            qkv.append(mixed.astype(low))
            mixed = jnp.dot(normed_first, qkv_proj[i][:, query:], preferred_element_type=f32)
            kv_first.append((mixed + qkv_add[layer][i][:, query:]).astype(low))
        coming = groups[2 * layer + 2] if layer + 1 < layers else []
        rest = jnp.stack(
            [small[i][layer][0] for i in (2, 3, 4, 5)] + [small[i][(layer + 1) % layers][0] for i in (0, 1)]
        )
        weights, made = forward_layer(
            ring,
            [shard for shard, early in groups[2 * layer + 1]],
            coming,
            2 + layer,
            (qkv, kv_first, slopes, prefix_len, scale),
            states,
            out_proj,
            rest,
            up_add[layer].reshape(tensor, -1),
        )
        gathered += weights
        heads_out, lse, middle, normed_two, hidden, active, after = (
            made[:2],
            made[2:4],
            made[4],
            made[5],
            made[6:8],
            made[8:10],
            made[10],
        )
        kept.append((states, normed, normed_first, qkv, kv_first, lse, heads_out, middle, normed_two, hidden, active))
        states, following = (after, made[11:])

    final_states = from_ring(states.astype(low)).astype(low)[None]
    factor = local_rows * tensor * dp / valid_count
    grad = factor * valid_mask[0][:, None].astype(f32) * (states - target)
    weight_grads = [None] * layers
    vector_grads = [None] * layers
    bias_grads = [None] * layers
    for layer in reversed(range(layers)):
        before, normed, normed_first, qkv, kv_first, lse, heads_out, middle, normed_two, hidden, active = kept[layer]
        qkv_proj, out_proj, up_proj, down_proj = [gathered[8 * layer + i : 8 * layer + i + 2] for i in (0, 2, 4, 6)]
        grad_mlp = grad.astype(low)
        down_shift = jnp.sum(grad_mlp.astype(f32), axis=0)
        grad_hidden = []
        for i in range(tensor):
            grad_active = jnp.dot(grad_mlp, down_proj[i], preferred_element_type=f32)
            grad_hidden.append(jax.vjp(gelu_tanh, hidden[i])[1](grad_active)[0].astype(low))
        up_shift = jnp.stack([jnp.sum(values.astype(f32), axis=0) for values in grad_hidden])
        grad_normed = mm(grad_hidden[0], up_proj[0], NT) + mm(grad_hidden[1], up_proj[1], NT)
        part, gain_two, shift_two = norm_back(middle, small[3][layer], grad_normed)
        grad_middle = grad + part
        grad_attn = grad_middle.astype(low)
        out_shift = jnp.sum(grad_attn.astype(f32), axis=0)
        grad_heads = [jnp.dot(grad_attn, out_proj[i], preferred_element_type=f32).astype(low) for i in range(tensor)]
        lefts = [normed.T, normed_first.T]
        (down_grad, up_grad, out_grad, *mixed), grads = backward_layer(
            ring,
            [
                [([grad_mlp.T], [[values] for values in active], 512)],
                [([normed_two.T], [[values] for values in grad_hidden], 512)],
                [
                    ([grad_attn.T], [[values] for values in heads_out], 256),
                    (lefts[:1], [[0], [5]], 256),
                    (lefts, [[1, 3], [6, 8]], 256),
                    (lefts, [[2, 4], [7, 9]], 256),
                ],
            ],
            10 + layer,
            (qkv, kv_first, grad_heads, lse, slopes, prefix_len, scale),
        )
        weight_grads[layer] = (jnp.stack(mixed, axis=1), out_grad.T, up_grad, down_grad)
        grad_normed = 0.0
        qkv_shift = []
        sent = 0.0
        for i in range(tensor):
            query = grads[5 * i].shape[1]
            grad_qkv = jnp.concatenate(grads[5 * i : 5 * i + 3], axis=1)
            grad_first = jnp.concatenate(grads[5 * i + 3 : 5 * i + 5], axis=1)
            sent = sent + mm(grad_first, qkv_proj[i][:, query:], NT)
            shift = jnp.sum(grad_qkv.astype(f32), axis=0)
            qkv_shift.append(shift + jnp.pad(jnp.sum(grad_first.astype(f32), axis=0), (query, 0)))
            grad_normed = grad_normed + mm(grad_qkv, qkv_proj[i], NT)
        arrived = lax.ppermute(sent.astype(low), "tensor", [(1, 0)])
        qkv_shift = jnp.stack(qkv_shift)
        grad_normed = grad_normed + arrived.astype(f32)
        part, gain_one, shift_one = norm_back(before, small[0][layer], grad_normed)
        grad = grad_middle + part
        vector_grads[layer] = (gain_one, shift_one, out_shift, gain_two, shift_two, down_shift)
        bias_grads[layer] = (qkv_shift, up_shift)

    summed = scatter_given(ring, small_parts(vector_grads, bias_grads, by_half, placed, piece, lane), 256, 20)
    summed = summed.reshape(-1)
    input_grad = from_ring(grad, lax.Precision.HIGHEST)[None]
    qkv_grad, out_grad, up_grad, down_grad = [
        jnp.stack([weight_grads[layer][i] for layer in range(layers)]) for i in range(4)
    ]
    vectors = summed[:first].reshape(6, layers, piece)
    return (
        final_states,
        input_grad,
        vectors[0],
        vectors[1],
        qkv_grad,
        summed[first:second].reshape(qkv_bias.shape),
        out_grad,
        vectors[2],
        vectors[3],
        vectors[4],
        up_grad,
        summed[second:third].reshape(up_bias.shape),
        down_grad.transpose(0, 2, 1),
        vectors[5],
    )


def solution(mesh):
    return jax.shard_map(
        local,
        mesh=mesh,
        in_specs=(
            P("dp", "tensor", None),
            P("dp", "tensor", None),
            P("dp", "tensor"),
            P("dp"),
            P(None, ("dp", "tensor")),
            P(None, ("dp", "tensor")),
            P(None, "dp", None, "tensor"),
            P(None, None, "tensor", "dp"),
            P(None, "tensor", "dp"),
            P(None, ("dp", "tensor")),
            P(None, ("dp", "tensor")),
            P(None, ("dp", "tensor")),
            P(None, "dp", "tensor"),
            P(None, "tensor", "dp"),
            P(None, "tensor", "dp"),
            P(None, ("dp", "tensor")),
        ),
        out_specs=(
            P("dp", "tensor", None),
            P("dp", "tensor", None),
            P(None, ("dp", "tensor")),
            P(None, ("dp", "tensor")),
            P(None, "dp", None, "tensor"),
            P(None, None, "tensor", "dp"),
            P(None, "tensor", "dp"),
            P(None, ("dp", "tensor")),
            P(None, ("dp", "tensor")),
            P(None, ("dp", "tensor")),
            P(None, "dp", "tensor"),
            P(None, "tensor", "dp"),
            P(None, "tensor", "dp"),
            P(None, ("dp", "tensor")),
        ),
        check_vma=False,
    )
```

```python
import functools

import jax
import jax.numpy as jnp
import numpy as np
from jax import lax
from jax.experimental import pallas as pl
from jax.experimental.pallas import tpu as pltpu
from jax.sharding import PartitionSpec as P

LOG2E = 1.4426950408889634
BIG = 1000000000.0
NT = (((1,), (1,)), ((), ()))
NN = (((1,), (0,)), ((), ()))


def mm(a, b, dims):
    return lax.dot_general(a, b, dims, preferred_element_type=jnp.float32)


def lane_masks(width):
    lanes = lax.broadcasted_iota(jnp.int32, (1, width), 1)
    low = jnp.where(lanes < width // 2, 1.0, 0.0)
    return (low.astype(jnp.bfloat16), (1.0 - low).astype(jnp.bfloat16))


def rows_iota(n, m):
    return lax.broadcasted_iota(jnp.int32, (n, m), 0)


def cols_iota(n, m):
    return lax.broadcasted_iota(jnp.int32, (n, m), 1)


def scores_first(keys, query, slope, scale, prefix, start):
    n, m = (keys.shape[0], query.shape[0])
    key_pos = rows_iota(n, m)
    query_pos = cols_iota(n, m) + start
    distance = jnp.abs(query_pos - key_pos).astype(jnp.float32)
    raw = mm(keys, query, NT) * scale - slope * distance
    visible = (key_pos <= query_pos) | (key_pos < prefix)
    return jnp.where(visible, raw, -BIG)


def scores_second(keys, query, slope, scale, offset, mask_start):
    n, m = (keys.shape[0], query.shape[0])
    bias = slope * (rows_iota(n, 1) + offset).astype(jnp.float32)
    raw = mm(keys, query, NT) * scale + bias
    if mask_start is None:
        return raw
    return jnp.where(rows_iota(n, m) + mask_start <= cols_iota(n, m), raw, -BIG)


def score_parts(half, k_ref, k0_ref, query, slope, scale, prefix, start, step):
    rows = k_ref.shape[0]
    if half == 0:
        return [(None, 0, rows, scores_first(k_ref[...], query, slope, scale, prefix, start))]
    parts = [(0, 0, rows, scores_second(k0_ref[...], query, slope, scale, -2 * rows, None))]
    if start > 0:
        parts.append((1, 0, start, scores_second(k_ref[:start], query, slope, scale, -rows, None)))
    parts.append(
        (1, start, start + step, scores_second(k_ref[start : start + step], query, slope, scale, start - rows, 0))
    )
    return parts


def forward_body(half, pair, slopes, prefix, scale, q_ref, k_ref, v_ref, k0_ref, v0_ref, o_ref, lse_ref, step):
    rows, width = q_ref.shape
    masks = lane_masks(width)
    head = width // 2
    values = v_ref[...].T
    values0 = v0_ref[...].T if half else None
    for start in range(0, rows, step):
        outs = []
        for side in range(2):
            query = q_ref[start : start + step] * masks[side]
            slope = slopes[pair * 2 + side]
            parts = score_parts(half, k_ref, k0_ref, query, slope, scale, prefix, start, step)
            top = parts[0][3].max(axis=0, keepdims=True)
            for part in parts[1:]:
                top = jnp.maximum(top, part[3].max(axis=0, keepdims=True))
            total = None
            out = None
            for which, low, high, raw in parts:
                raised = jnp.exp2(raw - top)
                part_sum = raised.sum(axis=0, keepdims=True)
                held = values0 if which == 0 else values
                held = held[side * head : (side + 1) * head, low:high]
                part_out = mm(held, raised.astype(jnp.bfloat16), NN)
                total = part_sum if total is None else total + part_sum
                out = part_out if out is None else out + part_out
            outs.append(out / total)
            lse_ref[0, side : side + 1, start : start + step] = top + jnp.log2(total)
        o_ref[start : start + step] = jnp.concatenate(outs, axis=0).T.astype(jnp.bfloat16)


def backward_body(half, pair, slopes, prefix, scale, refs, step):
    q_ref, k_ref, v_ref, k0_ref, v0_ref, g_ref, lse_ref, gq_ref, gk_ref, gv_ref, gk0_ref, gv0_ref, sums = refs
    rows, width = q_ref.shape
    masks = lane_masks(width)
    head = width // 2
    keys = k_ref[...].T
    keys0 = k0_ref[...].T if half else None
    sums[...] = jnp.zeros_like(sums)
    for start in range(0, rows, step):
        outs = []
        for side in range(2):
            query = q_ref[start : start + step] * masks[side]
            grad = g_ref[start : start + step] * masks[side]
            slope = slopes[pair * 2 + side]
            parts = score_parts(half, k_ref, k0_ref, query, slope, scale * LOG2E, prefix, start, step)
            lse = lse_ref[0, side : side + 1, start : start + step]
            inner = None
            held = []
            for which, low, high, raw in parts:
                share = jnp.exp2(raw - lse)
                value = v0_ref[low:high] if which == 0 else v_ref[low:high]
                slot = 2 if which == 0 else 0
                grad_share = mm(value, grad, NT)
                part = (share * grad_share).sum(axis=0, keepdims=True)
                inner = part if inner is None else inner + part
                sums[slot + 1, low:high] += mm(share.astype(jnp.bfloat16), grad, NN)
                held.append((which, low, high, share, grad_share, slot))
            out = None
            for which, low, high, share, grad_share, slot in held:
                grad_score = (share * (grad_share - inner)).astype(jnp.bfloat16)
                sums[slot, low:high] += mm(grad_score, query, NN)
                key = keys0 if which == 0 else keys
                part = mm(key[side * head : (side + 1) * head, low:high], grad_score, NN)
                out = part if out is None else out + part
            outs.append(out)
        gq_ref[start : start + step] = (jnp.concatenate(outs, axis=0).T * scale).astype(jnp.bfloat16)
    gk_ref[...] = (sums[0] * scale).astype(jnp.bfloat16)
    gv_ref[...] = sums[1].astype(jnp.bfloat16)
    gk0_ref[...] = (sums[2] * scale).astype(jnp.bfloat16)
    gv0_ref[...] = sums[3].astype(jnp.bfloat16)


def head_pairs(low, high, body):
    @pl.loop(low, high)
    def step(pair):
        columns = pl.multiple_of(pair * 128, 128)
        for half in range(2):
            @pl.when(lax.axis_index("tensor") == half)
            def one():
                body(half, pair, columns)


def forward_work(parts, slopes, prefix, scale):
    work = []
    for e, (qkv, first, out, lse) in enumerate(parts):
        pairs = out.shape[1] // 128
        rows = out.shape[0]

        def body(half, pair, columns, e=e, qkv=qkv, first=first, out=out, lse=lse, pairs=pairs, rows=rows):
            at = lambda ref, base: ref.at[:, pl.ds(columns + base * pairs * 128, 128)]
            forward_body(
                half,
                pair + e * pairs,
                slopes,
                prefix,
                scale * LOG2E,
                at(qkv, 0),
                at(qkv, 1),
                at(qkv, 2),
                at(first, 0),
                at(first, 1),
                at(out, 0),
                lse.at[pl.ds(pair, 1)],
                rows // 2,
            )

        for low in range(0, pairs, 2):
            work.append(functools.partial(head_pairs, low, low + 2, body))
    return work


def backward_work(parts, slopes, prefix, scale, sums):
    work = []
    for e, (qkv, first, grad, lse, outs) in enumerate(parts):
        pairs = grad.shape[1] // 128
        rows = grad.shape[0]

        def body(half, pair, columns, e=e, qkv=qkv, first=first, grad=grad, lse=lse, outs=outs, pairs=pairs, rows=rows):
            at = lambda ref, base: ref.at[:, pl.ds(columns + base * pairs * 128, 128)]
            refs = [at(qkv, 0), at(qkv, 1), at(qkv, 2), at(first, 0), at(first, 1), at(grad, 0), lse.at[pl.ds(pair, 1)]]
            refs += [at(out, 0) for out in outs] + [sums]
            backward_body(half, pair + e * pairs, slopes, prefix, scale, refs, rows // 2)

        for low in range(0, pairs, 2):
            work.append(functools.partial(head_pairs, low, low + 2, body))
    return work


EPS = 1e-05
H = 16
HD = 64
ROWS_CONTRACT = (((0,), (0,)), ((), ()))


def norm_parts(states):
    centered = states - jnp.mean(states, axis=-1, keepdims=True)
    inverse = lax.rsqrt(jnp.mean(centered * centered, axis=-1, keepdims=True) + EPS)
    return (centered * inverse, inverse)


def norm_rows(states, gain, shift):
    return norm_parts(states)[0] * gain + shift


def norm_back(states, gain, grad):
    unit, inverse = norm_parts(states)
    scaled = grad * gain
    first = jnp.mean(scaled, axis=-1, keepdims=True)
    second = jnp.mean(scaled * unit, axis=-1, keepdims=True)
    return (inverse * (scaled - first - unit * second), jnp.sum(grad * unit, axis=0), jnp.sum(grad, axis=0))


def gelu_tanh(values):
    return 0.5 * values * (1.0 + jnp.tanh(0.7978845608028654 * (values + 0.044715 * values * values * values)))


MESH = pl.DeviceIdType.MESH


class Ring:
    def __init__(self, devices):
        self.chips = devices // 2
        self.order = list(range(0, self.chips, 2)) + list(range(self.chips - 1, 0, -2))
        self.place = {chip: spot for spot, chip in enumerate(self.order)}
        half = self.chips // 2
        self.turns = [half] + [step for hop in range(half - 1, 0, -1) for step in (self.chips - hop, hop)] + [0]

    def owners(self):
        table = []
        for device in range(2 * self.chips):
            spot = self.place[device // 2]
            table.append(
                [
                    2 * self.order[(spot - step) % self.chips] + ((device % 2) ^ core)
                    for core in range(2)
                    for step in self.turns
                ]
            )
        return np.array(table, np.int32)

    def spot_chip(self, spot):
        half = self.chips // 2
        return jnp.where(spot < half, 2 * spot, 2 * (self.chips - 1 - spot) + 1)

    def neighbours(self):
        here, side = (lax.axis_index("dp"), lax.axis_index("tensor"))
        chip, core = (here // 2, here % 2)
        spot = jnp.where(chip % 2 == 0, chip // 2, self.chips - 1 - chip // 2)
        ahead = self.spot_chip((spot + 1) % self.chips) * 2 + core
        behind = self.spot_chip((spot + self.chips - 1) % self.chips) * 2 + core
        sibling = chip * 2 + (1 - core)
        return ((ahead, side), (behind, side), (sibling, side), (here, 1 - side))


def greet(targets):
    barrier = pltpu.get_barrier_semaphore()
    for target in targets:
        pl.semaphore_signal(barrier, inc=1, device_id=target, device_id_type=MESH)
    pl.semaphore_wait(barrier, len(targets))


class Copies:
    def __init__(self, send, recv, near):
        self.send, self.recv, self.near = (send, recv, near)
        self.sent, self.moved, self.spots = ([], [], 0)

    def push(self, source, target, device):
        spot = self.spots
        copy = pltpu.make_async_remote_copy(
            src_ref=source,
            dst_ref=target,
            send_sem=self.send.at[spot],
            recv_sem=self.recv.at[spot],
            device_id=device,
            device_id_type=MESH,
        )
        copy.start()
        self.sent.append(copy)
        self.spots += 1
        return copy

    def move(self, source, target):
        copy = pltpu.make_async_copy(source, target, self.near.at[len(self.moved)])
        copy.start()
        self.moved.append(copy)
        return copy

    def settle(self, copy):
        copy.wait_send()
        self.sent = [other for other in self.sent if other is not copy]

    def finish(self):
        for copy in self.sent:
            copy.wait_send()


def run_all(steps):
    for unused in steps:
        pass


def gather_steps(copies, ids, ring, arrays):
    ahead, behind, sibling, across = ids
    chips = ring.chips
    half = chips // 2
    slot = ring.turns.index
    local, siblings, early_in, late_in, up, down = ([], [], [], [], {}, {})
    for shard, own, other, early in arrays:
        early_in.append(copies.push(shard.at[:, pl.ds(0, early)], other.at[0, slot(0), :, pl.ds(0, early)], across))
    for i, (shard, own, other, early) in enumerate(arrays):
        local.append(copies.move(shard, own.at[0, slot(0)]))
        up[i, 1] = [copies.push(shard, own.at[0, slot(1)], ahead)]
        down[i, 1] = [copies.push(shard, own.at[0, slot(chips - 1)], behind)]
        siblings.append(copies.push(shard, own.at[1, slot(0)], sibling))
    for shard, own, other, early in arrays:
        width = shard.shape[1] - early
        late_in.append(copies.push(shard.at[:, pl.ds(early, width)], other.at[0, slot(0), :, pl.ds(early, width)], across))
    yield
    for i, (shard, own, other, early) in enumerate(arrays):
        early_in[i].wait_recv()
        part = other.at[0, slot(0), :, pl.ds(0, early)]
        up[i, 1].append(copies.push(part, other.at[0, slot(1), :, pl.ds(0, early)], ahead))
        down[i, 1].append(copies.push(part, other.at[0, slot(chips - 1), :, pl.ds(0, early)], behind))
    late = [(0, late_in)]
    for hop in range(1, half + 1):
        yield
        spots = [(hop, up, ahead), (chips - hop, down, behind)]
        crossing = {}
        if hop < half:
            for spot, arrivals, target in spots:
                crossing[spot] = []
                step = 1 if target is ahead else -1
                for i, (shard, own, other, early) in enumerate(arrays):
                    size = shard.shape[1]
                    arrivals[i, hop][0].wait_recv()
                    if hop + 1 < half:
                        window, slim = (pl.ds(0, size), pl.ds(0, early))
                    elif step == 1:
                        window, slim = (pl.ds(0, size // 2), pl.ds(0, early // 2))
                    else:
                        window, slim = (pl.ds(size // 2, size // 2), pl.ds(early // 2, early // 2))
                    arrivals[i, hop + 1] = [
                        copies.push(own.at[0, slot(spot), :, window], own.at[0, slot(spot + step), :, window], target)
                    ]
                    rest = pl.ds(early, size - early)
                    crossing[spot].append(copies.push(own.at[0, slot(spot), :, rest], other.at[0, slot(spot), :, rest], across))
                    siblings.append(copies.push(own.at[0, slot(spot)], own.at[1, slot(spot)], sibling))
                    arrivals[i, hop][1].wait_recv()
                    arrivals[i, hop + 1].append(
                        copies.push(other.at[0, slot(spot), :, slim], other.at[0, slot(spot + step), :, slim], target)
                    )
        else:
            crossing[half] = []
            for i, (shard, own, other, early) in enumerate(arrays):
                up[i, half][0].wait_recv()
                down[i, half][0].wait_recv()
                rest = pl.ds(early, shard.shape[1] - early)
                crossing[half].append(copies.push(own.at[0, slot(half), :, rest], other.at[0, slot(half), :, rest], across))
                siblings.append(copies.push(own.at[0, slot(half)], own.at[1, slot(half)], sibling))
                up[i, half][1].wait_recv()
                down[i, half][1].wait_recv()
        for spot, arrivals in late:
            for i, (shard, own, other, early) in enumerate(arrays):
                arrivals[i].wait_recv()
                siblings.append(copies.push(other.at[0, slot(spot)], other.at[1, slot(spot)], sibling))
        late = list(crossing.items())
    yield
    for spot, arrivals in late:
        for i, (shard, own, other, early) in enumerate(arrays):
            arrivals[i].wait_recv()
            siblings.append(copies.push(other.at[0, slot(spot)], other.at[1, slot(spot)], sibling))
    for copy in local:
        copy.wait()
    yield
    for copy in siblings:
        copy.wait_recv()


def gather_count(chips, arrays):
    half = chips // 2
    return arrays * (5 + 2 + (half - 1) * 2 * 4 + 2 + chips)


def on_vmem(count):
    return [pl.BlockSpec(memory_space=pltpu.VMEM)] * count


def on_smem(count):
    return [pl.BlockSpec(memory_space=pltpu.SMEM)] * count


def anywhere(count):
    return [pl.BlockSpec(memory_space=pl.ANY)] * count


def gather_weights(ring, groups, collective, attention=None):
    flat = [member for group in groups for member in group]
    total = len(flat)
    count = sum(gather_count(ring.chips, len(group)) for group in groups)
    shapes = [
        jax.ShapeDtypeStruct((2, ring.chips) + shard.shape, shard.dtype) for shard, early in flat for unused in range(2)
    ]
    inputs, more = ([], [])
    if attention is not None:
        qkv, first, slopes, prefix, scale = attention
        inputs = list(qkv) + list(first) + [slopes, prefix]
        rows, width = (qkv[0].shape[0], qkv[0].shape[1] // 3)
        more = [jax.ShapeDtypeStruct((rows, width), jnp.bfloat16)] * 2
        more += [jax.ShapeDtypeStruct((width // 128, 2, rows), jnp.float32)] * 2

    def kernel(*refs):
        shards, extra, refs = (refs[:total], refs[total : total + len(inputs)], refs[total + len(inputs) :])
        outs, made, scratch = (refs[: 2 * total], refs[2 * total : 2 * total + len(more)], refs[2 * total + len(more) :])
        ids = ring.neighbours()
        greet(ids)
        copies = Copies(*scratch)
        members = [(shards[i], outs[2 * i], outs[2 * i + 1], flat[i][1]) for i in range(total)]
        at = 0
        running = []
        for group in groups:
            running.append(gather_steps(copies, ids, ring, members[at : at + len(group)]))
            at += len(group)
        work = []
        if attention is not None:
            parts = [(extra[e], extra[2 + e], made[e], made[2 + e]) for e in range(2)]
            work = [(piece, None) for piece in forward_work(parts, extra[4], extra[5][0], scale)]
        run_staggered(running, (3,), work)
        copies.finish()

    outs = pl.pallas_call(
        kernel,
        in_specs=anywhere(total) + (on_vmem(4) + on_smem(2) if inputs else []),
        out_specs=anywhere(len(shapes)) + on_vmem(len(more)),
        out_shape=shapes + more,
        scratch_shapes=[
            pltpu.SemaphoreType.DMA((count,)),
            pltpu.SemaphoreType.DMA((count,)),
            pltpu.SemaphoreType.DMA((total,)),
        ],
        compiler_params=pltpu.CompilerParams(
            collective_id=collective, has_side_effects=True, vmem_limit_bytes=40 * 1024 * 1024
        ),
        name="gather_weights",
    )(*[shard for shard, early in flat], *inputs)
    weights = [out.reshape(-1, out.shape[-1]) for out in outs[: 2 * total]]
    return (weights, outs[2 * total : 2 * total + 2], outs[2 * total + 2 :])


def run_staggered(running, leads, work=(), most=1):
    waiting, work = (list(enumerate(running)), list(work))
    active, ended = ([], {None})
    leads = list(leads)
    needed, youngest = (0, 0)
    while waiting or active:
        if waiting and (youngest >= needed or not active):
            active.append(waiting.pop(0))
            needed, youngest = (leads.pop(0) if leads else 0, 0)
        youngest += 1
        for member in list(active):
            try:
                next(member[1])
            except StopIteration:
                active.remove(member)
                ended.add(member[0])
        for unused in range(most):
            if work and work[0][1] in ended:
                work.pop(0)[0]()
    for piece, need in work:
        piece()


def unit_rows(values):
    centered = values - jnp.mean(values, axis=-1, keepdims=True)
    return centered * lax.rsqrt(jnp.mean(centered * centered, axis=-1, keepdims=True) + EPS)


def row_chunks(rows, body):
    step = 256

    @pl.loop(0, rows // step)
    def chunk(i):
        body(pl.ds(pl.multiple_of(i * step, step), step))


FORWARD_SPANS = ((0, 1536, (512, 512)), (1536, 512, (256, 256)))
FORWARD_LEADS = (3, 3)


def forward_layer(ring, mlp, coming, collective, attention, states, out_proj, vectors, up_add):
    qkv, first, slopes, prefix, scale = attention
    shards = list(mlp) + [shard for shard, early in coming]
    total = len(shards)
    chips = ring.chips
    tokens, width = states.shape
    inner = mlp[0].shape[1]
    rows = mlp[0].shape[0]
    heads = qkv[0].shape[1] // 3
    tile = 512
    spans = FORWARD_SPANS
    count = len(spans) * gather_count(chips, 2) + gather_count(chips, max(len(coming), 1)) + 1
    shapes = [jax.ShapeDtypeStruct((2, chips) + shard.shape, shard.dtype) for shard in shards for unused in range(2)]
    f32, low = (jnp.float32, jnp.bfloat16)
    more = [jax.ShapeDtypeStruct((tokens, heads), low)] * 2
    more += [jax.ShapeDtypeStruct((heads // 128, 2, tokens), f32)] * 2
    more += [jax.ShapeDtypeStruct((tokens, width), f32), jax.ShapeDtypeStruct((tokens, width), low)]
    more += [jax.ShapeDtypeStruct((tokens, inner), f32)] * 2 + [jax.ShapeDtypeStruct((tokens, inner), low)] * 2
    more += [jax.ShapeDtypeStruct((tokens, width), f32)]
    if coming:
        more += [jax.ShapeDtypeStruct((tokens, width), low)] * 2
    inputs = list(qkv) + list(first) + [states] + list(out_proj) + [vectors, up_add, slopes, prefix]

    def kernel(*refs):
        sources, refs = (refs[:total], refs[total:])
        qkv, first, (states, out_0, out_1, vectors, up_add, slopes, prefix) = (refs[:2], refs[2:4], refs[4:11])
        outs, refs = (refs[11 : 11 + 2 * total], refs[11 + 2 * total :])
        heads_out, lse, middle, normed, hidden, active, after = (refs[:2], refs[2:4], refs[4], refs[5], refs[6:8], refs[8:10], refs[10])
        following, scratch = (refs[11 : len(more)], refs[len(more) :])
        up_tile, down_tile, send, recv, near = scratch
        ids = ring.neighbours()
        greet(ids)
        copies = Copies(send, recv, near)
        running = []
        for column, size, earlies in spans:
            window = pl.ds(column, size)
            members = []
            for i, early in enumerate(earlies):
                views = [outs[2 * i + j].at[:, :, :, window] for j in range(2)]
                members.append((sources[i].at[:, window], views[0], views[1], early))
            running.append(gather_steps(copies, ids, ring, members))
        if coming:
            members = [(sources[2 + i], outs[4 + 2 * i], outs[5 + 2 * i], coming[i][1]) for i in range(len(coming))]
            running.append(gather_steps(copies, ids, ring, members))
        parts = [(qkv[e], first[e], heads_out[e], lse[e]) for e in range(2)]
        work = [(piece, None) for piece in forward_work(parts, slopes, prefix[0], scale)]

        def project():
            def body(span):
                value = states[span] + mm(heads_out[0][span], out_0[...], NT) + mm(heads_out[1][span], out_1[...], NT)
                value = value + vectors[0:1]
                middle[span] = value
                normed[span] = (unit_rows(value) * vectors[1:2] + vectors[2:3]).astype(low)
                after[span] = value + vectors[3:4]

            row_chunks(tokens, body)

        work.append((project, None))
        tiles = [
            (group, e, column + i * tile)
            for group, (column, size, earlies) in enumerate(spans)
            for e in range(2)
            for i in range(size // tile)
        ]
        loads = {}

        def load(spot):
            half, e, column = tiles[spot]
            window = pl.ds(column, tile)
            loads[spot] = [
                copies.move(outs[e].at[:, :, :, window], up_tile.at[spot % 2]),
                copies.move(outs[2 + e].at[:, :, :, window], down_tile.at[spot % 2]),
            ]

        def feed(spot):
            half, e, column = tiles[spot]
            if spot not in loads:
                load(spot)
            for copy in loads[spot]:
                copy.wait()
            if spot + 1 < len(tiles) and tiles[spot + 1][0] == half:
                load(spot + 1)
            up = up_tile.at[spot % 2]
            down = down_tile.at[spot % 2]

            def body(span):
                value = mm(normed[span], up[...].reshape(width, tile), NN) + up_add[e : e + 1, column : column + tile]
                hidden[e][span, column : column + tile] = value
                value = gelu_tanh(value).astype(low)
                active[e][span, column : column + tile] = value
                after[span] += mm(value, down[...].reshape(width, tile), NT)

            row_chunks(tokens, body)

        work += [(functools.partial(feed, spot), tiles[spot][0]) for spot in range(len(tiles))]
        crossing = []

        def follow():
            def body(span):
                following[0][span] = (unit_rows(after[span]) * vectors[4:5] + vectors[5:6]).astype(low)

            row_chunks(tokens, body)
            crossing.append(copies.push(following[0], following[1], ids[3]))

        if coming:
            work.append((follow, None))
        run_staggered(running, FORWARD_LEADS, work, 2)
        for copy in crossing:
            copy.wait_recv()
        copies.finish()

    outs = pl.pallas_call(
        kernel,
        in_specs=anywhere(total) + on_vmem(len(inputs) - 2) + on_smem(2),
        out_specs=anywhere(len(shapes)) + on_vmem(len(more)),
        out_shape=shapes + more,
        scratch_shapes=[
            pltpu.VMEM((2, 2, chips, rows, tile), low),
            pltpu.VMEM((2, 2, chips, rows, tile), low),
            pltpu.SemaphoreType.DMA((count,)),
            pltpu.SemaphoreType.DMA((count,)),
            pltpu.SemaphoreType.DMA((total + 2 + 8 * inner // tile,)),
        ],
        compiler_params=pltpu.CompilerParams(
            collective_id=collective, has_side_effects=True, vmem_limit_bytes=58 * 1024 * 1024
        ),
        name="forward_layer",
    )(*shards, *inputs)
    weights = [out.reshape(-1, out.shape[-1]) for out in outs[: 2 * total]]
    return (weights, outs[2 * total :])


def add_rows(target, source):
    rows, columns = target.shape
    step = 256 if columns % 256 == 0 else 128

    @pl.loop(0, columns // step)
    def tile(i):
        window = pl.ds(pl.multiple_of(i * step, step), step)
        target[:, window] = (target[:, window].astype(jnp.float32) + source[:, window].astype(jnp.float32)).astype(
            target.dtype
        )


def products(lefts, rights, span, target, near):
    blocks, rows, width = target.shape
    step = 512

    def tile(window):
        out = mm(lefts[0][span], rights[0][:, window], NN)
        for j in range(1, len(rights)):
            out = out + mm(lefts[j][span], rights[j][:, window], NN)
        out = out.reshape(blocks, rows, step)
        if near is not None:
            out = out + near[:, :, window].astype(jnp.float32)
        target[:, :, window] = out.astype(target.dtype)

    if width == step:
        tile(slice(None))
        return

    @pl.loop(0, width // step)
    def one(i):
        tile(pl.ds(pl.multiple_of(i * step, step), step))


def scatter_steps(copies, ids, ring, arrays, shared, place):
    ahead, behind, sibling, across = ids
    chips = ring.chips
    half = chips // 2
    group_blocks = chips // 2
    slot = ring.turns.index
    near = {}
    crossed = {}
    loads = {}

    def rights(i, e):
        source = arrays[i][0]
        if not source[3]:
            return source[2][e]
        if e in loads:
            loads.pop(e).wait()
        return [shared["wide"].at[e]]

    def outgoing(group):
        blocks = pl.ds(group * group_blocks, group_blocks)
        if group == 0:
            for source, early, out, room in arrays:
                if source[0] == "product" and source[3]:
                    for e in (1, 0):
                        loads[e] = pltpu.make_async_copy(source[2][e][0], shared["wide"].at[e], shared["loaded"].at[e])
                        loads[e].start()
        for copy in shared["busy"]:
            copies.settle(copy)
        shared["busy"] = []
        if group == 0 and not place[0]:
            pl.semaphore_wait(shared["free"], 1)
        for i, (source, early, out, room) in enumerate(arrays):
            for e in (1, 0):
                if source[0] == "given":
                    near[i, e, group] = copies.push(source[1][e][1].at[blocks], room["near"].at[e, blocks], sibling)
                    continue
                sent = room["outbox"].at[e]
                height = group_blocks * out.shape[0]
                span = pl.ds((2 + group) * height, height)
                products(source[1], rights(i, e), span, sent, None)
                near[i, e, group] = copies.push(sent, room["near"].at[e, blocks], sibling)
                shared["busy"].append(near[i, e, group])

    def own(group):
        blocks = pl.ds(group * group_blocks, group_blocks)
        for e in (1, 0):
            for i, (source, early, out, room) in enumerate(arrays):
                near[i, e, group].wait_recv()
                target = room["sum"].at[e, blocks]
                if source[0] == "given":
                    target[...] = source[1][e][0][blocks] + room["near"][e, blocks]
                else:
                    height = group_blocks * out.shape[0]
                    span = pl.ds(group * height, height)
                    products(source[1], rights(i, e), span, target, room["near"].at[e, blocks])
                if e == 1:
                    rest = pl.ds(early, out.shape[1] - early)
                    for block in range(group * group_blocks, (group + 1) * group_blocks):
                        crossed[i, block] = copies.push(room["sum"].at[1, block, :, rest], room["far"].at[block], across)
        if group == 1 and not place[1]:
            pl.semaphore_signal(shared["free"], inc=1, device_id=sibling, device_id_type=MESH)

    def second(spot):
        block = slot(spot)
        for i, (source, early, out, room) in enumerate(arrays):
            rest = pl.ds(early, out.shape[1] - early)
            crossed[i, block].wait_recv()
            add_rows(room["sum"].at[0, block, :, rest], room["far"].at[block])

    def windows(size, hop, upward):
        if hop > 0:
            return pl.ds(0, size)
        return pl.ds(size // 2, size // 2) if upward else pl.ds(0, size // 2)

    def send(hop, spot, upward):
        target = ahead if upward else behind
        kinds = ("up", "up_slim") if upward else ("down", "down_slim")
        out_copies = []
        for i, (source, early, out, room) in enumerate(arrays):
            for e, size in ((0, out.shape[1]), (1, early)):
                window = windows(size, hop, upward)
                out_copies.append(
                    copies.push(room["sum"].at[e, slot(spot), :, window], room[kinds[e]].at[hop, :, window], target)
                )
        return out_copies

    def receive(hop, spot, upward, arrivals):
        kinds = ("up", "up_slim") if upward else ("down", "down_slim")
        at = 0
        for i, (source, early, out, room) in enumerate(arrays):
            for e, size in ((0, out.shape[1]), (1, early)):
                window = windows(size, hop, upward)
                arrivals[at].wait_recv()
                add_rows(room["sum"].at[e, slot(spot), :, window], room[kinds[e]].at[hop, :, window])
                at += 1

    place[2]()
    outgoing(0)
    yield
    own(0)
    yield
    outgoing(1)
    own(1)
    yield
    second(half)
    up = send(0, half, True)
    down = send(0, half, False)
    yield
    for hop in range(1, half):
        second(chips - half + hop)
        second(half - hop)
        receive(hop - 1, chips - half + hop, True, up)
        up = send(hop, chips - half + hop, True)
        receive(hop - 1, half - hop, False, down)
        down = send(hop, half - hop, False)
        yield
    second(0)
    final = []
    at = 0
    for i, (source, early, out, room) in enumerate(arrays):
        for e in range(2):
            up[at].wait_recv()
            down[at].wait_recv()
            at += 1
        part = room["sum"][1, slot(0), :, :early].astype(jnp.float32)
        part = part + room["up_slim"][half - 1].astype(jnp.float32) + room["down_slim"][half - 1].astype(jnp.float32)
        room["slim_out"][...] = part.astype(room["slim_out"].dtype)
        final.append(copies.push(room["slim_out"], room["slim_in"], across))
    yield
    for i, (source, early, out, room) in enumerate(arrays):
        total = room["sum"][0, slot(0)].astype(jnp.float32) + room["up"][half - 1].astype(jnp.float32)
        out[...] = total + room["down"][half - 1].astype(jnp.float32)
        final[i].wait_recv()
        out[:, :early] += room["slim_in"][...].astype(jnp.float32)


def scatter_order(chips, groups):
    hops = chips // 2 - 1
    if groups == 1:
        return [0] * (hops + 6)
    order = [0] * 4 + [1] * 3 + [0, -1] * hops + [1, 0, -1] + [1, -1] * (hops - 1)
    return order + [-2] + [2] * 3 + [1] + [2, 1] + [2] * hops + [2] + [0, 1, 2]


def scatter_count(chips, arrays):
    half = chips // 2
    return arrays * (4 + chips + half * 4 + 1)


ROOM = ("sum", "far", "up", "down", "up_slim", "down_slim", "slim_out", "slim_in", "near")


def scatter_room(chips, rows, columns, early, dtype, given):
    half = chips // 2
    shapes = [
        (2, chips, rows, columns),
        (chips, rows, columns - early),
        (half, rows, columns),
        (half, rows, columns),
        (half, rows, early),
        (half, rows, early),
        (rows, early),
        (rows, early),
    ]
    if given:
        shapes.append((2, chips, rows, columns))
    return [pltpu.VMEM(shape, dtype) for shape in shapes]


def last_sum(ring, parts, early, collective, states, grad, to_ring):
    chips = ring.chips
    height, columns = parts[0][0].shape
    rows = height // chips
    dtype = parts[0][0].dtype
    low = jnp.bfloat16
    room = scatter_room(chips, rows, columns, early, dtype, True)
    count = scatter_count(chips, 1)

    def kernel(*refs):
        ids = ring.neighbours()
        greet(ids)
        states, grad, to_ring, out, final, back = refs[4:10]
        scratch = refs[10:]
        copies = Copies(scratch[len(room)], scratch[len(room) + 1], None)
        source = ("given", (refs[:2], refs[2:4]))
        members = [(source, early, out, dict(zip(ROOM, scratch)))]

        def leave(span):
            final[span] = mm(states[span].astype(low), to_ring[...], NT).astype(low)

        def leave_grad(span):
            rest = grad[span]
            total = None
            for unused in range(3):
                part = rest.astype(low)
                rest = rest - part.astype(jnp.float32)
                moved = mm(part, to_ring[...], NT)
                total = moved if total is None else total + moved
            back[span] = total

        work = [functools.partial(row_chunks, states.shape[0], body) for body in (leave_grad, leave)]
        for unused in scatter_steps(copies, ids, ring, members, {"busy": []}, (True, True, lambda: None)):
            if work:
                work.pop(0)()
        copies.finish()

    return pl.pallas_call(
        kernel,
        in_specs=on_vmem(7),
        out_specs=on_vmem(3),
        out_shape=[
            jax.ShapeDtypeStruct((rows, columns), dtype),
            jax.ShapeDtypeStruct(states.shape, low),
            jax.ShapeDtypeStruct(grad.shape, jnp.float32),
        ],
        scratch_shapes=room + [pltpu.SemaphoreType.DMA((count,)), pltpu.SemaphoreType.DMA((count,))],
        compiler_params=pltpu.CompilerParams(
            collective_id=collective, has_side_effects=True, vmem_limit_bytes=40 * 1024 * 1024
        ),
        name="last_sum",
    )(*[parts[e][c].reshape(chips, rows, columns) for e in range(2) for c in range(2)], states, grad, to_ring)


def turn_all(order, ins, turned):
    step = 256
    for i, (unused, spot) in enumerate(order):

        @pl.loop(0, ins[spot].shape[1] // step)
        def chunk(j):
            window = pl.ds(pl.multiple_of(j * step, step), step)
            turned[i, window] = ins[spot][:, window].T


def backward_layer(ring, groups, collective, attention):
    chips = ring.chips
    arrays = [member for group in groups for member in group]
    total = len(arrays)
    qkv, first, grad_heads, lse, slopes, prefix, scale = attention
    tokens, height = arrays[0][0][0].shape
    rows = height // chips // 2
    low = jnp.bfloat16
    inputs, wide = ([], [])

    def entry(array):
        if isinstance(array, int):
            return array
        for spot, other in enumerate(inputs):
            if other is array:
                return ("in", spot)
        inputs.append(array)
        wide.append(array.shape[1] > 1024)
        return ("in", len(inputs) - 1)

    plans, shapes, rooms, widths = ([], [], [], [])
    for lefts, rights, early in arrays:
        plans.append(([entry(left) for left in lefts], [[entry(right) for right in side] for side in rights], early))
        sample = rights[0][0]
        columns = grad_heads[0].shape[1] if isinstance(sample, int) else sample.shape[1]
        widths.append(columns)
        shapes.append(jax.ShapeDtypeStruct((rows, columns), jnp.float32))
        rooms += scatter_room(chips, rows, columns, early, low, False)
    extra = list(qkv) + list(first) + list(grad_heads) + list(lse) + [slopes, prefix]
    made = [jax.ShapeDtypeStruct(grad_heads[0].shape, low)] * 10
    sizes = iter(widths)
    span = max(sum(next(sizes) for unused in group) for group in groups)

    def kernel(*refs):
        ins, refs = (refs[: len(inputs)], refs[len(inputs) :])
        more, refs = (refs[: len(extra)], refs[len(extra) :])
        outs, refs = (refs[:total], refs[total:])
        back, scratch = (refs[: len(made)], refs[len(made) :])
        ids = ring.neighbours()
        greet(ids)
        held, turned, outbox, near, sums, send, recv, loaded, free = scratch[len(rooms) :]
        copies = Copies(send, recv, None)
        shared = {"wide": held, "loaded": loaded, "free": free, "busy": []}
        find = lambda spot: back[spot] if isinstance(spot, int) else ins[spot[1]]
        running = []
        at = 0
        for number, group in enumerate(groups):
            members = []
            order = []
            column = 0
            for unused in group:
                lefts, rights, early = plans[at]
                for spot in lefts:
                    if spot not in order:
                        order.append(spot)
                source = ("product", [turned.at[order.index(spot)] for spot in lefts], [[find(spot) for spot in half] for half in rights])
                source += (widths[at] > 1024,)
                room = dict(zip(ROOM, scratch[at * (len(ROOM) - 1) : (at + 1) * (len(ROOM) - 1)]))
                window = pl.ds(column, widths[at])
                room["outbox"] = outbox.at[:, :, :, window]
                room["near"] = near.at[:, :, :, window]
                members.append((source, early, outs[at], room))
                column += widths[at]
                at += 1
            place = (number == 0, number == len(groups) - 1, functools.partial(turn_all, order, ins, turned))
            running.append(scatter_steps(copies, ids, ring, members, shared, place))
        parts = [(more[e], more[2 + e], more[4 + e], more[6 + e], back[5 * e : 5 * e + 5]) for e in range(2)]
        work = backward_work(parts, more[8], more[9][0], scale, sums)
        for turn in scatter_order(chips, len(groups)):
            if turn >= 0:
                next(running[turn], None)
            elif turn == -1 and work:
                work.pop(0)()
            elif turn == -2:
                while work:
                    work.pop(0)()
        copies.finish()

    count = scatter_count(chips, total)
    outs = pl.pallas_call(
        kernel,
        in_specs=[pl.BlockSpec(memory_space=pl.ANY if far else pltpu.VMEM) for far in wide] + on_vmem(8) + on_smem(2),
        out_specs=on_vmem(total + len(made)),
        out_shape=shapes + made,
        scratch_shapes=rooms
        + [
            pltpu.VMEM((2, tokens, max(widths)), low),
            pltpu.VMEM((3, height, tokens), low),
            pltpu.VMEM((2, chips // 2, rows, span), low),
            pltpu.VMEM((2, chips, rows, span), low),
            pltpu.VMEM((4, tokens, 128), jnp.float32),
            pltpu.SemaphoreType.DMA((count,)),
            pltpu.SemaphoreType.DMA((count,)),
            pltpu.SemaphoreType.DMA((2,)),
            pltpu.SemaphoreType.REGULAR,
        ],
        compiler_params=pltpu.CompilerParams(
            collective_id=collective, has_side_effects=True, vmem_limit_bytes=62 * 1024 * 1024
        ),
        name="backward_layer",
    )(*inputs, *extra)
    return (outs[:total], outs[total:])


def small_parts(vector_grads, bias_grads, by_half, placed, piece, lane):
    layers, dp = (len(vector_grads), placed.shape[0])
    vectors = jnp.stack([vector_grads[layer][i] for i in range(6) for layer in range(layers)])
    vectors = by_half(vectors.reshape(6 * layers, dp, 2, piece).transpose(2, 1, 0, 3), 0).reshape(2, dp, -1)
    shifts = [jnp.stack([bias_grads[layer][i] for layer in range(layers)], axis=1) for i in range(2)]
    shifts = jnp.concatenate([member.reshape(2, -1, dp, lane) for member in shifts], axis=1)
    shifts = jnp.einsum("tndl,bd->tbnl", shifts, placed, precision=lax.Precision.HIGHEST).reshape(2, dp, -1)
    packed = jnp.concatenate([vectors, shifts], axis=2)
    packed = jnp.pad(packed, ((0, 0), (0, 0), (0, 8 * 512 - packed.shape[2]))).reshape(2, 2, -1, 512)
    return [[packed[e, c] for c in range(2)] for e in range(2)]


def local(
    states_in,
    teacher,
    valid_mask,
    prefix_len,
    ln1_gain,
    ln1_shift,
    qkv_weight,
    qkv_bias,
    out_weight,
    out_bias,
    ln2_gain,
    ln2_shift,
    up_weight,
    up_bias,
    down_weight,
    down_bias,
):
    f32, low = (jnp.float32, jnp.bfloat16)
    layers, local_rows = (qkv_weight.shape[0], states_in.shape[1])
    width = states_in.shape[2]
    dp, tensor = (lax.axis_size("dp"), lax.axis_size("tensor"))
    here, side = (lax.axis_index("dp"), lax.axis_index("tensor"))
    ring = Ring(dp)
    piece = width // (dp * tensor)

    def by_half(pair, axis):
        return jnp.where(side == 0, pair, jnp.flip(pair, axis))

    owners = lax.dynamic_index_in_dim(jnp.asarray(ring.owners()), here, 0, keepdims=False)
    rows = width // dp
    columns = (owners[:, None] * rows + jnp.arange(rows, dtype=jnp.int32)[None]).reshape(1, width)
    to_ring = (jnp.arange(width, dtype=jnp.int32)[:, None] == columns).astype(low)

    placed = (owners[:, None] == jnp.arange(dp, dtype=jnp.int32)[None]).astype(f32)

    def into_ring(values):
        return jnp.dot(values, to_ring, preferred_element_type=f32)

    count = jnp.sum(valid_mask)
    vectors = jnp.stack([ln1_gain, ln1_shift, out_bias, ln2_gain, ln2_shift, down_bias])
    packed = jnp.concatenate(
        [vectors.reshape(-1), qkv_bias.reshape(-1), up_bias.reshape(-1), jnp.stack([count // 256, count % 256]).astype(low)]
    )
    first, second, third = (vectors.size, vectors.size + qkv_bias.size, vectors.size + qkv_bias.size + up_bias.size)
    packed_size = packed.size
    packed = jnp.pad(packed, (0, 16 * 512 - packed.size)).reshape(16, 512)
    groups = []
    for layer in range(layers):
        groups.append([(qkv_weight[layer].reshape(rows, -1), 512), (out_weight[layer].T, 256)])
        groups.append([(up_weight[layer], 768), (down_weight[layer].T, 768)])
    weights = gather_weights(ring, [[(packed, 256)] + groups[0]], 1)[0]
    used = -(-packed_size // 512)
    everything = [member.reshape(dp, -1, 512)[:, :used].reshape(dp, -1) for member in weights[:2]]
    everything = by_half(jnp.stack(everything), 0)
    gathered = weights[2:]
    vectors = everything[:, :, :first].reshape(tensor, dp, 6, layers, piece).transpose(2, 3, 1, 0, 4)
    small = vectors.reshape(6, layers, 1, width).astype(f32)
    lane = qkv_bias.shape[3]
    biases = everything[:, :, first:third].reshape(tensor, dp, -1, lane)
    biases = jnp.einsum("tbnl,bd->tndl", biases, placed.astype(low), preferred_element_type=f32)
    biases = by_half(biases.reshape(tensor, -1, dp * lane), 0)
    split = (second - first) // lane
    qkv_add = biases[:, :split].reshape(tensor, layers, 1, -1).transpose(1, 0, 2, 3)
    up_add = biases[:, split:].reshape(tensor, layers, 1, -1).transpose(1, 0, 2, 3)
    counts = jnp.sum(everything[:, :, third : third + 2].astype(f32), axis=(0, 1))
    valid_count = counts[0] * 256.0 + counts[1]

    scale = HD ** (-0.5)
    pieces = jnp.arange(H, dtype=jnp.int32)
    heads_half = H // tensor
    heads = (pieces // heads_half ^ side) * heads_half + pieces % heads_half
    slopes = jnp.exp2(-(heads.astype(f32) + 1.0) * 8.0 / H) * LOG2E

    before_first = lax.ppermute(states_in[0], "tensor", [(0, 1)])
    states = into_ring(states_in[0])
    target = into_ring(teacher[0])
    kept = []
    for layer in range(layers):
        qkv_proj, out_proj = (gathered[8 * layer : 8 * layer + 2], gathered[8 * layer + 2 : 8 * layer + 4])
        if layer == 0:
            normed = norm_rows(states, small[0][layer], small[1][layer]).astype(low)
            normed_first = norm_rows(into_ring(before_first), small[0][layer], small[1][layer]).astype(low)
        else:
            normed, normed_first = following
        qkv, kv_first = ([], [])
        for i in range(tensor):
            query = qkv_proj[i].shape[1] // 3
            mixed = jnp.dot(normed, qkv_proj[i], preferred_element_type=f32) + qkv_add[layer][i]
            qkv.append(mixed.astype(low))
            mixed = jnp.dot(normed_first, qkv_proj[i][:, query:], preferred_element_type=f32)
            kv_first.append((mixed + qkv_add[layer][i][:, query:]).astype(low))
        coming = groups[2 * layer + 2] if layer + 1 < layers else []
        rest = jnp.stack(
            [small[i][layer][0] for i in (2, 3, 4, 5)] + [small[i][(layer + 1) % layers][0] for i in (0, 1)]
        )
        weights, made = forward_layer(
            ring,
            [shard for shard, early in groups[2 * layer + 1]],
            coming,
            2 + layer,
            (qkv, kv_first, slopes, prefix_len, scale),
            states,
            out_proj,
            rest,
            up_add[layer].reshape(tensor, -1),
        )
        gathered += weights
        heads_out, lse, middle, normed_two, hidden, active, after = (
            made[:2],
            made[2:4],
            made[4],
            made[5],
            made[6:8],
            made[8:10],
            made[10],
        )
        kept.append((states, normed, normed_first, qkv, kv_first, lse, heads_out, middle, normed_two, hidden, active))
        states, following = (after, made[11:])

    factor = local_rows * tensor * dp / valid_count
    grad = factor * valid_mask[0][:, None].astype(f32) * (states - target)
    weight_grads = [None] * layers
    vector_grads = [None] * layers
    bias_grads = [None] * layers
    for layer in reversed(range(layers)):
        before, normed, normed_first, qkv, kv_first, lse, heads_out, middle, normed_two, hidden, active = kept[layer]
        qkv_proj, out_proj, up_proj, down_proj = [gathered[8 * layer + i : 8 * layer + i + 2] for i in (0, 2, 4, 6)]
        grad_mlp = grad.astype(low)
        down_shift = jnp.sum(grad_mlp.astype(f32), axis=0)
        grad_hidden = []
        for i in range(tensor):
            grad_active = jnp.dot(grad_mlp, down_proj[i], preferred_element_type=f32)
            grad_hidden.append(jax.vjp(gelu_tanh, hidden[i])[1](grad_active)[0].astype(low))
        up_shift = jnp.stack([jnp.sum(values.astype(f32), axis=0) for values in grad_hidden])
        grad_normed = mm(grad_hidden[0], up_proj[0], NT) + mm(grad_hidden[1], up_proj[1], NT)
        part, gain_two, shift_two = norm_back(middle, small[3][layer], grad_normed)
        grad_middle = grad + part
        grad_attn = grad_middle.astype(low)
        out_shift = jnp.sum(grad_attn.astype(f32), axis=0)
        grad_heads = [jnp.dot(grad_attn, out_proj[i], preferred_element_type=f32).astype(low) for i in range(tensor)]
        lefts = [normed, normed_first]
        (down_grad, up_grad, out_grad, *mixed), grads = backward_layer(
            ring,
            [
                [([grad_mlp], [[values] for values in active], 512)],
                [([normed_two], [[values] for values in grad_hidden], 512)],
                [
                    ([grad_attn], [[values] for values in heads_out], 256),
                    (lefts[:1], [[0], [5]], 256),
                    (lefts, [[1, 3], [6, 8]], 256),
                    (lefts, [[2, 4], [7, 9]], 256),
                ],
            ],
            10 + layer,
            (qkv, kv_first, grad_heads, lse, slopes, prefix_len, scale),
        )
        weight_grads[layer] = (jnp.stack(mixed, axis=1), out_grad.T, up_grad, down_grad)
        grad_normed = 0.0
        qkv_shift = []
        sent = 0.0
        for i in range(tensor):
            query = grads[5 * i].shape[1]
            grad_qkv = jnp.concatenate(grads[5 * i : 5 * i + 3], axis=1)
            grad_first = jnp.concatenate(grads[5 * i + 3 : 5 * i + 5], axis=1)
            sent = sent + mm(grad_first, qkv_proj[i][:, query:], NT)
            shift = jnp.sum(grad_qkv.astype(f32), axis=0)
            qkv_shift.append(shift + jnp.pad(jnp.sum(grad_first.astype(f32), axis=0), (query, 0)))
            grad_normed = grad_normed + mm(grad_qkv, qkv_proj[i], NT)
        arrived = lax.ppermute(sent.astype(low), "tensor", [(1, 0)])
        qkv_shift = jnp.stack(qkv_shift)
        grad_normed = grad_normed + arrived.astype(f32)
        part, gain_one, shift_one = norm_back(before, small[0][layer], grad_normed)
        grad = grad_middle + part
        vector_grads[layer] = (gain_one, shift_one, out_shift, gain_two, shift_two, down_shift)
        bias_grads[layer] = (qkv_shift, up_shift)

    parts = small_parts(vector_grads, bias_grads, by_half, placed, piece, lane)
    summed, final_states, input_grad = last_sum(ring, parts, 256, 20, states, grad, to_ring)
    summed = summed.reshape(-1)
    qkv_grad, out_grad, up_grad, down_grad = [
        jnp.stack([weight_grads[layer][i] for layer in range(layers)]) for i in range(4)
    ]
    vectors = summed[:first].reshape(6, layers, piece)
    return (
        final_states[None],
        input_grad[None],
        vectors[0],
        vectors[1],
        qkv_grad,
        summed[first:second].reshape(qkv_bias.shape),
        out_grad,
        vectors[2],
        vectors[3],
        vectors[4],
        up_grad,
        summed[second:third].reshape(up_bias.shape),
        down_grad.transpose(0, 2, 1),
        vectors[5],
    )


def solution(mesh):
    return jax.shard_map(
        local,
        mesh=mesh,
        in_specs=(
            P("dp", "tensor", None),
            P("dp", "tensor", None),
            P("dp", "tensor"),
            P("dp"),
            P(None, ("dp", "tensor")),
            P(None, ("dp", "tensor")),
            P(None, "dp", None, "tensor"),
            P(None, None, "tensor", "dp"),
            P(None, "tensor", "dp"),
            P(None, ("dp", "tensor")),
            P(None, ("dp", "tensor")),
            P(None, ("dp", "tensor")),
            P(None, "dp", "tensor"),
            P(None, "tensor", "dp"),
            P(None, "tensor", "dp"),
            P(None, ("dp", "tensor")),
        ),
        out_specs=(
            P("dp", "tensor", None),
            P("dp", "tensor", None),
            P(None, ("dp", "tensor")),
            P(None, ("dp", "tensor")),
            P(None, "dp", None, "tensor"),
            P(None, None, "tensor", "dp"),
            P(None, "tensor", "dp"),
            P(None, ("dp", "tensor")),
            P(None, ("dp", "tensor")),
            P(None, ("dp", "tensor")),
            P(None, "dp", "tensor"),
            P(None, "tensor", "dp"),
            P(None, "tensor", "dp"),
            P(None, ("dp", "tensor")),
        ),
        check_vma=False,
    )
```
